32 devices in a mesh: ctx: 8 (over z, x), tp: 4 (over y, core).
Axes of the slice: x: 2, y: 2, z: 4, core: 2. Of those that a mesh axis runs over, the one named last changes fastest.
Arguments:
- streams: bfloat16 [3, 1024, 8192], P(None, 'ctx', 'tp'), may hold values from -6 to 6
- short_filter: bfloat16 [3, 512, 7], P(None, 'tp'), may hold values from -3 to 3
- decay_rate: float32 [16, 8192], P(None, 'tp'), may hold values from 0.00029296876 to 0.05
- residue: float32 [16, 8192], P(None, 'tp'), may hold values from -5 to 5
- norm_gain: float32 [8192], P('tp'), may hold values from 0.5 to 1.5
- out_grad: bfloat16 [1024, 8192], P('ctx', 'tp'), may hold values from -6 to 6
Outputs:
- output: bfloat16 [1024, 8192], P('ctx', 'tp')
- stream_grads: bfloat16 [3, 1024, 8192], P(None, 'ctx', 'tp')
The draws below stay inside these ranges and needn't reach their ends.
All inputs are finite; a program needn't handle non-finite values.
Results may differ from the reference program's by a relative error of at most 0.002.
Values may be sent and summed in bfloat16 or wider, within the bound.
No kernel may reach another device: no remote copies, remote signals or barrier semaphores. Data moves between devices by JAX's collectives and lax.ppermute only.
A program may use at most 64 MiB of HBM per device.

```python
import math
import jax
import jax.numpy as jnp
from jax import lax

D = 8192
MODES = 16
TAPS = 7
GROUP = 16
BLOCK = 16
SEQ = 1024


def level_of(own_key, shape, split, smallest, high):
    loudness = 1.0
    for position, blocks in split:
        draws = jax.random.uniform(jax.random.fold_in(jax.random.fold_in(own_key, 6), position), (blocks,), jnp.float32, smallest / len(split), high / len(split))
        loudness = loudness * jnp.repeat(jnp.exp(draws), shape[position] // blocks).reshape((-1,) + (1,) * (len(shape) - 1 - position))
    return loudness


def gaussian(own_key, dims, width, bound, shards=(), held_as=jnp.bfloat16):
    drawn = jax.random.normal(own_key, dims, jnp.float32) * width
    if len(shards) > 0:
        drawn = level_of(own_key, dims, shards, -0.22, 0.18) * drawn
    return jnp.clip(drawn, min=-bound, max=bound).astype(held_as)


def setup_inputs(seed: int = 0) -> dict:
    seeds = jax.random.split(jax.random.key(seed), 7)
    streams = gaussian(seeds[0], (3, SEQ, D), 1.0, 6.0, ((1, 8), (2, 4)))
    short_filter = gaussian(seeds[1], (3, D // GROUP, TAPS), 0.5, 3.0, ((1, 4),))
    decay_rate = jnp.clip(jnp.exp(math.log(0.05) - 5.1397123 * jax.random.uniform(seeds[2], (MODES, D), jnp.float32) ** level_of(seeds[2], (MODES, D), ((1, 4),), -0.2, 0.2)), 0.00029296876, 0.05)
    residue = gaussian(seeds[3], (MODES, D), 1.0, 5.0, ((1, 4),), jnp.float32)
    norm_gain = jnp.clip(1.0 + 0.1 * jax.random.normal(seeds[4], (D,), jnp.float32), 0.5, 1.5)
    out_grad = gaussian(seeds[5], (SEQ, D), 1.0, 6.0, ((0, 8), (1, 4)))
    return {"streams": streams, "short_filter": short_filter, "decay_rate": decay_rate, "residue": residue, "norm_gain": norm_gain, "out_grad": out_grad}


EPSILON = 1e-05

def channel_weights(short_filter):
    stream_count, group_count, tap_count = short_filter.shape
    spread = jnp.broadcast_to(short_filter.astype(jnp.float32)[:, :, None, :], (stream_count, group_count, GROUP, tap_count))
    return jnp.transpose(spread.reshape(stream_count, group_count * GROUP, tap_count), (0, 2, 1))

def filter_tables(decay_rate, residue):
    lag_steps = jnp.arange(BLOCK, dtype=jnp.float32)
    scaled = residue * jnp.sqrt(2.0 * decay_rate)
    places = jnp.arange(BLOCK, dtype=jnp.int32)
    lagged = places[:, None] - places[None, :]
    lag_float = jnp.maximum(lagged, 0).astype(jnp.float32)
    terms = scaled[:, None, None, :] * jnp.exp(-decay_rate[:, None, None, :] * lag_float[None, :, :, None])
    toeplitz = jnp.where((lagged >= 0)[:, :, None], lax.optimization_barrier(jnp.sum(terms, axis=0)), jnp.zeros((), jnp.float32))
    end_weight = jnp.exp(-decay_rate[:, None, :] * (BLOCK - 1.0 - lag_steps)[None, :, None])
    out_weight = scaled[:, None, :] * jnp.exp(-decay_rate[:, None, :] * (lag_steps + 1.0)[None, :, None])
    return (toeplitz, end_weight, out_weight)

def causal_modal(signal, tables, block_decay):
    toeplitz, end_weight, out_weight = tables
    pieces = signal.reshape(-1, BLOCK, signal.shape[-1])

    def advance(carried_state, block_rows):
        within = lax.optimization_barrier(jnp.sum(toeplitz * block_rows[None, :, :], axis=1))
        carried = lax.optimization_barrier(jnp.sum(out_weight * carried_state[:, None, :], axis=0))
        ending = lax.optimization_barrier(jnp.sum(end_weight * block_rows[None, :, :], axis=1))
        return (block_decay * carried_state + ending, within + carried)
    zero_state = jnp.zeros(block_decay.shape, jnp.float32)
    return lax.scan(advance, zero_state, pieces)[1].reshape(signal.shape)

def short_causal(signal, weights):
    reach_rows = weights.shape[1] - 1
    length = signal.shape[1]
    padded = jnp.pad(signal, ((0, 0), (reach_rows, 0), (0, 0)))
    summed = weights[:, 0, None, :] * signal
    for offset in range(1, reach_rows + 1):
        summed = summed + weights[:, offset, None, :] * padded[:, reach_rows - offset:reach_rows - offset + length, :]
    return summed

def short_anticausal(signal, weights):
    reach_rows = weights.shape[1] - 1
    length = signal.shape[1]
    padded = jnp.pad(signal, ((0, 0), (0, reach_rows), (0, 0)))
    summed = weights[:, 0, None, :] * signal
    for offset in range(1, reach_rows + 1):
        summed = summed + weights[:, offset, None, :] * padded[:, offset:offset + length, :]
    return summed

def reference(streams, short_filter, decay_rate, residue, norm_gain, out_grad):
    stream_count, length, full_width = streams.shape
    piece_width = math.gcd(full_width, 1024)
    piece_count = full_width // piece_width
    weights_all = channel_weights(short_filter)

    def forward(piece_index):
        first_column = piece_index * piece_width
        stream_part = lax.dynamic_slice_in_dim(streams, first_column, piece_width, 2)
        weights = lax.dynamic_slice_in_dim(weights_all, first_column, piece_width, 2)
        rate_part = lax.dynamic_slice_in_dim(decay_rate, first_column, piece_width, 1)
        residue_part = lax.dynamic_slice_in_dim(residue, first_column, piece_width, 1)
        gain_part = lax.dynamic_slice_in_dim(norm_gain, first_column, piece_width, 0)
        grad_part = lax.dynamic_slice_in_dim(out_grad, first_column, piece_width, 1)
        convolved = short_causal(stream_part.astype(jnp.float32), weights)
        tables = filter_tables(rate_part, residue_part)
        block_decay = jnp.exp(-rate_part * BLOCK)
        long_conv = causal_modal(convolved[1] * convolved[2], tables, block_decay)
        modulated = convolved[0] * long_conv
        scaled_grad = gain_part * grad_part.astype(jnp.float32)
        return (convolved, tables, block_decay, long_conv, modulated, scaled_grad, weights, gain_part)

    def statistics(piece_index):
        parts = forward(piece_index)
        modulated, scaled_grad = (parts[4], parts[5])
        return (lax.optimization_barrier(jnp.sum(modulated * modulated, axis=1)), lax.optimization_barrier(jnp.sum(scaled_grad * modulated, axis=1)))
    indices = jnp.arange(piece_count, dtype=jnp.int32)
    squares, crosses = lax.map(statistics, indices)
    inverse = lax.rsqrt(lax.optimization_barrier(jnp.sum(squares, axis=0)) / full_width + EPSILON)
    cross_mean = lax.optimization_barrier(jnp.sum(crosses, axis=0)) / full_width

    def finish(piece_index):
        convolved, tables, block_decay, long_conv, modulated, scaled_grad, weights, gain_part = forward(piece_index)
        output = (gain_part * modulated * inverse[:, None]).astype(jnp.bfloat16)
        mixed_grad = inverse[:, None] * scaled_grad - modulated * (inverse * inverse * inverse * cross_mean)[:, None]
        query_grad = mixed_grad * long_conv
        long_grad = mixed_grad * convolved[0]
        gated_grad = jnp.flip(causal_modal(jnp.flip(long_grad, axis=0), tables, block_decay), axis=0)
        conv_grad = jnp.stack([query_grad, gated_grad * convolved[2], gated_grad * convolved[1]])
        return (output, short_anticausal(conv_grad, weights).astype(jnp.bfloat16))
    outputs, grads = lax.map(finish, indices)
    output = jnp.transpose(outputs, (1, 0, 2)).reshape(length, full_width)
    stream_grads = jnp.transpose(grads, (1, 2, 0, 3)).reshape(stream_count, length, full_width)
    return (output, stream_grads)
```

```python
import functools

import jax
import jax.numpy as jnp
from jax import lax
from jax.experimental import pallas as pl
from jax.experimental.pallas import tpu as pltpu
from jax.sharding import PartitionSpec as P

GROUP = 16
LANES = 128
SUB = 8
EPSILON = 1e-05
VMEM_LIMIT = 48 * 1024 * 1024


def halves(lane_blocks):
    return [pl.ds(SUB * h, SUB) for h in range(lane_blocks // SUB)]


def total(terms):
    terms = list(terms)
    while len(terms) > 1:
        paired = [terms[i] + terms[i + 1] for i in range(0, len(terms) - 1, 2)]
        terms = paired + ([terms[-1]] if len(terms) % 2 else [])
    return terms[0]


def spread_rows(source, target, first, pitch, lane_blocks):
    rows = source.shape[0]
    for lb in range(lane_blocks):
        tile = source[:, lb * LANES : (lb + 1) * LANES]
        target[pl.ds(first + lb * pitch, rows), :] = tile.astype(jnp.float32)


def row_at(ref, first, pitch, half, place):
    return ref[pl.ds(first + half * SUB * pitch + place, SUB, stride=pitch), :]


def prepare_kernel(x, filt, rate, res, conv, table, taps, ends, xs, ps):
    rows, channels = x.shape[1:]
    modes = rate.shape[0]
    lane_blocks = channels // LANES
    tap_count = taps.shape[1]
    pitch = rows + SUB
    spread = (
        lax.broadcasted_iota(jnp.int32, (SUB, LANES), 1) // GROUP
        == lax.broadcasted_iota(jnp.int32, (SUB, LANES), 0)
    ).astype(jnp.bfloat16)
    weights = jnp.dot(filt[...], spread, preferred_element_type=jnp.float32)
    taps[...] = weights.reshape(taps.shape)
    spread_rows(rate, ps, 0, modes, lane_blocks)
    spread_rows(res, ps, lane_blocks * modes, modes, lane_blocks)
    for h, half in enumerate(halves(lane_blocks)):
        for m in range(modes):
            r = row_at(ps, 0, modes, h, m)
            c = row_at(ps, lane_blocks * modes, modes, h, m)
            table[0, m, half, :] = jnp.exp(-r)
            table[1, m, half, :] = c * jnp.sqrt(2.0 * r)
            table[2, m, half, :] = r
    zero = jnp.zeros((SUB, LANES), jnp.float32)
    for s in range(3):
        first = s * lane_blocks * pitch
        for lb in range(lane_blocks):
            xs[pl.ds(first + lb * pitch, SUB), :] = zero
        spread_rows(x.at[s], xs, first + SUB, pitch, lane_blocks)
    for h, half in enumerate(halves(lane_blocks)):
        for s in range(3):
            first = s * lane_blocks * pitch + SUB
            w = [taps[s, i, half, :] for i in range(tap_count)]

            def body(block, window):
                window = list(window)
                for k in range(SUB):
                    t = block * SUB + k
                    window.append(row_at(xs, first, pitch, h, t))
                    conv[s, t, half, :] = total(
                        w[i] * window[-1 - i] for i in range(tap_count)
                    )
                return tuple(window[-(tap_count - 1) :])

            lax.fori_loop(0, rows // SUB, body, (zero,) * (tap_count - 1))
        decay = [table[0, m, half, :] for m in range(modes)]

        def step(t, state):
            u = conv[1, t, half, :] * conv[2, t, half, :]
            return tuple(decay[m] * state[m] + u for m in range(modes))

        state = (zero,) * modes
        for t in range(tap_count - 1, SUB):
            state = step(t, state)

        def block_step(block, state):
            for k in range(SUB):
                state = step(block * SUB + k, state)
            return state

        state = lax.fori_loop(1, rows // SUB, block_step, state)
        for m in range(modes):
            ends[m, half, :] = state[m]


def head_kernel(conv_in, halo, table, taps, ends, conv, state_out, hs):
    del conv_in
    rows = conv.shape[1]
    modes, lane_blocks = ends.shape[:2]
    reach = taps.shape[1] - 1
    for s in range(3):
        spread_rows(halo.at[s], hs, s * lane_blocks * SUB, SUB, lane_blocks)
    for h, half in enumerate(halves(lane_blocks)):
        heads = []
        for s in range(3):
            w = [taps[s, i, half, :] for i in range(reach + 1)]
            before = [row_at(hs, s * lane_blocks * SUB, SUB, h, j) for j in range(SUB)]
            head = []
            for t in range(reach):
                row = conv[s, t, half, :] + total(
                    w[i] * before[SUB + t - i] for i in range(t + 1, reach + 1)
                )
                conv[s, t, half, :] = row
                head.append(row)
            heads.append(head)
        product = [heads[1][t] * heads[2][t] for t in range(reach)]
        for m in range(modes):
            decay = table[0, m, half, :]
            state = product[0]
            for t in range(1, reach):
                state = decay * state + product[t]
            fade = jnp.exp(table[2, m, half, :] * -float(rows - reach))
            state_out[m, half, :] = ends[m, half, :] + fade * state


def local_kernel(conv, table, local):
    rows = conv.shape[1]
    modes, lane_blocks = table.shape[1:3]
    zero = jnp.zeros((SUB, LANES), jnp.float32)
    for half in halves(lane_blocks):
        decay = [table[0, m, half, :] for m in range(modes)]
        scale = [table[1, m, half, :] for m in range(modes)]

        def block_step(block, state):
            for k in range(SUB):
                t = block * SUB + k
                u = conv[1, t, half, :] * conv[2, t, half, :]
                state = tuple(decay[m] * state[m] + u for m in range(modes))
                local[t, half, :] = total(scale[m] * state[m] for m in range(modes))
            return state

        lax.fori_loop(0, rows // SUB, block_step, (zero,) * modes)


def carry_kernel(entering, received, table, conv, local, gain, grad, long_conv, scaled, sums, gs, sq, cr):
    rows = local.shape[0]
    modes, lane_blocks = table.shape[1:3]
    pitch = rows + SUB
    spread_rows(grad, gs, 0, pitch, lane_blocks)
    for h, half in enumerate(halves(lane_blocks)):
        decay = [table[0, m, half, :] for m in range(modes)]
        start = []
        for m in range(modes):
            fade = jnp.exp(table[2, m, half, :] * -float(rows))
            incoming = fade * entering[m, half, :] + received[m, half, :]
            start.append(table[1, m, half, :] * decay[m] * incoming)
        g = gain[half, :]

        def block_step(block, state):
            for k in range(SUB):
                t = block * SUB + k
                row = local[t, half, :] + total(state)
                state = tuple(decay[m] * state[m] for m in range(modes))
                long_conv[t, half, :] = row
                modulated = conv[0, t, half, :] * row
                sg = g * row_at(gs, 0, pitch, h, t)
                scaled[t, half, :] = sg
                place = pl.ds(pl.multiple_of(t * SUB, SUB), SUB)
                if h == 0:
                    sq[place, :] = modulated * modulated
                    cr[place, :] = sg * modulated
                else:
                    sq[place, :] += modulated * modulated
                    cr[place, :] += sg * modulated
            return state

        lax.fori_loop(0, rows // SUB, block_step, tuple(start))
    for which, ref in enumerate((sq, cr)):
        blocks = []
        for b in range(rows // SUB):
            blocks.append(
                total(
                    ref[pl.ds(b * SUB * SUB + s, SUB, stride=SUB), :] for s in range(SUB)
                )
            )
        by_row = jnp.concatenate(blocks, axis=0)
        sums[which : which + 1, :] = jnp.sum(jnp.transpose(by_row), axis=0, keepdims=True)


def mixed_kernel(width, sums, table, conv, long_conv, scaled, mixed, long_grad, state_out, inv, inv_s, off_s):
    rows = long_conv.shape[0]
    modes, lane_blocks = table.shape[1:3]
    zero = jnp.zeros((SUB, LANES), jnp.float32)
    inverse = lax.rsqrt(sums[0:1, :] / width + EPSILON)
    offset = inverse * inverse * inverse * sums[1:2, :] / width
    inv_s[...] = jnp.transpose(jnp.broadcast_to(inverse, (LANES, rows)))
    off_s[...] = jnp.transpose(jnp.broadcast_to(offset, (LANES, rows)))
    inv[...] = inv_s[...]
    blocks = rows // SUB
    for half in halves(lane_blocks):
        decay = [table[0, m, half, :] for m in range(modes)]

        def block_step(block, state):
            for k in range(SUB):
                t = (blocks - 1 - block) * SUB + SUB - 1 - k
                q = conv[0, t, half, :]
                modulated = q * long_conv[t, half, :]
                mix = (
                    inv_s[pl.ds(t, 1), :] * scaled[t, half, :] - off_s[pl.ds(t, 1), :] * modulated
                )
                mixed[t, half, :] = mix
                lg = mix * q
                long_grad[t, half, :] = lg
                state = tuple(decay[m] * state[m] + lg for m in range(modes))
            return state

        state = lax.fori_loop(0, blocks, block_step, (zero,) * modes)
        for m in range(modes):
            state_out[m, half, :] = state[m]


def output_kernel(inv, table, gain, conv, long_conv, mixed, long_grad, output, query_grad, local, head, os):
    rows = long_conv.shape[0]
    modes, lane_blocks = table.shape[1:3]
    pitch = rows + SUB
    blocks = rows // SUB
    zero = jnp.zeros((SUB, LANES), jnp.float32)
    for h, half in enumerate(halves(lane_blocks)):
        decay = [table[0, m, half, :] for m in range(modes)]
        scale = [table[1, m, half, :] for m in range(modes)]
        g = gain[half, :]

        def block_step(block, state):
            for k in range(SUB):
                t = (blocks - 1 - block) * SUB + SUB - 1 - k
                lg = long_grad[t, half, :]
                state = tuple(decay[m] * state[m] + lg for m in range(modes))
                local[t, half, :] = total(scale[m] * state[m] for m in range(modes))
            return state

        lax.fori_loop(0, blocks, block_step, (zero,) * modes)

        def out_step(block, _):
            for k in range(SUB):
                t = block * SUB + k
                long_row = long_conv[t, half, :]
                query_grad[t, half, :] = mixed[t, half, :] * long_row
                row = g * (conv[0, t, half, :] * long_row) * inv[pl.ds(t, 1), :]
                os[pl.ds(h * SUB * pitch + t, SUB, stride=pitch), :] = row
            return 0

        lax.fori_loop(0, blocks, out_step, 0)
        for t in range(SUB):
            head[0, t, half, :] = query_grad[t, half, :]
            head[1, t, half, :] = local[t, half, :]
            head[2, t, half, :] = conv[2, t, half, :]
            head[3, t, half, :] = conv[1, t, half, :]
    for lb in range(lane_blocks):
        output[:, lb * LANES : (lb + 1) * LANES] = os[pl.ds(lb * pitch, rows), :].astype(output.dtype)


def far_rows(table, half, state, rows, reach, fade_first):
    modes = table.shape[1]
    at = [
        table[1, m, half, :]
        * state[m]
        * jnp.exp(table[2, m, half, :] * -float(rows - reach + 1 + fade_first))
        for m in range(modes)
    ]
    found = [None] * reach
    for i in reversed(range(reach)):
        found[i] = total(at)
        if i:
            at = [at[m] * table[0, m, half, :] for m in range(modes)]
    return found


def turn_kernel(rows, reach, lower, near, beyond, table, own, entering, message):
    modes, lane_blocks = own.shape[:2]
    is_lower = jnp.full((SUB, LANES), lower[0]) > 0
    for half in halves(lane_blocks):
        state = []
        for m in range(modes):
            step = jnp.exp(table[2, m, half, :] * -float(2 * rows))
            e = near[m, half, :] + step * beyond[m, half, :]
            entering[m, half, :] = e
            message[m, half, :] = jnp.where(is_lower, e, own[m, half, :] + step * e)
            state.append(jnp.where(is_lower, beyond[m, half, :], e))
        added = far_rows(table, half, state, rows, reach, rows)
        for i in range(reach):
            message[modes + i, half, :] = added[i]
        for i in range(reach, SUB):
            message[modes + i, half, :] = jnp.zeros((SUB, LANES), jnp.float32)


def final_kernel(entering, received, table, taps, conv, local, query_grad, head, grads, cg, os):
    rows = local.shape[0]
    modes, lane_blocks = table.shape[1:3]
    tap_count = taps.shape[1]
    reach = tap_count - 1
    pitch = rows + SUB
    blocks = rows // SUB
    for h, half in enumerate(halves(lane_blocks)):
        decay = [table[0, m, half, :] for m in range(modes)]
        start = []
        for m in range(modes):
            fade = jnp.exp(table[2, m, half, :] * -float(rows))
            incoming = fade * entering[m, half, :] + received[m, half, :]
            start.append(table[1, m, half, :] * decay[m] * incoming)

        def block_step(block, state):
            for k in range(SUB):
                t = (blocks - 1 - block) * SUB + SUB - 1 - k
                gated = local[t, half, :] + total(state)
                state = tuple(decay[m] * state[m] for m in range(modes))
                cg[0, t, half, :] = gated * conv[2, t, half, :]
                cg[1, t, half, :] = gated * conv[1, t, half, :]
            return state

        lax.fori_loop(0, blocks, block_step, tuple(start))
        own = far_rows(table, half, [entering[m, half, :] for m in range(modes)], rows, reach, 0)
        beyond = [[], [], []]
        for i in range(reach):
            gated = head[1, i, half, :] + received[modes + i, half, :] + own[i]
            beyond[0].append(head[0, i, half, :])
            beyond[1].append(gated * head[2, i, half, :])
            beyond[2].append(gated * head[3, i, half, :])
        for s in range(3):
            w = [taps[s, i, half, :] for i in range(tap_count)]

            def conv_step(block, window):
                window = list(window)
                for k in range(SUB):
                    t = (blocks - 1 - block) * SUB + SUB - 1 - k
                    row = query_grad[t, half, :] if s == 0 else cg[s - 1, t, half, :]
                    window.insert(0, row)
                    os[pl.ds((s * lane_blocks + h * SUB) * pitch + t, SUB, stride=pitch), :] = total(
                        w[i] * window[i] for i in range(tap_count)
                    )
                return tuple(window[:reach])

            lax.fori_loop(0, blocks, conv_step, tuple(beyond[s]))
    for s in range(3):
        for lb in range(lane_blocks):
            grads[s, :, lb * LANES : (lb + 1) * LANES] = os[
                pl.ds((s * lane_blocks + lb) * pitch, rows), :
            ].astype(grads.dtype)


def run(kernel, ins, outs, scratch=(), flops=0, aliases=None, kept=True):
    out_shapes, out_specs = [], []
    for shape, dtype in outs:
        out_shapes.append(jax.ShapeDtypeStruct(shape, dtype))
        out_specs.append(pl.BlockSpec(memory_space=pltpu.VMEM))
    in_specs = [
        pl.BlockSpec(memory_space=pltpu.SMEM if i.dtype == jnp.int32 else pltpu.VMEM) for i in ins
    ]
    return pl.pallas_call(
        kernel,
        out_shape=out_shapes,
        in_specs=in_specs,
        out_specs=out_specs,
        scratch_shapes=[pltpu.VMEM(s, jnp.float32) for s in scratch],
        input_output_aliases=aliases or {},
        compiler_params=pltpu.CompilerParams(vmem_limit_bytes=VMEM_LIMIT),
        cost_estimate=pl.CostEstimate(flops=flops, bytes_accessed=4 * 1024 * 1024, transcendentals=0),
    )(*ins)


def shifted(block, distance):
    devices = range(lax.axis_size("ctx"))
    route = [(i, i + distance) for i in devices if i + distance in devices]
    return lax.ppermute(block, "ctx", route)


def swapped(block):
    return lax.ppermute(block, "ctx", [(i, i ^ 1) for i in range(lax.axis_size("ctx"))])


def on_device(streams, short_filter, decay_rate, residue, norm_gain, out_grad):
    f32 = jnp.float32
    stream_count, rows, channels = streams.shape
    modes = decay_rate.shape[0]
    lane_blocks = channels // LANES
    tap_count = short_filter.shape[2]
    reach = tap_count - 1
    pitch = rows + SUB
    count = lax.axis_size("ctx")
    row_shape = (rows, lane_blocks, LANES)
    state_shape = (modes, lane_blocks, LANES)

    halo = shifted(streams[:, rows - SUB :, :], 1)
    filt = jnp.transpose(
        short_filter.reshape(stream_count, lane_blocks, SUB, tap_count), (0, 3, 1, 2)
    ).reshape(stream_count * tap_count * lane_blocks, SUB)
    gain = norm_gain.reshape(lane_blocks, LANES)
    conv, table, taps, ends = run(
        prepare_kernel,
        (streams, filt, decay_rate, residue),
        (
            ((3,) + row_shape, f32),
            ((3,) + state_shape, f32),
            ((3, tap_count, lane_blocks, LANES), f32),
            (state_shape, f32),
        ),
        ((3 * lane_blocks * pitch, LANES), (2 * lane_blocks * modes, LANES)),
    )
    conv, state = run(
        head_kernel,
        (conv, halo, table, taps, ends),
        (((3,) + row_shape, f32), (state_shape, f32)),
        ((3 * lane_blocks * SUB, LANES),),
        aliases={0: 0},
    )
    rate = table[2]
    lower = (1 - lax.axis_index("ctx") % 2).astype(jnp.int32)

    inclusive = state
    entering = None
    width = 1
    while 2 * width < count:
        got = shifted(inclusive, 2 * width)
        if entering is None:
            entering = got
        else:
            entering = entering + jnp.exp(rate * -float(2 * rows * (width - 1))) * got
        inclusive = state + jnp.exp(rate * -float(2 * rows)) * entering
        width *= 2
    received = swapped(jnp.where(lower > 0, inclusive, entering))
    (local,) = run(local_kernel, (conv, table), ((row_shape, f32),), flops=10**9)
    long_conv, scaled, sums = run(
        carry_kernel,
        (entering, received, table, conv, local, gain, out_grad),
        ((row_shape, f32), (row_shape, f32), ((2, rows), f32)),
        ((lane_blocks * pitch, LANES), (rows * SUB, LANES), (rows * SUB, LANES)),
    )
    sums = lax.psum(sums, "tp")
    mixed, long_grad, back, inv = run(
        functools.partial(mixed_kernel, float(channels * lax.axis_size("tp"))),
        (sums, table, conv, long_conv, scaled),
        ((row_shape, f32), (row_shape, f32), (state_shape, f32), ((rows, LANES), f32)),
        ((rows, LANES), (rows, LANES)),
    )

    inclusive = back
    near = beyond = None
    width = 1
    while 2 * width < count:
        got = shifted(inclusive, -2 * width)
        if near is None:
            near, beyond = got, jnp.zeros_like(got)
            inclusive = back + jnp.exp(rate * -float(2 * rows)) * near
        else:
            beyond = beyond + jnp.exp(rate * -float(2 * rows * (width - 2))) * got
            if 4 * width < count:
                step = jnp.exp(rate * -float(2 * rows))
                inclusive = back + step * (near + step * beyond)
        width *= 2
    output, query_grad, local_back, head = run(
        output_kernel,
        (inv, table, gain, conv, long_conv, mixed, long_grad),
        (
            ((rows, channels), jnp.bfloat16),
            (row_shape, f32),
            (row_shape, f32),
            ((4, SUB, lane_blocks, LANES), f32),
        ),
        ((lane_blocks * pitch, LANES),),
        flops=10**9,
    )
    head = shifted(head, -1)
    entering_back, message = run(
        functools.partial(turn_kernel, rows, reach),
        (lower[None], near, beyond, table, back),
        ((state_shape, f32), ((modes + SUB, lane_blocks, LANES), f32)),
    )
    received_back = swapped(message)
    (grads,) = run(
        final_kernel,
        (entering_back, received_back, table, taps, conv, local_back, query_grad, head),
        (((3, rows, channels), jnp.bfloat16),),
        ((2, rows, lane_blocks, LANES), (3 * lane_blocks * pitch, LANES)),
    )
    return output, grads


def solution(mesh):
    return jax.shard_map(
        on_device,
        mesh=mesh,
        in_specs=(
            P(None, "ctx", "tp"),
            P(None, "tp", None),
            P(None, "tp"),
            P(None, "tp"),
            P("tp"),
            P("ctx", "tp"),
        ),
        out_specs=(P("ctx", "tp"), P(None, "ctx", "tp")),
        check_vma=False,
    )
```

```python
import functools

import jax
import jax.numpy as jnp
from jax import lax
from jax.experimental import pallas as pl
from jax.experimental.pallas import tpu as pltpu
from jax.sharding import PartitionSpec as P

GROUP = 16
LANES = 128
SUB = 8
EPSILON = 1e-05
VMEM_LIMIT = 16 * 1024 * 1024


def halves(lane_blocks):
    return [pl.ds(SUB * h, SUB) for h in range(lane_blocks // SUB)]


def total(terms):
    terms = list(terms)
    while len(terms) > 1:
        paired = [terms[i] + terms[i + 1] for i in range(0, len(terms) - 1, 2)]
        terms = paired + ([terms[-1]] if len(terms) % 2 else [])
    return terms[0]


def spread_rows(source, target, first, pitch, lane_blocks):
    rows = source.shape[0]
    for lb in range(lane_blocks):
        tile = source[:, lb * LANES : (lb + 1) * LANES]
        target[pl.ds(first + lb * pitch, rows), :] = tile.astype(jnp.float32)


def row_at(ref, first, pitch, half, place):
    return ref[pl.ds(first + half * SUB * pitch + place, SUB, stride=pitch), :]


def tail_kernel(x, tail, edge, sem):
    rows = x.shape[1]
    move = pltpu.make_async_copy(x.at[:, pl.ds(rows - 2 * SUB, 2 * SUB), :], edge, sem)
    move.start()
    move.wait()
    tail[...] = edge[:, SUB:, :]


def prepare_kernel(
    x_far, filt_far, rate_far, res_far, pair_far, taps_far, first_rows, table, taps, ends,
    x, filt, rate, res, pair, xs, ps, sems,
):
    rows, channels = x.shape[1:]
    modes = rate.shape[0]
    lane_blocks = channels // LANES
    tap_count = taps.shape[1]
    pitch = rows + SUB
    fetches = [
        pltpu.make_async_copy(source, target, sems.at[i])
        for i, (source, target) in enumerate(
            [(filt_far, filt), (rate_far, rate), (res_far, res)]
            + [(x_far.at[1 + s], x.at[s]) for s in range(2)]
        )
    ]
    for fetch in fetches:
        fetch.start()
    spread = (
        lax.broadcasted_iota(jnp.int32, (channels // GROUP, channels), 1) // GROUP
        == lax.broadcasted_iota(jnp.int32, (channels // GROUP, channels), 0)
    ).astype(jnp.bfloat16)
    fetches[0].wait()
    for s in range(3):
        weights = jnp.dot(filt[s], spread, preferred_element_type=jnp.float32)
        for lb in range(lane_blocks):
            ps[pl.ds(lb * SUB, tap_count), :] = weights[:, lb * LANES : (lb + 1) * LANES]
        for h, half in enumerate(halves(lane_blocks)):
            for i in range(tap_count):
                taps[s, i, half, :] = row_at(ps, 0, SUB, h, i)
    stores = [pltpu.make_async_copy(taps, taps_far, sems.at[5])]
    stores[0].start()
    fetches[1].wait()
    fetches[2].wait()
    spread_rows(rate, ps, 0, modes, lane_blocks)
    spread_rows(res, ps, lane_blocks * modes, modes, lane_blocks)
    for h, half in enumerate(halves(lane_blocks)):
        for m in range(modes):
            r = row_at(ps, 0, modes, h, m)
            c = row_at(ps, lane_blocks * modes, modes, h, m)
            table[0, m, half, :] = jnp.exp(-r)
            table[1, m, half, :] = c * jnp.sqrt(2.0 * r)
            table[2, m, half, :] = r
    zero = jnp.zeros((SUB, LANES), jnp.float32)
    for s in range(2):
        fetches[3 + s].wait()
        spread_rows(x.at[s], xs, s * lane_blocks * pitch, pitch, lane_blocks)
    for h, half in enumerate(halves(lane_blocks)):
        for s in range(2):
            w = [taps[1 + s, i, half, :] for i in range(tap_count)]

            def body(block, window):
                window = list(window)
                for k in range(SUB):
                    t = block * SUB + k
                    window.append(row_at(xs, s * lane_blocks * pitch, pitch, h, t))
                    pair[s, t, half, :] = total(w[i] * window[-1 - i] for i in range(tap_count))
                return tuple(window[-(tap_count - 1) :])

            lax.fori_loop(0, rows // SUB, body, (zero,) * (tap_count - 1))
            stores.append(
                pltpu.make_async_copy(
                    pair.at[s, :, half, :], pair_far.at[s, :, half, :], sems.at[6 + 2 * h + s]
                )
            )
            stores[-1].start()
            first_rows[s, :, half, :] = pair[s, :SUB, half, :]
        decay = [table[0, m, half, :] for m in range(modes)]

        def step(t, state):
            u = pair[0, t, half, :] * pair[1, t, half, :]
            return tuple(decay[m] * state[m] + u for m in range(modes))

        state = (zero,) * modes
        for t in range(tap_count - 1, SUB):
            state = step(t, state)

        def block_step(block, state):
            for k in range(SUB):
                state = step(block * SUB + k, state)
            return state

        state = lax.fori_loop(1, rows // SUB, block_step, state)
        for m in range(modes):
            ends[m, half, :] = state[m]
    for store in stores:
        store.wait()


def head_kernel(rows, first_in, halo, table, taps, ends, first_rows, state_out, hs):
    modes, lane_blocks = ends.shape[:2]
    reach = taps.shape[1] - 1
    for s in range(2):
        spread_rows(halo.at[1 + s], hs, s * lane_blocks * SUB, SUB, lane_blocks)
    for h, half in enumerate(halves(lane_blocks)):
        heads = []
        for s in range(2):
            w = [taps[1 + s, i, half, :] for i in range(reach + 1)]
            before = [row_at(hs, s * lane_blocks * SUB, SUB, h, j) for j in range(SUB)]
            head = []
            for t in range(SUB):
                row = first_in[s, t, half, :]
                if t < reach:
                    row = row + total(w[i] * before[SUB + t - i] for i in range(t + 1, reach + 1))
                    head.append(row)
                first_rows[s, t, half, :] = row
            heads.append(head)
        product = [heads[0][t] * heads[1][t] for t in range(reach)]
        for m in range(modes):
            decay = table[0, m, half, :]
            state = product[0]
            for t in range(1, reach):
                state = decay * state + product[t]
            fade = jnp.exp(table[2, m, half, :] * -float(rows - reach))
            state_out[m, half, :] = ends[m, half, :] + fade * state


def query_kernel(x_far, halo, taps, gain, grad_far, query, scaled, x, grad, xs, gs, sems):
    rows, channels = x.shape
    lane_blocks = channels // LANES
    tap_count = taps.shape[1]
    pitch = rows + SUB
    fetches = [
        pltpu.make_async_copy(x_far.at[0], x, sems.at[0]),
        pltpu.make_async_copy(grad_far, grad, sems.at[1]),
    ]
    for fetch in fetches:
        fetch.start()
    spread_rows(halo.at[0], xs, 0, pitch, lane_blocks)
    fetches[0].wait()
    spread_rows(x, xs, SUB, pitch, lane_blocks)
    fetches[1].wait()
    spread_rows(grad, gs, 0, pitch, lane_blocks)
    for h, half in enumerate(halves(lane_blocks)):
        w = [taps[0, i, half, :] for i in range(tap_count)]
        g = gain[half, :]

        def body(block, window):
            window = list(window)
            for k in range(SUB):
                t = block * SUB + k
                window.append(row_at(xs, SUB, pitch, h, t))
                query[t, half, :] = total(w[i] * window[-1 - i] for i in range(tap_count))
                scaled[t, half, :] = g * row_at(gs, 0, pitch, h, t)
            return tuple(window[-(tap_count - 1) :])

        lax.fori_loop(
            0, rows // SUB, body, tuple(row_at(xs, 0, pitch, h, SUB + 1 - tap_count + j) for j in range(tap_count - 1))
        )


def local_kernel(pair, first_rows, table, local):
    rows = local.shape[0]
    modes, lane_blocks = table.shape[1:3]
    zero = jnp.zeros((SUB, LANES), jnp.float32)
    for half in halves(lane_blocks):
        decay = [table[0, m, half, :] for m in range(modes)]
        scale = [table[1, m, half, :] for m in range(modes)]

        def block_step(source, block, state):
            for k in range(SUB):
                t = block * SUB + k
                u = source[0, t, half, :] * source[1, t, half, :]
                state = tuple(decay[m] * state[m] + u for m in range(modes))
                local[t, half, :] = total(scale[m] * state[m] for m in range(modes))
            return state

        state = block_step(first_rows, 0, (zero,) * modes)
        lax.fori_loop(1, rows // SUB, functools.partial(block_step, pair), state)


def carry_kernel(entering, received, table, query, local, scaled, long_conv, sums, sq, cr):
    rows = local.shape[0]
    modes, lane_blocks = table.shape[1:3]
    for h, half in enumerate(halves(lane_blocks)):
        decay = [table[0, m, half, :] for m in range(modes)]
        start = []
        for m in range(modes):
            fade = jnp.exp(table[2, m, half, :] * -float(rows))
            incoming = fade * entering[m, half, :] + received[m, half, :]
            start.append(table[1, m, half, :] * decay[m] * incoming)

        def block_step(block, state):
            for k in range(SUB):
                t = block * SUB + k
                row = local[t, half, :] + total(state)
                state = tuple(decay[m] * state[m] for m in range(modes))
                long_conv[t, half, :] = row
                modulated = query[t, half, :] * row
                place = pl.ds(pl.multiple_of(t * SUB, SUB), SUB)
                square = modulated * modulated
                cross = scaled[t, half, :] * modulated
                sq[place, :] = square if h == 0 else sq[place, :] + square
                cr[place, :] = cross if h == 0 else cr[place, :] + cross
            return state

        lax.fori_loop(0, rows // SUB, block_step, tuple(start))
    for which, ref in enumerate((sq, cr)):
        blocks = []
        for b in range(rows // SUB):
            blocks.append(
                total(
                    ref[pl.ds(b * SUB * SUB + s, SUB, stride=SUB), :] for s in range(SUB)
                )
            )
        by_row = jnp.concatenate(blocks, axis=0)
        sums[which : which + 1, :] = jnp.sum(jnp.transpose(by_row), axis=0, keepdims=True)


def mixed_kernel(width, sums, table, query, long_conv, scaled, mixed, long_grad, state_out, inv, inv_s, off_s):
    rows = long_conv.shape[0]
    modes, lane_blocks = table.shape[1:3]
    zero = jnp.zeros((SUB, LANES), jnp.float32)
    inverse = lax.rsqrt(sums[0:1, :] / width + EPSILON)
    offset = inverse * inverse * inverse * sums[1:2, :] / width
    inv_s[...] = jnp.transpose(jnp.broadcast_to(inverse, (LANES, rows)))
    off_s[...] = jnp.transpose(jnp.broadcast_to(offset, (LANES, rows)))
    inv[...] = inv_s[...]
    blocks = rows // SUB
    for half in halves(lane_blocks):
        decay = [table[0, m, half, :] for m in range(modes)]

        def block_step(block, state):
            for k in range(SUB):
                t = (blocks - 1 - block) * SUB + SUB - 1 - k
                q = query[t, half, :]
                modulated = q * long_conv[t, half, :]
                mix = (
                    inv_s[pl.ds(t, 1), :] * scaled[t, half, :] - off_s[pl.ds(t, 1), :] * modulated
                )
                mixed[t, half, :] = mix
                lg = mix * q
                long_grad[t, half, :] = lg
                state = tuple(decay[m] * state[m] + lg for m in range(modes))
            return state

        state = lax.fori_loop(0, blocks, block_step, (zero,) * modes)
        for m in range(modes):
            state_out[m, half, :] = state[m]


def back_kernel(table, first_rows, long_conv, mixed, long_grad, local, head):
    rows = long_conv.shape[0]
    modes, lane_blocks = table.shape[1:3]
    reach = head.shape[1]
    blocks = rows // SUB
    zero = jnp.zeros((SUB, LANES), jnp.float32)
    for half in halves(lane_blocks):
        decay = [table[0, m, half, :] for m in range(modes)]
        scale = [table[1, m, half, :] for m in range(modes)]

        def block_step(block, state):
            for k in range(SUB):
                t = (blocks - 1 - block) * SUB + SUB - 1 - k
                lg = long_grad[t, half, :]
                state = tuple(decay[m] * state[m] + lg for m in range(modes))
                local[t, half, :] = total(scale[m] * state[m] for m in range(modes))
            return state

        lax.fori_loop(0, blocks, block_step, (zero,) * modes)
    for t in range(reach):
        head[0, t] = (mixed[t] * long_conv[t]).astype(head.dtype)
        head[1, t] = local[t].astype(head.dtype)
        head[2, t] = first_rows[1, t].astype(head.dtype)
        head[3, t] = first_rows[0, t].astype(head.dtype)


def output_kernel(inv, taps, gain, query, long_conv, mixed, output, finished, last, os, qs):
    rows = long_conv.shape[0]
    lane_blocks = taps.shape[2]
    tap_count = taps.shape[1]
    pitch = rows + SUB
    blocks = rows // SUB
    zero = jnp.zeros((SUB, LANES), jnp.float32)
    for h, half in enumerate(halves(lane_blocks)):
        g = gain[half, :]
        w = [taps[0, i, half, :] for i in range(tap_count)]

        def out_step(block, window):
            window = list(window)
            for k in range(SUB):
                t = (blocks - 1 - block) * SUB + SUB - 1 - k
                long_row = long_conv[t, half, :]
                window.insert(0, mixed[t, half, :] * long_row)
                row = g * (query[t, half, :] * long_row) * inv[pl.ds(t, 1), :]
                os[pl.ds(h * SUB * pitch + t, SUB, stride=pitch), :] = row
                qs[pl.ds(h * SUB * pitch + t, SUB, stride=pitch), :] = total(
                    w[i] * window[i] for i in range(tap_count)
                )
            return tuple(window[: tap_count - 1])

        lax.fori_loop(0, blocks, out_step, (zero,) * (tap_count - 1))
    for lb in range(lane_blocks):
        columns = slice(lb * LANES, (lb + 1) * LANES)
        output[:, columns] = os[pl.ds(lb * pitch, rows), :].astype(output.dtype)
        finished[:, columns] = qs[pl.ds(lb * pitch, rows), :].astype(finished.dtype)
        last[pl.ds(lb * SUB, SUB), :] = qs[pl.ds(lb * pitch + rows - SUB, SUB), :]


def far_rows(table, half, state, rows, reach, fade_first):
    modes = table.shape[1]
    at = [
        table[1, m, half, :]
        * state[m]
        * jnp.exp(table[2, m, half, :] * -float(rows - reach + 1 + fade_first))
        for m in range(modes)
    ]
    found = [None] * reach
    for i in reversed(range(reach)):
        found[i] = total(at)
        if i:
            at = [at[m] * table[0, m, half, :] for m in range(modes)]
    return found


def turn_kernel(rows, reach, lower, near, beyond, table, own, entering, message):
    modes, lane_blocks = own.shape[:2]
    is_lower = jnp.full((SUB, LANES), lower[0]) > 0
    for half in halves(lane_blocks):
        state = []
        for m in range(modes):
            step = jnp.exp(table[2, m, half, :] * -float(2 * rows))
            e = near[m, half, :] + step * beyond[m, half, :]
            entering[m, half, :] = e
            message[m, half, :] = jnp.where(is_lower, e, own[m, half, :] + step * e)
            state.append(jnp.where(is_lower, beyond[m, half, :], e))
        added = far_rows(table, half, state, rows, reach, rows)
        for i in range(reach):
            message[modes + i, half, :] = added[i]
        for i in range(reach, SUB):
            message[modes + i, half, :] = jnp.zeros((SUB, LANES), jnp.float32)


def final_kernel(
    entering, received, table, taps, pair, first_rows, local, query, last, head, grads, cg, os, ls, made, edge, sems
):
    rows = local.shape[0]
    modes, lane_blocks = table.shape[1:3]
    tap_count = taps.shape[1]
    reach = tap_count - 1
    pitch = rows + SUB
    blocks = rows // SUB
    kept = rows - 2 * SUB
    moves = [
        pltpu.make_async_copy(
            query.at[pl.ds(0, kept), :], grads.at[0, pl.ds(0, kept), :], sems.at[0]
        )
    ]
    moves[0].start()
    ls[...] = last[...]
    for h, half in enumerate(halves(lane_blocks)):
        decay = [table[0, m, half, :] for m in range(modes)]
        start = []
        for m in range(modes):
            fade = jnp.exp(table[2, m, half, :] * -float(rows))
            incoming = fade * entering[m, half, :] + received[m, half, :]
            start.append(table[1, m, half, :] * decay[m] * incoming)

        def block_step(source, block, state):
            for k in range(SUB):
                t = (blocks - 1 - block) * SUB + SUB - 1 - k
                gated = local[t, half, :] + total(state)
                state = tuple(decay[m] * state[m] for m in range(modes))
                cg[0, t, :, :] = gated * source[1, t, half, :]
                cg[1, t, :, :] = gated * source[0, t, half, :]
            return state

        state = lax.fori_loop(0, blocks - 1, functools.partial(block_step, pair), tuple(start))
        block_step(first_rows, blocks - 1, state)
        own = far_rows(table, half, [entering[m, half, :] for m in range(modes)], rows, reach, 0)
        beyond = [[], [], []]
        for i in range(reach):
            gated = head[1, i, half, :].astype(jnp.float32) + received[modes + i, half, :] + own[i]
            beyond[0].append(head[0, i, half, :].astype(jnp.float32))
            beyond[1].append(gated * head[2, i, half, :].astype(jnp.float32))
            beyond[2].append(gated * head[3, i, half, :].astype(jnp.float32))
        for t in range(SUB - reach, SUB):
            place = pl.ds(h * SUB * SUB + t, SUB, stride=SUB)
            ls[place, :] += total(
                taps[0, i, half, :] * beyond[0][t + i - SUB] for i in range(SUB - t, tap_count)
            )
        for s in range(1, 3):
            w = [taps[s, i, half, :] for i in range(tap_count)]

            def conv_step(block, window):
                window = list(window)
                for k in range(SUB):
                    t = (blocks - 1 - block) * SUB + SUB - 1 - k
                    window.insert(0, cg[s - 1, t, :, :])
                    os[pl.ds(t, SUB, stride=pitch), :] = total(
                        w[i] * window[i] for i in range(tap_count)
                    )
                return tuple(window[:reach])

            lax.fori_loop(0, blocks, conv_step, tuple(beyond[s]))
            for lb in range(SUB):
                first = (h * SUB + lb) * LANES
                made[s - 1, :, first : first + LANES] = os[pl.ds(lb * pitch, rows), :].astype(made.dtype)
            columns = pl.ds(h * SUB * LANES, SUB * LANES)
            moves.append(
                pltpu.make_async_copy(
                    made.at[s - 1, :, columns], grads.at[s, :, columns], sems.at[len(moves)]
                )
            )
            moves[-1].start()
    for lb in range(lane_blocks):
        columns = slice(lb * LANES, (lb + 1) * LANES)
        ending = jnp.concatenate(
            [query[kept : kept + SUB, columns].astype(jnp.float32), ls[pl.ds(lb * SUB, SUB), :]], axis=0
        )
        edge[:, columns] = ending.astype(edge.dtype)
    moves.append(
        pltpu.make_async_copy(edge, grads.at[0, pl.ds(kept, 2 * SUB), :], sems.at[len(moves)])
    )
    moves[-1].start()
    for move in moves:
        move.wait()


def kept(*shape, dtype=jnp.float32):
    return pltpu.VMEM(shape, dtype)


def run(kernel, ins, outs, scratch=(), work=0, aliases=None):
    ins = [pltpu.with_memory_space_constraint(a, space) for a, space in ins]
    spaces = [getattr(o, "memory_space", pltpu.VMEM) for o in outs]
    return pl.pallas_call(
        kernel,
        out_shape=outs,
        in_specs=[pl.BlockSpec(memory_space=jax.typeof(a).memory_space) for a in ins],
        out_specs=[pl.BlockSpec(memory_space=space) for space in spaces],
        scratch_shapes=[pltpu.VMEM(s, jnp.float32) if isinstance(s, tuple) else s for s in scratch],
        input_output_aliases=aliases or {},
        compiler_params=pltpu.CompilerParams(vmem_limit_bytes=VMEM_LIMIT),
        cost_estimate=pl.CostEstimate(flops=work, bytes_accessed=4 * 1024 * 1024, transcendentals=0),
    )(*ins)


def shifted(block, distance):
    devices = range(lax.axis_size("ctx"))
    route = [(i, i + distance) for i in devices if i + distance in devices]
    return lax.ppermute(block, "ctx", route)


def swapped(block):
    return lax.ppermute(block, "ctx", [(i, i ^ 1) for i in range(lax.axis_size("ctx"))])


def on_device(streams, short_filter, decay_rate, residue, norm_gain, out_grad):
    rows, channels = streams.shape[1:]
    modes = decay_rate.shape[0]
    lane_blocks = channels // LANES
    tap_count = short_filter.shape[2]
    reach = tap_count - 1
    pitch = rows + SUB
    count = lax.axis_size("ctx")
    row_shape = (rows, lane_blocks, LANES)
    state_shape = (modes, lane_blocks, LANES)
    bf16 = jnp.bfloat16

    def v(*arrays):
        return [(a, pltpu.VMEM) for a in arrays]

    def far(*arrays):
        return [(a, pltpu.HBM) for a in arrays]

    (tail,) = run(
        tail_kernel,
        far(streams),
        [jax.ShapeDtypeStruct((3, SUB, channels), bf16)],
        (pltpu.VMEM((3, 2 * SUB, channels), bf16), pltpu.SemaphoreType.DMA(())),
    )
    halo = shifted(tail, 1)
    gain = norm_gain.reshape(lane_blocks, LANES)
    pair_far, taps_far, first_rows, table, taps, ends = run(
        prepare_kernel,
        far(streams, jnp.swapaxes(short_filter, 1, 2), decay_rate, residue),
        [
            pltpu.HBM((2, *row_shape), jnp.float32),
            pltpu.HBM((3, tap_count, lane_blocks, LANES), jnp.float32),
            kept(2, SUB, lane_blocks, LANES),
            kept(3, *state_shape),
            kept(3, tap_count, lane_blocks, LANES),
            kept(*state_shape),
        ],
        (
            pltpu.VMEM((2, rows, channels), bf16),
            pltpu.VMEM((3, tap_count, channels // GROUP), bf16),
            (modes, channels),
            (modes, channels),
            (2, *row_shape),
            (2 * lane_blocks * pitch, LANES),
            (2 * lane_blocks * modes, LANES),
            pltpu.SemaphoreType.DMA((6 + lane_blocks // 4,)),
        ),
        work=10**9,
    )
    first_rows, state = run(
        functools.partial(head_kernel, rows),
        v(first_rows, halo, table, taps, ends),
        [kept(2, SUB, lane_blocks, LANES), jax.ShapeDtypeStruct(state_shape, jnp.float32)],
        ((2 * lane_blocks * SUB, LANES),),
    )
    rate = table[2]
    lower = (1 - lax.axis_index("ctx") % 2).astype(jnp.int32)

    query, scaled = run(
        query_kernel,
        far(streams) + v(halo, taps, gain) + far(out_grad),
        [kept(*row_shape), kept(*row_shape)],
        (
            pltpu.VMEM((rows, channels), bf16),
            pltpu.VMEM((rows, channels), bf16),
            (lane_blocks * pitch, LANES),
            (lane_blocks * pitch, LANES),
            pltpu.SemaphoreType.DMA((2,)),
        ),
        work=2 * 10**9,
    )
    (local,) = run(
        local_kernel, v(pair_far, first_rows, table), [kept(*row_shape)], work=2 * 10**9
    )
    step = jnp.exp(rate * -float(2 * rows))
    inclusive, entering = state, jnp.zeros_like(state)
    width = 1
    while 2 * width < count:
        got = shifted(inclusive, 2 * width)
        if width == 1:
            got, query, scaled = lax.optimization_barrier((got, query, scaled))
            entering = got
        else:
            if 4 * width >= count:
                got, local = lax.optimization_barrier((got, local))
            entering = entering + jnp.exp(rate * -float(2 * rows * (width - 1))) * got
        inclusive = state + step * entering
        width *= 2
    received = swapped(jnp.where(lower > 0, inclusive, entering))
    long_conv, sums = run(
        carry_kernel,
        v(entering, received, table, query, local, scaled),
        [kept(*row_shape), kept(2, rows)],
        ((rows * SUB, LANES), (rows * SUB, LANES)),
    )
    sums = lax.psum(sums, "tp")
    mixed, long_grad, back, inv = run(
        functools.partial(mixed_kernel, float(channels * lax.axis_size("tp"))),
        v(sums, table, query, long_conv, scaled),
        [
            kept(*row_shape),
            kept(*row_shape),
            jax.ShapeDtypeStruct(state_shape, jnp.float32),
            kept(rows, LANES),
        ],
        ((rows, LANES), (rows, LANES)),
    )

    local_back, head = run(
        back_kernel,
        v(table, first_rows, long_conv, mixed, long_grad),
        [kept(*row_shape), kept(4, reach, lane_blocks, LANES, dtype=bf16)],
        work=2 * 10**9,
    )
    output, finished, last = run(
        output_kernel,
        v(inv, taps_far, gain, query, long_conv, mixed),
        [
            jax.ShapeDtypeStruct((rows, channels), bf16),
            kept(rows, channels, dtype=bf16),
            kept(lane_blocks * SUB, LANES),
        ],
        ((lane_blocks * pitch, LANES), (lane_blocks * pitch, LANES)),
        work=2 * 10**9,
    )
    inclusive, near, beyond = back, jnp.zeros_like(back), jnp.zeros_like(back)
    width = 1
    while 2 * width < count:
        got = shifted(inclusive, -2 * width)
        if width == 1:
            got, head = lax.optimization_barrier((got, head))
            near = got
        else:
            if 4 * width >= count:
                got, head, finished = lax.optimization_barrier((got, shifted(head, -1), finished))
            beyond = beyond + jnp.exp(rate * -float(2 * rows * (width - 2))) * got
        inclusive = back + step * (near + step * beyond if width > 1 else near)
        width *= 2
    entering_back, message = run(
        functools.partial(turn_kernel, rows, reach),
        [(lower[None], pltpu.SMEM)] + v(near, beyond, table, back),
        [kept(*state_shape), jax.ShapeDtypeStruct((modes + SUB, lane_blocks, LANES), jnp.float32)],
    )
    received_back = swapped(message)
    (grads,) = run(
        final_kernel,
        v(entering_back, received_back, table, taps_far, pair_far, first_rows, local_back, finished, last, head),
        [pltpu.HBM((3, rows, channels), bf16)],
        (
            (2, rows, SUB, LANES),
            (SUB * pitch, LANES),
            (lane_blocks * SUB, LANES),
            pltpu.VMEM((2, rows, channels), bf16),
            pltpu.VMEM((2 * SUB, channels), bf16),
            pltpu.SemaphoreType.DMA((2 + lane_blocks // 4,)),
        ),
    )
    return output, grads


def solution(mesh):
    return jax.shard_map(
        on_device,
        mesh=mesh,
        in_specs=(
            P(None, "ctx", "tp"),
            P(None, "tp", None),
            P(None, "tp"),
            P(None, "tp"),
            P("tp"),
            P("ctx", "tp"),
        ),
        out_specs=(P("ctx", "tp"), P(None, "ctx", "tp")),
        check_vma=False,
    )
```

```python
import functools

import jax
import jax.numpy as jnp
from jax import lax
from jax.experimental import pallas as pl
from jax.experimental.pallas import tpu as pltpu
from jax.sharding import PartitionSpec as P

GROUP = 16
LANES = 128
SUB = 8
EPSILON = 1e-05
VMEM_LIMIT = 16 * 1024 * 1024


def halves(lane_blocks):
    return [pl.ds(SUB * h, SUB) for h in range(lane_blocks // SUB)]


def total(terms):
    terms = list(terms)
    while len(terms) > 1:
        paired = [terms[i] + terms[i + 1] for i in range(0, len(terms) - 1, 2)]
        terms = paired + ([terms[-1]] if len(terms) % 2 else [])
    return terms[0]


def spread_rows(source, target, first, pitch, lane_blocks):
    rows = source.shape[0]
    for lb in range(lane_blocks):
        tile = source[:, lb * LANES : (lb + 1) * LANES]
        target[pl.ds(first + lb * pitch, rows), :] = tile.astype(jnp.float32)


def row_at(ref, first, pitch, half, place):
    return ref[pl.ds(first + half * SUB * pitch + place, SUB, stride=pitch), :]


def tail_kernel(x, tail, edge, sem):
    rows = x.shape[1]
    move = pltpu.make_async_copy(x.at[:, pl.ds(rows - 2 * SUB, 2 * SUB), :], edge, sem)
    move.start()
    move.wait()
    tail[...] = edge[:, SUB:, :]


def prepare_kernel(
    x_far, filt_far, rate_far, res_far, pair_far, taps_far, first_rows, table, taps, ends,
    x, filt, rate, res, pair, xs, ps, sems,
):
    rows, channels = x.shape[1:]
    modes = rate.shape[0]
    lane_blocks = channels // LANES
    tap_count = taps.shape[1]
    pitch = rows + SUB
    fetches = [
        pltpu.make_async_copy(source, target, sems.at[i])
        for i, (source, target) in enumerate(
            [(filt_far, filt), (rate_far, rate), (res_far, res)]
            + [(x_far.at[1 + s], x.at[s]) for s in range(2)]
        )
    ]
    for fetch in fetches:
        fetch.start()
    spread = (
        lax.broadcasted_iota(jnp.int32, (channels // GROUP, channels), 1) // GROUP
        == lax.broadcasted_iota(jnp.int32, (channels // GROUP, channels), 0)
    ).astype(jnp.bfloat16)
    fetches[0].wait()
    for s in range(3):
        weights = jnp.dot(filt[s], spread, preferred_element_type=jnp.float32)
        for lb in range(lane_blocks):
            ps[pl.ds(lb * SUB, tap_count), :] = weights[:, lb * LANES : (lb + 1) * LANES]
        for h, half in enumerate(halves(lane_blocks)):
            for i in range(tap_count):
                taps[s, i, half, :] = row_at(ps, 0, SUB, h, i)
    stores = [pltpu.make_async_copy(taps, taps_far, sems.at[5])]
    stores[0].start()
    fetches[1].wait()
    fetches[2].wait()
    spread_rows(rate, ps, 0, modes, lane_blocks)
    spread_rows(res, ps, lane_blocks * modes, modes, lane_blocks)
    for h, half in enumerate(halves(lane_blocks)):
        for m in range(modes):
            r = row_at(ps, 0, modes, h, m)
            c = row_at(ps, lane_blocks * modes, modes, h, m)
            table[0, m, half, :] = jnp.exp(-r)
            table[1, m, half, :] = c * jnp.sqrt(2.0 * r)
            table[2, m, half, :] = r
    zero = jnp.zeros((SUB, LANES), jnp.float32)
    for s in range(2):
        fetches[3 + s].wait()
        spread_rows(x.at[s], xs, s * lane_blocks * pitch, pitch, lane_blocks)
    for h, half in enumerate(halves(lane_blocks)):
        for s in range(2):
            w = [taps[1 + s, i, half, :] for i in range(tap_count)]

            def body(block, window):
                window = list(window)
                for k in range(SUB):
                    t = block * SUB + k
                    window.append(row_at(xs, s * lane_blocks * pitch, pitch, h, t))
                    pair[s, t, half, :] = total(w[i] * window[-1 - i] for i in range(tap_count))
                return tuple(window[-(tap_count - 1) :])

            lax.fori_loop(0, rows // SUB, body, (zero,) * (tap_count - 1))
            stores.append(
                pltpu.make_async_copy(
                    pair.at[s, :, half, :], pair_far.at[s, :, half, :], sems.at[6 + 2 * h + s]
                )
            )
            stores[-1].start()
            first_rows[s, :, half, :] = pair[s, :SUB, half, :]
        decay = [table[0, m, half, :] for m in range(modes)]

        def step(t, state):
            u = pair[0, t, half, :] * pair[1, t, half, :]
            return tuple(decay[m] * state[m] + u for m in range(modes))

        state = (zero,) * modes
        for t in range(tap_count - 1, SUB):
            state = step(t, state)

        def block_step(block, state):
            for k in range(SUB):
                state = step(block * SUB + k, state)
            return state

        state = lax.fori_loop(1, rows // SUB, block_step, state)
        for m in range(modes):
            ends[m, half, :] = state[m]
    for store in stores:
        store.wait()


def head_kernel(rows, first_in, halo, table, taps, ends, first_rows, state_out, hs):
    modes, lane_blocks = ends.shape[:2]
    reach = taps.shape[1] - 1
    for s in range(2):
        spread_rows(halo.at[1 + s], hs, s * lane_blocks * SUB, SUB, lane_blocks)
    for h, half in enumerate(halves(lane_blocks)):
        heads = []
        for s in range(2):
            w = [taps[1 + s, i, half, :] for i in range(reach + 1)]
            before = [row_at(hs, s * lane_blocks * SUB, SUB, h, j) for j in range(SUB)]
            head = []
            for t in range(SUB):
                row = first_in[s, t, half, :]
                if t < reach:
                    row = row + total(w[i] * before[SUB + t - i] for i in range(t + 1, reach + 1))
                    head.append(row)
                first_rows[s, t, half, :] = row
            heads.append(head)
        product = [heads[0][t] * heads[1][t] for t in range(reach)]
        for m in range(modes):
            decay = table[0, m, half, :]
            state = product[0]
            for t in range(1, reach):
                state = decay * state + product[t]
            fade = jnp.exp(table[2, m, half, :] * -float(rows - reach))
            state_out[m, half, :] = ends[m, half, :] + fade * state


def query_kernel(x_far, halo, taps, gain, grad_far, query, scaled, x, grad, xs, gs, sems):
    rows, channels = x.shape
    lane_blocks = channels // LANES
    tap_count = taps.shape[1]
    pitch = rows + SUB
    fetches = [
        pltpu.make_async_copy(x_far.at[0], x, sems.at[0]),
        pltpu.make_async_copy(grad_far, grad, sems.at[1]),
    ]
    for fetch in fetches:
        fetch.start()
    spread_rows(halo.at[0], xs, 0, pitch, lane_blocks)
    fetches[0].wait()
    spread_rows(x, xs, SUB, pitch, lane_blocks)
    fetches[1].wait()
    spread_rows(grad, gs, 0, pitch, lane_blocks)
    for h, half in enumerate(halves(lane_blocks)):
        w = [taps[0, i, half, :] for i in range(tap_count)]
        g = gain[half, :]

        def body(block, window):
            window = list(window)
            for k in range(SUB):
                t = block * SUB + k
                window.append(row_at(xs, SUB, pitch, h, t))
                query[t, half, :] = total(w[i] * window[-1 - i] for i in range(tap_count))
                scaled[t, half, :] = g * row_at(gs, 0, pitch, h, t)
            return tuple(window[-(tap_count - 1) :])

        lax.fori_loop(
            0, rows // SUB, body, tuple(row_at(xs, 0, pitch, h, SUB + 1 - tap_count + j) for j in range(tap_count - 1))
        )


def local_kernel(pair, first_rows, table, local, rows_far, sem):
    rows = local.shape[0]
    modes, lane_blocks = table.shape[1:3]
    zero = jnp.zeros((SUB, LANES), jnp.float32)
    store = pltpu.make_async_copy(first_rows, rows_far, sem)
    store.start()
    for half in halves(lane_blocks):
        decay = [table[0, m, half, :] for m in range(modes)]
        scale = [table[1, m, half, :] for m in range(modes)]

        def block_step(source, block, state):
            for k in range(SUB):
                t = block * SUB + k
                u = source[0, t, half, :] * source[1, t, half, :]
                state = tuple(decay[m] * state[m] + u for m in range(modes))
                local[t, half, :] = total(scale[m] * state[m] for m in range(modes))
            return state

        state = block_step(first_rows, 0, (zero,) * modes)
        lax.fori_loop(1, rows // SUB, functools.partial(block_step, pair), state)
    store.wait()


def carry_kernel(entering, received, table, query, local, scaled, long_conv, sums, sq, cr):
    rows = local.shape[0]
    modes, lane_blocks = table.shape[1:3]
    for h, half in enumerate(halves(lane_blocks)):
        decay = [table[0, m, half, :] for m in range(modes)]
        start = []
        for m in range(modes):
            fade = jnp.exp(table[2, m, half, :] * -float(rows))
            incoming = fade * entering[m, half, :] + received[m, half, :]
            start.append(table[1, m, half, :] * decay[m] * incoming)

        def block_step(block, state):
            for k in range(SUB):
                t = block * SUB + k
                row = local[t, half, :] + total(state)
                state = tuple(decay[m] * state[m] for m in range(modes))
                long_conv[t, half, :] = row
                modulated = query[t, half, :] * row
                place = pl.ds(pl.multiple_of(t * SUB, SUB), SUB)
                square = modulated * modulated
                cross = scaled[t, half, :] * modulated
                sq[place, :] = square if h == 0 else sq[place, :] + square
                cr[place, :] = cross if h == 0 else cr[place, :] + cross
            return state

        lax.fori_loop(0, rows // SUB, block_step, tuple(start))
    for which, ref in enumerate((sq, cr)):
        blocks = []
        for b in range(rows // SUB):
            blocks.append(
                total(
                    ref[pl.ds(b * SUB * SUB + s, SUB, stride=SUB), :] for s in range(SUB)
                )
            )
        by_row = jnp.concatenate(blocks, axis=0)
        sums[which : which + 1, :] = jnp.sum(jnp.transpose(by_row), axis=0, keepdims=True)


def mixed_kernel(
    width, sums, table, query, long_conv, scaled, rows_far, mixed, long_grad, state_out, inv, head, inv_s, off_s,
    first_rows, sem,
):
    fetch = pltpu.make_async_copy(rows_far, first_rows, sem)
    fetch.start()
    rows = long_conv.shape[0]
    modes, lane_blocks = table.shape[1:3]
    zero = jnp.zeros((SUB, LANES), jnp.float32)
    inverse = lax.rsqrt(sums[0:1, :] / width + EPSILON)
    offset = inverse * inverse * inverse * sums[1:2, :] / width
    inv_s[...] = jnp.transpose(jnp.broadcast_to(inverse, (LANES, rows)))
    off_s[...] = jnp.transpose(jnp.broadcast_to(offset, (LANES, rows)))
    inv[...] = inv_s[...]
    blocks = rows // SUB
    for half in halves(lane_blocks):
        decay = [table[0, m, half, :] for m in range(modes)]

        def row(t, state):
            q = query[t, half, :]
            modulated = q * long_conv[t, half, :]
            mix = inv_s[pl.ds(t, 1), :] * scaled[t, half, :] - off_s[pl.ds(t, 1), :] * modulated
            mixed[t, half, :] = mix
            lg = mix * q
            long_grad[t, half, :] = lg
            return tuple(decay[m] * state[m] + lg for m in range(modes))

        def block_step(block, state):
            for k in range(SUB):
                state = row((blocks - 1 - block) * SUB + SUB - 1 - k, state)
            return state

        state = lax.fori_loop(0, blocks - 1, block_step, (zero,) * modes)
        if half.start == 0:
            fetch.wait()
        for t in reversed(range(SUB)):
            state = row(t, state)
            if t < head.shape[1]:
                gated = total(table[1, m, half, :] * state[m] for m in range(modes))
                found = (
                    mixed[t, half, :] * long_conv[t, half, :],
                    gated,
                    first_rows[1, t, half, :],
                    first_rows[0, t, half, :],
                )
                for i, value in enumerate(found):
                    head[i, t, half, :] = value
        for m in range(modes):
            state_out[m, half, :] = state[m]


def back_kernel(table, long_grad, local):
    rows = long_grad.shape[0]
    modes, lane_blocks = table.shape[1:3]
    blocks = rows // SUB
    zero = jnp.zeros((SUB, LANES), jnp.float32)
    for half in halves(lane_blocks):
        decay = [table[0, m, half, :] for m in range(modes)]
        scale = [table[1, m, half, :] for m in range(modes)]

        def block_step(block, state):
            for k in range(SUB):
                t = (blocks - 1 - block) * SUB + SUB - 1 - k
                lg = long_grad[t, half, :]
                state = tuple(decay[m] * state[m] + lg for m in range(modes))
                local[t, half, :] = total(scale[m] * state[m] for m in range(modes))
            return state

        lax.fori_loop(0, blocks, block_step, (zero,) * modes)

def output_kernel(inv, taps, gain, query, long_conv, mixed, head_in, output, finished, last, head, os, qs):
    head[...] = head_in[...].astype(head.dtype)
    rows = long_conv.shape[0]
    lane_blocks = taps.shape[2]
    tap_count = taps.shape[1]
    pitch = rows + SUB
    blocks = rows // SUB
    zero = jnp.zeros((SUB, LANES), jnp.float32)
    for h, half in enumerate(halves(lane_blocks)):
        g = gain[half, :]
        w = [taps[0, i, half, :] for i in range(tap_count)]

        def out_step(block, window):
            window = list(window)
            for k in range(SUB):
                t = (blocks - 1 - block) * SUB + SUB - 1 - k
                long_row = long_conv[t, half, :]
                window.insert(0, mixed[t, half, :] * long_row)
                row = g * (query[t, half, :] * long_row) * inv[pl.ds(t, 1), :]
                os[pl.ds(h * SUB * pitch + t, SUB, stride=pitch), :] = row
                qs[pl.ds(h * SUB * pitch + t, SUB, stride=pitch), :] = total(
                    w[i] * window[i] for i in range(tap_count)
                )
            return tuple(window[: tap_count - 1])

        lax.fori_loop(0, blocks, out_step, (zero,) * (tap_count - 1))
    for lb in range(lane_blocks):
        columns = slice(lb * LANES, (lb + 1) * LANES)
        output[:, columns] = os[pl.ds(lb * pitch, rows), :].astype(output.dtype)
        finished[:, columns] = qs[pl.ds(lb * pitch, rows), :].astype(finished.dtype)
        last[pl.ds(lb * SUB, SUB), :] = qs[pl.ds(lb * pitch + rows - SUB, SUB), :]


def far_rows(table, half, state, rows, reach, fade_first):
    modes = table.shape[1]
    at = [
        table[1, m, half, :]
        * state[m]
        * jnp.exp(table[2, m, half, :] * -float(rows - reach + 1 + fade_first))
        for m in range(modes)
    ]
    found = [None] * reach
    for i in reversed(range(reach)):
        found[i] = total(at)
        if i:
            at = [at[m] * table[0, m, half, :] for m in range(modes)]
    return found


def join_kernel(rows, span, place, table, state, entering, gathered, got, entering_out, message):
    modes, lane_blocks = state.shape[:2]
    column = lax.div(place[0], 2)
    upper = jnp.full((SUB, LANES), lax.rem(lax.div(column, span), 2)) > 0
    offset = lax.rem(column, span).astype(jnp.float32) * float(2 * rows)
    is_lower = jnp.full((SUB, LANES), lax.rem(place[0], 2)) == 0
    last = message.dtype == jnp.float32
    for half in halves(lane_blocks):
        for m in range(modes):
            rate = table[2, m, half, :]
            other = got[m, half, :].astype(jnp.float32)
            e = jnp.where(upper, jnp.exp(rate * -offset) * other, 0.0)
            if span > 1:
                e = entering[m, half, :] + e
            entering_out[m, half, :] = e
            if last:
                joined = jnp.exp(rate * -float(2 * rows)) * e + state[m, half, :]
                message[m, half, :] = jnp.where(is_lower, joined, e)
            else:
                mine = gathered[m, half, :].astype(jnp.float32)
                fade = jnp.exp(rate * -float(2 * rows * span))
                message[m, half, :] = (
                    jnp.where(upper, mine, other) + fade * jnp.where(upper, other, mine)
                ).astype(message.dtype)


def join_back_kernel(
    rows, reach, span, place, table, state, entering, beyond, added, gathered, got,
    entering_out, beyond_out, added_out, message, *extra,
):
    modes, lane_blocks = state.shape[:2]
    column = lax.div(place[0], 2)
    within = lax.rem(column, span)
    upper = jnp.full((SUB, LANES), lax.rem(lax.div(column, span), 2)) > 0
    is_last = jnp.full((SUB, LANES), within) == span - 1
    to_end = (span - 1 - within).astype(jnp.float32) * float(2 * rows)
    is_lower = jnp.full((SUB, LANES), lax.rem(place[0], 2)) == 0
    last = message.dtype == jnp.float32
    for half in halves(lane_blocks):
        sent = []
        for m in range(modes):
            rate = table[2, m, half, :]
            other = got[m, half, :].astype(jnp.float32)
            reached = jnp.where(upper, 0.0, jnp.exp(rate * -to_end) * other)
            e, f = reached, jnp.zeros((SUB, LANES), jnp.float32)
            if span > 1:
                e = entering[m, half, :] + e
                onward = jnp.exp(rate * -jnp.maximum(to_end - float(2 * rows), 0.0)) * other
                f = beyond[m, half, :] + jnp.where(upper | is_last, 0.0, onward)
            entering_out[m, half, :] = e
            beyond_out[m, half, :] = f
            if last:
                joined = jnp.exp(rate * -float(2 * rows)) * e + state[m, half, :]
                message[m, half, :] = jnp.where(is_lower, e, joined)
                sent.append(jnp.where(is_lower, f, e))
            else:
                mine = gathered[m, half, :].astype(jnp.float32)
                low, high = jnp.where(upper, other, mine), jnp.where(upper, mine, other)
                fade = jnp.exp(rate * -float(2 * rows * span))
                message[m, half, :] = (low + fade * high).astype(message.dtype)
                fade = jnp.exp(rate * -float(2 * rows * (span - 1)))
                sent.append(fade * high)
        found = far_rows(table, half, sent, rows, reach, rows)
        for i in range(reach):
            here = jnp.zeros((SUB, LANES), jnp.float32)
            if span > 1:
                mine, other = gathered[modes + i, half, :], got[modes + i, half, :]
                here = added[i, half, :] + jnp.where(upper | ~is_last, 0.0, other.astype(jnp.float32))
                low = jnp.where(upper, other.astype(jnp.float32), mine.astype(jnp.float32))
            added_out[i, half, :] = here
            if last:
                extra[0][i, half, :] = (found[i] + jnp.where(is_lower, here, 0.0)).astype(extra[0].dtype)
            else:
                rest = found[i] if span == 1 else found[i] + low
                message[modes + i, half, :] = rest.astype(message.dtype)


def final_kernel(
    entering, received, received_rows, table, taps, pair, first_rows, local, query, last, head, grads, cg, os, ls, made, edge, sems
):
    rows = local.shape[0]
    modes, lane_blocks = table.shape[1:3]
    tap_count = taps.shape[1]
    reach = tap_count - 1
    pitch = rows + SUB
    blocks = rows // SUB
    kept = rows - 2 * SUB
    moves = [
        pltpu.make_async_copy(
            query.at[pl.ds(0, kept), :], grads.at[0, pl.ds(0, kept), :], sems.at[0]
        )
    ]
    moves[0].start()
    ls[...] = last[...]
    for h, half in enumerate(halves(lane_blocks)):
        decay = [table[0, m, half, :] for m in range(modes)]
        start = []
        for m in range(modes):
            fade = jnp.exp(table[2, m, half, :] * -float(rows))
            incoming = fade * entering[m, half, :] + received[m, half, :]
            start.append(table[1, m, half, :] * decay[m] * incoming)

        def block_step(source, block, state):
            for k in range(SUB):
                t = (blocks - 1 - block) * SUB + SUB - 1 - k
                gated = local[t, half, :] + total(state)
                state = tuple(decay[m] * state[m] for m in range(modes))
                cg[0, t, :, :] = gated * source[1, t, half, :]
                cg[1, t, :, :] = gated * source[0, t, half, :]
            return state

        state = lax.fori_loop(0, blocks - 1, functools.partial(block_step, pair), tuple(start))
        block_step(first_rows, blocks - 1, state)
        own = far_rows(table, half, [entering[m, half, :] for m in range(modes)], rows, reach, 0)
        beyond = [[], [], []]
        for i in range(reach):
            gated = head[1, i, half, :].astype(jnp.float32) + received_rows[i, half, :].astype(jnp.float32) + own[i]
            beyond[0].append(head[0, i, half, :].astype(jnp.float32))
            beyond[1].append(gated * head[2, i, half, :].astype(jnp.float32))
            beyond[2].append(gated * head[3, i, half, :].astype(jnp.float32))
        for t in range(SUB - reach, SUB):
            place = pl.ds(h * SUB * SUB + t, SUB, stride=SUB)
            ls[place, :] += total(
                taps[0, i, half, :] * beyond[0][t + i - SUB] for i in range(SUB - t, tap_count)
            )
        for s in range(1, 3):
            w = [taps[s, i, half, :] for i in range(tap_count)]

            def conv_step(block, window):
                window = list(window)
                for k in range(SUB):
                    t = (blocks - 1 - block) * SUB + SUB - 1 - k
                    window.insert(0, cg[s - 1, t, :, :])
                    os[pl.ds(t, SUB, stride=pitch), :] = total(
                        w[i] * window[i] for i in range(tap_count)
                    )
                return tuple(window[:reach])

            lax.fori_loop(0, blocks, conv_step, tuple(beyond[s]))
            for lb in range(SUB):
                first = (h * SUB + lb) * LANES
                made[s - 1, :, first : first + LANES] = os[pl.ds(lb * pitch, rows), :].astype(made.dtype)
            columns = pl.ds(h * SUB * LANES, SUB * LANES)
            moves.append(
                pltpu.make_async_copy(
                    made.at[s - 1, :, columns], grads.at[s, :, columns], sems.at[len(moves)]
                )
            )
            moves[-1].start()
    for lb in range(lane_blocks):
        columns = slice(lb * LANES, (lb + 1) * LANES)
        ending = jnp.concatenate(
            [query[kept : kept + SUB, columns].astype(jnp.float32), ls[pl.ds(lb * SUB, SUB), :]], axis=0
        )
        edge[:, columns] = ending.astype(edge.dtype)
    moves.append(
        pltpu.make_async_copy(edge, grads.at[0, pl.ds(kept, 2 * SUB), :], sems.at[len(moves)])
    )
    moves[-1].start()
    for move in moves:
        move.wait()


def kept(*shape, dtype=jnp.float32):
    return pltpu.VMEM(shape, dtype)


def run(kernel, ins, outs, scratch=(), work=0, aliases=None):
    ins = [pltpu.with_memory_space_constraint(a, space) for a, space in ins]
    spaces = [getattr(o, "memory_space", pltpu.VMEM) for o in outs]
    return pl.pallas_call(
        kernel,
        out_shape=outs,
        in_specs=[pl.BlockSpec(memory_space=jax.typeof(a).memory_space) for a in ins],
        out_specs=[pl.BlockSpec(memory_space=space) for space in spaces],
        scratch_shapes=[pltpu.VMEM(s, jnp.float32) if isinstance(s, tuple) else s for s in scratch],
        input_output_aliases=aliases or {},
        compiler_params=pltpu.CompilerParams(vmem_limit_bytes=VMEM_LIMIT),
        cost_estimate=pl.CostEstimate(flops=work, bytes_accessed=4 * 1024 * 1024, transcendentals=0),
    )(*ins)


def shifted(block, distance):
    devices = range(lax.axis_size("ctx"))
    route = [(i, i + distance) for i in devices if i + distance in devices]
    return lax.ppermute(block, "ctx", route)


def swapped(block, distance):
    return lax.ppermute(block, "ctx", [(i, i ^ distance) for i in range(lax.axis_size("ctx"))])


def on_device(streams, short_filter, decay_rate, residue, norm_gain, out_grad):
    rows, channels = streams.shape[1:]
    modes = decay_rate.shape[0]
    lane_blocks = channels // LANES
    tap_count = short_filter.shape[2]
    reach = tap_count - 1
    pitch = rows + SUB
    count = lax.axis_size("ctx")
    row_shape = (rows, lane_blocks, LANES)
    state_shape = (modes, lane_blocks, LANES)
    bf16 = jnp.bfloat16

    def v(*arrays):
        return [(a, pltpu.VMEM) for a in arrays]

    def far(*arrays):
        return [(a, pltpu.HBM) for a in arrays]

    (tail,) = run(
        tail_kernel,
        far(streams),
        [jax.ShapeDtypeStruct((3, SUB, channels), bf16)],
        (pltpu.VMEM((3, 2 * SUB, channels), bf16), pltpu.SemaphoreType.DMA(())),
    )
    halo = shifted(tail, 1)
    gain = norm_gain.reshape(lane_blocks, LANES)
    pair_far, taps_far, first_rows, table, taps, ends = run(
        prepare_kernel,
        far(streams, jnp.swapaxes(short_filter, 1, 2), decay_rate, residue),
        [
            pltpu.HBM((2, *row_shape), jnp.float32),
            pltpu.HBM((3, tap_count, lane_blocks, LANES), jnp.float32),
            kept(2, SUB, lane_blocks, LANES),
            kept(3, *state_shape),
            kept(3, tap_count, lane_blocks, LANES),
            kept(*state_shape),
        ],
        (
            pltpu.VMEM((2, rows, channels), bf16),
            pltpu.VMEM((3, tap_count, channels // GROUP), bf16),
            (modes, channels),
            (modes, channels),
            (2, *row_shape),
            (2 * lane_blocks * pitch, LANES),
            (2 * lane_blocks * modes, LANES),
            pltpu.SemaphoreType.DMA((6 + lane_blocks // 4,)),
        ),
        work=10**9,
    )
    first_rows, state = run(
        functools.partial(head_kernel, rows),
        v(first_rows, halo, table, taps, ends),
        [kept(2, SUB, lane_blocks, LANES), jax.ShapeDtypeStruct(state_shape, jnp.float32)],
        ((2 * lane_blocks * SUB, LANES),),
    )
    place = lax.axis_index("ctx").astype(jnp.int32)[None]

    query, scaled = run(
        query_kernel,
        far(streams) + v(halo, taps, gain) + far(out_grad),
        [kept(*row_shape), kept(*row_shape)],
        (
            pltpu.VMEM((rows, channels), bf16),
            pltpu.VMEM((rows, channels), bf16),
            (lane_blocks * pitch, LANES),
            (lane_blocks * pitch, LANES),
            pltpu.SemaphoreType.DMA((2,)),
        ),
        work=2 * 10**9,
    )
    local, rows_far = run(
        local_kernel,
        v(pair_far, first_rows, table),
        [kept(*row_shape), pltpu.HBM((2, SUB, lane_blocks, LANES), jnp.float32)],
        (pltpu.SemaphoreType.DMA(()),),
        work=2 * 10**9,
    )
    entering = gathered = state
    span = 1
    while 2 * span < count:
        got = swapped(gathered, 2 * span)
        if span == 1:
            got, query, scaled = lax.optimization_barrier((got, query, scaled))
        if 4 * span >= count:
            got, local = lax.optimization_barrier((got, local))
        entering, gathered = run(
            functools.partial(join_kernel, rows, span),
            [(place, pltpu.SMEM)] + v(table, state, entering, gathered, got),
            [
                kept(*state_shape),
                jax.ShapeDtypeStruct(state_shape, jnp.float32 if 4 * span >= count else bf16),
            ],
        )
        span *= 2
    received = swapped(gathered, 1)
    long_conv, sums = run(
        carry_kernel,
        v(entering, received, table, query, local, scaled),
        [kept(*row_shape), kept(2, rows)],
        ((rows * SUB, LANES), (rows * SUB, LANES)),
        aliases={4: 0},
    )
    sums = lax.psum(sums, "tp")
    mixed, long_grad, back, inv, head = run(
        functools.partial(mixed_kernel, float(channels * lax.axis_size("tp"))),
        v(sums, table, query, long_conv, scaled) + far(rows_far),
        [
            kept(*row_shape),
            kept(*row_shape),
            jax.ShapeDtypeStruct(state_shape, jnp.float32),
            kept(rows, LANES),
            kept(4, reach, lane_blocks, LANES),
        ],
        (
            (rows, LANES),
            (rows, LANES),
            (2, SUB, lane_blocks, LANES),
            pltpu.SemaphoreType.DMA(()),
        ),
        aliases={4: 0},
    )

    (local_back,) = run(
        back_kernel, v(table, long_grad), [kept(*row_shape)], work=2 * 10**9
    )
    output, finished, last, head = run(
        output_kernel,
        v(inv, taps_far, gain, query, long_conv, mixed, head),
        [
            jax.ShapeDtypeStruct((rows, channels), bf16),
            kept(rows, channels, dtype=bf16),
            kept(lane_blocks * SUB, LANES),
            jax.ShapeDtypeStruct(head.shape, bf16),
        ],
        ((lane_blocks * pitch, LANES), (lane_blocks * pitch, LANES)),
        work=2 * 10**9,
    )
    entering = beyond = added = gathered = back
    message_shape = (modes + reach, lane_blocks, LANES)
    span = 1
    while 2 * span < count:
        got = swapped(gathered, 2 * span)
        if span == 1:
            got, local_back = lax.optimization_barrier((got, local_back))
        if 4 * span >= count:
            got, finished = lax.optimization_barrier((got, finished))
        entering, beyond, added, gathered, *extra = run(
            functools.partial(join_back_kernel, rows, reach, span),
            [(place, pltpu.SMEM)] + v(table, back, entering, beyond, added, gathered, got),
            [
                kept(*state_shape),
                kept(*state_shape),
                kept(reach, lane_blocks, LANES),
            ]
            + (
                [
                    jax.ShapeDtypeStruct(state_shape, jnp.float32),
                    jax.ShapeDtypeStruct((reach, lane_blocks, LANES), bf16),
                ]
                if 4 * span >= count
                else [jax.ShapeDtypeStruct(message_shape, bf16)]
            ),
        )
        span *= 2
    head = shifted(head, -1)
    received_back, received_rows = swapped(gathered, 1), swapped(extra[0], 1)
    (grads,) = run(
        final_kernel,
        v(entering, received_back, received_rows, table, taps_far, pair_far, rows_far, local_back, finished, last, head),
        [pltpu.HBM((3, rows, channels), bf16)],
        (
            (2, rows, SUB, LANES),
            (SUB * pitch, LANES),
            (lane_blocks * SUB, LANES),
            pltpu.VMEM((2, rows, channels), bf16),
            pltpu.VMEM((2 * SUB, channels), bf16),
            pltpu.SemaphoreType.DMA((2 + lane_blocks // 4,)),
        ),
    )
    return output, grads


def solution(mesh):
    return jax.shard_map(
        on_device,
        mesh=mesh,
        in_specs=(
            P(None, "ctx", "tp"),
            P(None, "tp", None),
            P(None, "tp"),
            P(None, "tp"),
            P("tp"),
            P("ctx", "tp"),
        ),
        out_specs=(P("ctx", "tp"), P(None, "ctx", "tp")),
        check_vma=False,
    )
```

```python
import functools

import jax
import jax.numpy as jnp
from jax import lax
from jax.experimental import pallas as pl
from jax.experimental.pallas import tpu as pltpu
from jax.sharding import PartitionSpec as P

GROUP = 16
LANES = 128
SUB = 8
EPSILON = 1e-05
VMEM_LIMIT = 16 * 1024 * 1024


def halves(lane_blocks):
    return [pl.ds(SUB * h, SUB) for h in range(lane_blocks // SUB)]


def total(terms):
    terms = list(terms)
    while len(terms) > 1:
        paired = [terms[i] + terms[i + 1] for i in range(0, len(terms) - 1, 2)]
        terms = paired + ([terms[-1]] if len(terms) % 2 else [])
    return terms[0]


def spread_rows(source, target, first, pitch, lane_blocks):
    rows = source.shape[0]
    for lb in range(lane_blocks):
        tile = source[:, lb * LANES : (lb + 1) * LANES]
        target[pl.ds(first + lb * pitch, rows), :] = tile.astype(jnp.float32)


def to_send(table, half, states, lag):
    modes = table.shape[1]
    down, off_down, up, off_up, chosen, off = [], [], [], [], [], []
    for m in range(modes):
        x = states[m]
        near = x.astype(jnp.bfloat16).astype(jnp.float32)
        other = (x + jnp.where(near < x, 0.00390625, -0.00390625) * jnp.abs(x)).astype(jnp.bfloat16).astype(jnp.float32)
        weight = table[1, m, half, :] * jnp.exp(table[2, m, half, :] * -float(lag))
        down.append(near)
        up.append(other)
        off_down.append(weight * (near - x))
        off_up.append(weight * (other - x))
    sum_off = jnp.zeros((SUB, LANES), jnp.float32)
    for turn in range(2):
        for m in range(modes):
            base = sum_off if turn == 0 else sum_off - off[m]
            first, second = base + off_down[m], base + off_up[m]
            take = jnp.abs(second) < jnp.abs(first)
            sum_off = jnp.where(take, second, first)
            if turn == 0:
                off.append(jnp.where(take, off_up[m], off_down[m]))
            else:
                chosen.append(jnp.where(take, up[m], down[m]).astype(jnp.bfloat16))
    return chosen


def row_at(ref, first, pitch, half, place):
    return ref[pl.ds(first + half * SUB * pitch + place, SUB, stride=pitch), :]


def tail_kernel(x, tail, edge, sem):
    rows = x.shape[1]
    move = pltpu.make_async_copy(x.at[:, pl.ds(rows - 2 * SUB, 2 * SUB), :], edge, sem)
    move.start()
    move.wait()
    tail[...] = edge[:, SUB:, :]


def prepare_kernel(
    x_far, filt_far, rate_far, res_far, pair_far, taps_far, first_rows, table, taps, ends,
    x, filt, rate, res, pair, xs, ps, sems,
):
    rows, channels = x.shape[1:]
    modes = rate.shape[0]
    lane_blocks = channels // LANES
    tap_count = taps.shape[1]
    pitch = rows + SUB
    fetches = [
        pltpu.make_async_copy(source, target, sems.at[i])
        for i, (source, target) in enumerate(
            [(filt_far, filt), (rate_far, rate), (res_far, res)]
            + [(x_far.at[1 + s], x.at[s]) for s in range(2)]
        )
    ]
    for fetch in fetches:
        fetch.start()
    spread = (
        lax.broadcasted_iota(jnp.int32, (channels // GROUP, channels), 1) // GROUP
        == lax.broadcasted_iota(jnp.int32, (channels // GROUP, channels), 0)
    ).astype(jnp.bfloat16)
    fetches[0].wait()
    for s in range(3):
        weights = jnp.dot(filt[s], spread, preferred_element_type=jnp.float32)
        for lb in range(lane_blocks):
            ps[pl.ds(lb * SUB, tap_count), :] = weights[:, lb * LANES : (lb + 1) * LANES]
        for h, half in enumerate(halves(lane_blocks)):
            for i in range(tap_count):
                taps[s, i, half, :] = row_at(ps, 0, SUB, h, i)
    stores = [pltpu.make_async_copy(taps, taps_far, sems.at[5])]
    stores[0].start()
    fetches[1].wait()
    fetches[2].wait()
    spread_rows(rate, ps, 0, modes, lane_blocks)
    spread_rows(res, ps, lane_blocks * modes, modes, lane_blocks)
    for h, half in enumerate(halves(lane_blocks)):
        for m in range(modes):
            r = row_at(ps, 0, modes, h, m)
            c = row_at(ps, lane_blocks * modes, modes, h, m)
            table[0, m, half, :] = jnp.exp(-r)
            table[1, m, half, :] = c * jnp.sqrt(2.0 * r)
            table[2, m, half, :] = r
    zero = jnp.zeros((SUB, LANES), jnp.float32)
    for s in range(2):
        fetches[3 + s].wait()
        spread_rows(x.at[s], xs, s * lane_blocks * pitch, pitch, lane_blocks)
    for h, half in enumerate(halves(lane_blocks)):
        for s in range(2):
            w = [taps[1 + s, i, half, :] for i in range(tap_count)]

            def body(block, window):
                window = list(window)
                for k in range(SUB):
                    t = block * SUB + k
                    window.append(row_at(xs, s * lane_blocks * pitch, pitch, h, t))
                    pair[s, t, half, :] = total(w[i] * window[-1 - i] for i in range(tap_count))
                return tuple(window[-(tap_count - 1) :])

            lax.fori_loop(0, rows // SUB, body, (zero,) * (tap_count - 1))
            stores.append(
                pltpu.make_async_copy(
                    pair.at[s, :, half, :], pair_far.at[s, :, half, :], sems.at[6 + 2 * h + s]
                )
            )
            stores[-1].start()
            first_rows[s, :, half, :] = pair[s, :SUB, half, :]
        decay = [table[0, m, half, :] for m in range(modes)]

        def step(t, state):
            u = pair[0, t, half, :] * pair[1, t, half, :]
            return tuple(decay[m] * state[m] + u for m in range(modes))

        state = (zero,) * modes
        for t in range(tap_count - 1, SUB):
            state = step(t, state)

        def block_step(block, state):
            for k in range(SUB):
                state = step(block * SUB + k, state)
            return state

        state = lax.fori_loop(1, rows // SUB, block_step, state)
        for m in range(modes):
            ends[m, half, :] = state[m]
    for store in stores:
        store.wait()


def head_kernel(rows, first_in, halo, table, taps, ends, first_rows, state_out, message, hs):
    modes, lane_blocks = ends.shape[:2]
    reach = taps.shape[1] - 1
    for s in range(2):
        spread_rows(halo.at[1 + s], hs, s * lane_blocks * SUB, SUB, lane_blocks)
    for h, half in enumerate(halves(lane_blocks)):
        heads = []
        for s in range(2):
            w = [taps[1 + s, i, half, :] for i in range(reach + 1)]
            before = [row_at(hs, s * lane_blocks * SUB, SUB, h, j) for j in range(SUB)]
            head = []
            for t in range(SUB):
                row = first_in[s, t, half, :]
                if t < reach:
                    row = row + total(w[i] * before[SUB + t - i] for i in range(t + 1, reach + 1))
                    head.append(row)
                first_rows[s, t, half, :] = row
            heads.append(head)
        product = [heads[0][t] * heads[1][t] for t in range(reach)]
        states = []
        for m in range(modes):
            decay = table[0, m, half, :]
            state = product[0]
            for t in range(1, reach):
                state = decay * state + product[t]
            fade = jnp.exp(table[2, m, half, :] * -float(rows - reach))
            states.append(ends[m, half, :] + fade * state)
            state_out[m, half, :] = states[m]
        for m, value in enumerate(to_send(table, half, states, rows)):
            message[m, half, :] = value


def query_kernel(x_far, halo, taps, gain, grad_far, query, scaled, x, grad, xs, gs, sems):
    rows, channels = x.shape
    lane_blocks = channels // LANES
    tap_count = taps.shape[1]
    pitch = rows + SUB
    fetches = [
        pltpu.make_async_copy(x_far.at[0], x, sems.at[0]),
        pltpu.make_async_copy(grad_far, grad, sems.at[1]),
    ]
    for fetch in fetches:
        fetch.start()
    spread_rows(halo.at[0], xs, 0, pitch, lane_blocks)
    fetches[0].wait()
    spread_rows(x, xs, SUB, pitch, lane_blocks)
    fetches[1].wait()
    spread_rows(grad, gs, 0, pitch, lane_blocks)
    for h, half in enumerate(halves(lane_blocks)):
        w = [taps[0, i, half, :] for i in range(tap_count)]
        g = gain[half, :]

        def body(block, window):
            window = list(window)
            for k in range(SUB):
                t = block * SUB + k
                window.append(row_at(xs, SUB, pitch, h, t))
                query[t, half, :] = total(w[i] * window[-1 - i] for i in range(tap_count))
                scaled[t, half, :] = g * row_at(gs, 0, pitch, h, t)
            return tuple(window[-(tap_count - 1) :])

        lax.fori_loop(
            0, rows // SUB, body, tuple(row_at(xs, 0, pitch, h, SUB + 1 - tap_count + j) for j in range(tap_count - 1))
        )


def local_kernel(pair, first_rows, table, local, rows_far, sem):
    rows = local.shape[0]
    modes, lane_blocks = table.shape[1:3]
    zero = jnp.zeros((SUB, LANES), jnp.float32)
    store = pltpu.make_async_copy(first_rows, rows_far, sem)
    store.start()
    for half in halves(lane_blocks):
        decay = [table[0, m, half, :] for m in range(modes)]
        scale = [table[1, m, half, :] for m in range(modes)]

        def block_step(source, block, state):
            for k in range(SUB):
                t = block * SUB + k
                u = source[0, t, half, :] * source[1, t, half, :]
                state = tuple(decay[m] * state[m] + u for m in range(modes))
                local[t, half, :] = total(scale[m] * state[m] for m in range(modes))
            return state

        state = block_step(first_rows, 0, (zero,) * modes)
        lax.fori_loop(1, rows // SUB, functools.partial(block_step, pair), state)
    store.wait()


def carry_kernel(entering, received, table, query, local, scaled, long_conv, sums, sq, cr):
    rows = local.shape[0]
    modes, lane_blocks = table.shape[1:3]
    for h, half in enumerate(halves(lane_blocks)):
        decay = [table[0, m, half, :] for m in range(modes)]
        start = []
        for m in range(modes):
            fade = jnp.exp(table[2, m, half, :] * -float(rows))
            incoming = fade * entering[m, half, :] + received[m, half, :].astype(jnp.float32)
            start.append(table[1, m, half, :] * decay[m] * incoming)

        def block_step(block, state):
            for k in range(SUB):
                t = block * SUB + k
                row = local[t, half, :] + total(state)
                state = tuple(decay[m] * state[m] for m in range(modes))
                long_conv[t, half, :] = row
                modulated = query[t, half, :] * row
                place = pl.ds(pl.multiple_of(t * SUB, SUB), SUB)
                square = modulated * modulated
                cross = scaled[t, half, :] * modulated
                sq[place, :] = square if h == 0 else sq[place, :] + square
                cr[place, :] = cross if h == 0 else cr[place, :] + cross
            return state

        lax.fori_loop(0, rows // SUB, block_step, tuple(start))
    for which, ref in enumerate((sq, cr)):
        blocks = []
        for b in range(rows // SUB):
            blocks.append(
                total(
                    ref[pl.ds(b * SUB * SUB + s, SUB, stride=SUB), :] for s in range(SUB)
                )
            )
        by_row = jnp.concatenate(blocks, axis=0)
        sums[which : which + 1, :] = jnp.sum(jnp.transpose(by_row), axis=0, keepdims=True)


def mixed_kernel(
    width, sums, table, query, long_conv, scaled, rows_far, mixed, long_grad, state_out, message, inv, head, inv_s, off_s,
    first_rows, sem,
):
    fetch = pltpu.make_async_copy(rows_far, first_rows, sem)
    fetch.start()
    rows = long_conv.shape[0]
    modes, lane_blocks = table.shape[1:3]
    zero = jnp.zeros((SUB, LANES), jnp.float32)
    inverse = lax.rsqrt(sums[0:1, :] / width + EPSILON)
    offset = inverse * inverse * inverse * sums[1:2, :] / width
    inv_s[...] = jnp.transpose(jnp.broadcast_to(inverse, (LANES, rows)))
    off_s[...] = jnp.transpose(jnp.broadcast_to(offset, (LANES, rows)))
    inv[...] = inv_s[...]
    blocks = rows // SUB
    for half in halves(lane_blocks):
        decay = [table[0, m, half, :] for m in range(modes)]

        def row(t, state):
            q = query[t, half, :]
            modulated = q * long_conv[t, half, :]
            mix = inv_s[pl.ds(t, 1), :] * scaled[t, half, :] - off_s[pl.ds(t, 1), :] * modulated
            mixed[t, half, :] = mix
            lg = mix * q
            long_grad[t, half, :] = lg
            return tuple(decay[m] * state[m] + lg for m in range(modes))

        def block_step(block, state):
            for k in range(SUB):
                state = row((blocks - 1 - block) * SUB + SUB - 1 - k, state)
            return state

        state = lax.fori_loop(0, blocks - 1, block_step, (zero,) * modes)
        if half.start == 0:
            fetch.wait()
        for t in reversed(range(SUB)):
            state = row(t, state)
            if t < head.shape[1]:
                gated = total(table[1, m, half, :] * state[m] for m in range(modes))
                found = (
                    mixed[t, half, :] * long_conv[t, half, :],
                    gated,
                    first_rows[1, t, half, :],
                    first_rows[0, t, half, :],
                )
                for i, value in enumerate(found):
                    head[i, t, half, :] = value
        for m, value in enumerate(to_send(table, half, state, rows)):
            state_out[m, half, :] = state[m]
            message[m, half, :] = value


def back_kernel(table, long_grad, local):
    rows = long_grad.shape[0]
    modes, lane_blocks = table.shape[1:3]
    blocks = rows // SUB
    zero = jnp.zeros((SUB, LANES), jnp.float32)
    for half in halves(lane_blocks):
        decay = [table[0, m, half, :] for m in range(modes)]
        scale = [table[1, m, half, :] for m in range(modes)]

        def block_step(block, state):
            for k in range(SUB):
                t = (blocks - 1 - block) * SUB + SUB - 1 - k
                lg = long_grad[t, half, :]
                state = tuple(decay[m] * state[m] + lg for m in range(modes))
                local[t, half, :] = total(scale[m] * state[m] for m in range(modes))
            return state

        lax.fori_loop(0, blocks, block_step, (zero,) * modes)

def output_kernel(inv, taps, gain, query, long_conv, mixed, head_in, output, finished, last, head, os, qs):
    head[...] = head_in[...].astype(head.dtype)
    rows = long_conv.shape[0]
    lane_blocks = taps.shape[2]
    tap_count = taps.shape[1]
    pitch = rows + SUB
    blocks = rows // SUB
    zero = jnp.zeros((SUB, LANES), jnp.float32)
    for h, half in enumerate(halves(lane_blocks)):
        g = gain[half, :]
        w = [taps[0, i, half, :] for i in range(tap_count)]

        def out_step(block, window):
            window = list(window)
            for k in range(SUB):
                t = (blocks - 1 - block) * SUB + SUB - 1 - k
                long_row = long_conv[t, half, :]
                window.insert(0, mixed[t, half, :] * long_row)
                row = g * (query[t, half, :] * long_row) * inv[pl.ds(t, 1), :]
                os[pl.ds(h * SUB * pitch + t, SUB, stride=pitch), :] = row
                qs[pl.ds(h * SUB * pitch + t, SUB, stride=pitch), :] = total(
                    w[i] * window[i] for i in range(tap_count)
                )
            return tuple(window[: tap_count - 1])

        lax.fori_loop(0, blocks, out_step, (zero,) * (tap_count - 1))
    for lb in range(lane_blocks):
        columns = slice(lb * LANES, (lb + 1) * LANES)
        output[:, columns] = os[pl.ds(lb * pitch, rows), :].astype(output.dtype)
        finished[:, columns] = qs[pl.ds(lb * pitch, rows), :].astype(finished.dtype)
        last[pl.ds(lb * SUB, SUB), :] = qs[pl.ds(lb * pitch + rows - SUB, SUB), :]


def far_rows(table, half, state, rows, reach, fade_first):
    modes = table.shape[1]
    at = [
        table[1, m, half, :]
        * state[m]
        * jnp.exp(table[2, m, half, :] * -float(rows - reach + 1 + fade_first))
        for m in range(modes)
    ]
    found = [None] * reach
    for i in reversed(range(reach)):
        found[i] = total(at)
        if i:
            at = [at[m] * table[0, m, half, :] for m in range(modes)]
    return found


def join_kernel(rows, span, last, place, table, state, entering, gathered, got, entering_out, message, *gathered_out):
    modes, lane_blocks = state.shape[:2]
    column = lax.div(place[0], 2)
    upper = jnp.full((SUB, LANES), lax.rem(lax.div(column, span), 2)) > 0
    offset = lax.rem(column, span).astype(jnp.float32) * float(2 * rows)
    is_lower = jnp.full((SUB, LANES), lax.rem(place[0], 2)) == 0
    for half in halves(lane_blocks):
        sent = []
        for m in range(modes):
            rate = table[2, m, half, :]
            other = got[m, half, :].astype(jnp.float32)
            e = jnp.where(upper, jnp.exp(rate * -offset) * other, 0.0)
            if span > 1:
                e = entering[m, half, :] + e
            entering_out[m, half, :] = e
            if last:
                joined = jnp.exp(rate * -float(2 * rows)) * e + state[m, half, :]
                sent.append(jnp.where(is_lower, joined, e))
            else:
                mine = gathered[m, half, :]
                fade = jnp.exp(rate * -float(2 * rows * span))
                sent.append(jnp.where(upper, mine, other) + fade * jnp.where(upper, other, mine))
                gathered_out[0][m, half, :] = sent[m]
        for m, value in enumerate(to_send(table, half, sent, rows // 2 if last else rows)):
            message[m, half, :] = value


def join_back_kernel(
    rows, reach, span, last, place, table, state, entering, beyond, added, gathered, got,
    entering_out, message, *kept_out,
):
    modes, lane_blocks = state.shape[:2]
    column = lax.div(place[0], 2)
    within = lax.rem(column, span)
    upper = jnp.full((SUB, LANES), lax.rem(lax.div(column, span), 2)) > 0
    is_last = jnp.full((SUB, LANES), within) == span - 1
    to_end = (span - 1 - within).astype(jnp.float32) * float(2 * rows)
    is_lower = jnp.full((SUB, LANES), lax.rem(place[0], 2)) == 0
    for half in halves(lane_blocks):
        sent, far_on = [], []
        for m in range(modes):
            rate = table[2, m, half, :]
            other = got[m, half, :].astype(jnp.float32)
            e, f = jnp.where(upper, 0.0, jnp.exp(rate * -to_end) * other), jnp.zeros((SUB, LANES), jnp.float32)
            if span > 1:
                e = entering[m, half, :] + e
                onward = jnp.exp(rate * -jnp.maximum(to_end - float(2 * rows), 0.0)) * other
                f = beyond[m, half, :] + jnp.where(upper | is_last, 0.0, onward)
            entering_out[m, half, :] = e
            if not last:
                kept_out[0][m, half, :] = f
            if last:
                joined = jnp.exp(rate * -float(2 * rows)) * e + state[m, half, :]
                sent.append(jnp.where(is_lower, e, joined))
                far_on.append(jnp.where(is_lower, f, e))
            else:
                mine = gathered[m, half, :]
                low, high = jnp.where(upper, other, mine), jnp.where(upper, mine, other)
                fade = jnp.exp(rate * -float(2 * rows * span))
                sent.append(low + fade * high)
                kept_out[2][m, half, :] = sent[m]
                fade = jnp.exp(rate * -float(2 * rows * (span - 1)))
                far_on.append(fade * high)
        for m, value in enumerate(to_send(table, half, sent, rows // 2 if last else rows)):
            message[m, half, :] = value
        found = far_rows(table, half, far_on, rows, reach, rows)
        for i in range(reach):
            here, rest = jnp.zeros((SUB, LANES), jnp.float32), found[i]
            if span > 1:
                mine, other = gathered[modes + i, half, :], got[modes + i, half, :].astype(jnp.float32)
                here = added[i, half, :] + jnp.where(upper | ~is_last, 0.0, other)
                rest = rest + jnp.where(upper, other, mine)
            if last:
                message[modes + i, half, :] = (found[i] + jnp.where(is_lower, here, 0.0)).astype(message.dtype)
            else:
                message[modes + i, half, :] = rest.astype(message.dtype)
                kept_out[1][i, half, :] = here
                kept_out[2][modes + i, half, :] = rest


def final_kernel(
    entering, received, table, taps, pair, first_rows, local, query, last, head, grads, cg, os, ls, made, edge, sems
):
    rows = local.shape[0]
    modes, lane_blocks = table.shape[1:3]
    tap_count = taps.shape[1]
    reach = tap_count - 1
    pitch = rows + SUB
    blocks = rows // SUB
    kept = rows - 2 * SUB
    moves = [
        pltpu.make_async_copy(
            query.at[pl.ds(0, kept), :], grads.at[0, pl.ds(0, kept), :], sems.at[0]
        )
    ]
    moves[0].start()
    ls[...] = last[...]
    for h, half in enumerate(halves(lane_blocks)):
        decay = [table[0, m, half, :] for m in range(modes)]
        start = []
        for m in range(modes):
            fade = jnp.exp(table[2, m, half, :] * -float(rows))
            incoming = fade * entering[m, half, :] + received[m, half, :].astype(jnp.float32)
            start.append(table[1, m, half, :] * decay[m] * incoming)

        def block_step(source, block, state):
            for k in range(SUB):
                t = (blocks - 1 - block) * SUB + SUB - 1 - k
                gated = local[t, half, :] + total(state)
                state = tuple(decay[m] * state[m] for m in range(modes))
                cg[0, t, :, :] = gated * source[1, t, half, :]
                cg[1, t, :, :] = gated * source[0, t, half, :]
            return state

        state = lax.fori_loop(0, blocks - 1, functools.partial(block_step, pair), tuple(start))
        block_step(first_rows, blocks - 1, state)
        own = far_rows(table, half, [entering[m, half, :] for m in range(modes)], rows, reach, 0)
        beyond = [[], [], []]
        for i in range(reach):
            gated = head[1, i, half, :].astype(jnp.float32) + received[modes + i, half, :].astype(jnp.float32) + own[i]
            beyond[0].append(head[0, i, half, :].astype(jnp.float32))
            beyond[1].append(gated * head[2, i, half, :].astype(jnp.float32))
            beyond[2].append(gated * head[3, i, half, :].astype(jnp.float32))
        for t in range(SUB - reach, SUB):
            place = pl.ds(h * SUB * SUB + t, SUB, stride=SUB)
            ls[place, :] += total(
                taps[0, i, half, :] * beyond[0][t + i - SUB] for i in range(SUB - t, tap_count)
            )
        for s in range(1, 3):
            w = [taps[s, i, half, :] for i in range(tap_count)]

            def conv_step(block, window):
                window = list(window)
                for k in range(SUB):
                    t = (blocks - 1 - block) * SUB + SUB - 1 - k
                    window.insert(0, cg[s - 1, t, :, :])
                    os[pl.ds(t, SUB, stride=pitch), :] = total(
                        w[i] * window[i] for i in range(tap_count)
                    )
                return tuple(window[:reach])

            lax.fori_loop(0, blocks, conv_step, tuple(beyond[s]))
            for lb in range(SUB):
                first = (h * SUB + lb) * LANES
                made[s - 1, :, first : first + LANES] = os[pl.ds(lb * pitch, rows), :].astype(made.dtype)
            columns = pl.ds(h * SUB * LANES, SUB * LANES)
            moves.append(
                pltpu.make_async_copy(
                    made.at[s - 1, :, columns], grads.at[s, :, columns], sems.at[len(moves)]
                )
            )
            moves[-1].start()
    for lb in range(lane_blocks):
        columns = slice(lb * LANES, (lb + 1) * LANES)
        ending = jnp.concatenate(
            [query[kept : kept + SUB, columns].astype(jnp.float32), ls[pl.ds(lb * SUB, SUB), :]], axis=0
        )
        edge[:, columns] = ending.astype(edge.dtype)
    moves.append(
        pltpu.make_async_copy(edge, grads.at[0, pl.ds(kept, 2 * SUB), :], sems.at[len(moves)])
    )
    moves[-1].start()
    for move in moves:
        move.wait()


def kept(*shape, dtype=jnp.float32):
    return pltpu.VMEM(shape, dtype)


def run(kernel, ins, outs, scratch=(), work=0, aliases=None):
    ins = [pltpu.with_memory_space_constraint(a, space) for a, space in ins]
    spaces = [getattr(o, "memory_space", pltpu.VMEM) for o in outs]
    return pl.pallas_call(
        kernel,
        out_shape=outs,
        in_specs=[pl.BlockSpec(memory_space=jax.typeof(a).memory_space) for a in ins],
        out_specs=[pl.BlockSpec(memory_space=space) for space in spaces],
        scratch_shapes=[pltpu.VMEM(s, jnp.float32) if isinstance(s, tuple) else s for s in scratch],
        input_output_aliases=aliases or {},
        compiler_params=pltpu.CompilerParams(vmem_limit_bytes=VMEM_LIMIT),
        cost_estimate=pl.CostEstimate(flops=work, bytes_accessed=4 * 1024 * 1024, transcendentals=0),
    )(*ins)


def shifted(block, distance):
    devices = range(lax.axis_size("ctx"))
    route = [(i, i + distance) for i in devices if i + distance in devices]
    return lax.ppermute(block, "ctx", route)


def swapped(block, distance):
    return lax.ppermute(block, "ctx", [(i, i ^ distance) for i in range(lax.axis_size("ctx"))])


def on_device(streams, short_filter, decay_rate, residue, norm_gain, out_grad):
    rows, channels = streams.shape[1:]
    modes = decay_rate.shape[0]
    lane_blocks = channels // LANES
    tap_count = short_filter.shape[2]
    reach = tap_count - 1
    pitch = rows + SUB
    count = lax.axis_size("ctx")
    row_shape = (rows, lane_blocks, LANES)
    state_shape = (modes, lane_blocks, LANES)
    bf16 = jnp.bfloat16

    def v(*arrays):
        return [(a, pltpu.VMEM) for a in arrays]

    def far(*arrays):
        return [(a, pltpu.HBM) for a in arrays]

    (tail,) = run(
        tail_kernel,
        far(streams),
        [jax.ShapeDtypeStruct((3, SUB, channels), bf16)],
        (pltpu.VMEM((3, 2 * SUB, channels), bf16), pltpu.SemaphoreType.DMA(())),
    )
    halo = shifted(tail, 1)
    gain = norm_gain.reshape(lane_blocks, LANES)
    pair_far, taps_far, first_rows, table, taps, ends = run(
        prepare_kernel,
        far(streams, jnp.swapaxes(short_filter, 1, 2), decay_rate, residue),
        [
            pltpu.HBM((2, *row_shape), jnp.float32),
            pltpu.HBM((3, tap_count, lane_blocks, LANES), jnp.float32),
            kept(2, SUB, lane_blocks, LANES),
            kept(3, *state_shape),
            kept(3, tap_count, lane_blocks, LANES),
            kept(*state_shape),
        ],
        (
            pltpu.VMEM((2, rows, channels), bf16),
            pltpu.VMEM((3, tap_count, channels // GROUP), bf16),
            (modes, channels),
            (modes, channels),
            (2, *row_shape),
            (2 * lane_blocks * pitch, LANES),
            (2 * lane_blocks * modes, LANES),
            pltpu.SemaphoreType.DMA((6 + lane_blocks // 4,)),
        ),
        work=10**9,
    )
    first_rows, state, message = run(
        functools.partial(head_kernel, rows),
        v(first_rows, halo, table, taps, ends),
        [kept(2, SUB, lane_blocks, LANES), kept(*state_shape), jax.ShapeDtypeStruct(state_shape, bf16)],
        ((2 * lane_blocks * SUB, LANES),),
    )
    place = lax.axis_index("ctx").astype(jnp.int32)[None]

    query, scaled = run(
        query_kernel,
        far(streams) + v(halo, taps, gain) + far(out_grad),
        [kept(*row_shape), kept(*row_shape)],
        (
            pltpu.VMEM((rows, channels), bf16),
            pltpu.VMEM((rows, channels), bf16),
            (lane_blocks * pitch, LANES),
            (lane_blocks * pitch, LANES),
            pltpu.SemaphoreType.DMA((2,)),
        ),
        work=2 * 10**9,
    )
    local, rows_far = run(
        local_kernel,
        v(pair_far, first_rows, table),
        [kept(*row_shape), pltpu.HBM((2, SUB, lane_blocks, LANES), jnp.float32)],
        (pltpu.SemaphoreType.DMA(()),),
        work=2 * 10**9,
    )
    entering = gathered = state
    span = 1
    while 2 * span < count:
        final = 4 * span >= count
        got = swapped(message, 2 * span)
        if span == 1:
            got, query, scaled = lax.optimization_barrier((got, query, scaled))
        if final:
            got, local = lax.optimization_barrier((got, local))
        entering, message, *more = run(
            functools.partial(join_kernel, rows, span, final),
            [(place, pltpu.SMEM)] + v(table, state, entering, gathered, got),
            [
                kept(*state_shape),
                jax.ShapeDtypeStruct(state_shape, bf16),
            ]
            + ([] if final else [kept(*state_shape)]),
        )
        gathered = None if final else more[0]
        span *= 2
    received = swapped(message, 1)
    long_conv, sums = run(
        carry_kernel,
        v(entering, received, table, query, local, scaled),
        [kept(*row_shape), kept(2, rows)],
        ((rows * SUB, LANES), (rows * SUB, LANES)),
        aliases={4: 0},
    )
    sums = lax.psum(sums, "tp")
    mixed, long_grad, back, message, inv, head = run(
        functools.partial(mixed_kernel, float(channels * lax.axis_size("tp"))),
        v(sums, table, query, long_conv, scaled) + far(rows_far),
        [
            kept(*row_shape),
            kept(*row_shape),
            kept(*state_shape),
            jax.ShapeDtypeStruct(state_shape, bf16),
            kept(rows, LANES),
            kept(4, reach, lane_blocks, LANES),
        ],
        (
            (rows, LANES),
            (rows, LANES),
            (2, SUB, lane_blocks, LANES),
            pltpu.SemaphoreType.DMA(()),
        ),
        aliases={4: 0},
    )

    (local_back,) = run(
        back_kernel, v(table, long_grad), [kept(*row_shape)], work=2 * 10**9
    )
    output, finished, last, head = run(
        output_kernel,
        v(inv, taps_far, gain, query, long_conv, mixed, head),
        [
            jax.ShapeDtypeStruct((rows, channels), bf16),
            kept(rows, channels, dtype=bf16),
            kept(lane_blocks * SUB, LANES),
            jax.ShapeDtypeStruct(head.shape, bf16),
        ],
        ((lane_blocks * pitch, LANES), (lane_blocks * pitch, LANES)),
        work=2 * 10**9,
    )
    entering = beyond = added = gathered = back
    message_shape = (modes + reach, lane_blocks, LANES)
    span = 1
    while 2 * span < count:
        final = 4 * span >= count
        got = swapped(message, 2 * span)
        if span == 1:
            got, local_back = lax.optimization_barrier((got, local_back))
        if final:
            got, finished = lax.optimization_barrier((got, finished))
        entering, message, *more = run(
            functools.partial(join_back_kernel, rows, reach, span, final),
            [(place, pltpu.SMEM)] + v(table, back, entering, beyond, added, gathered, got),
            [
                kept(*state_shape),
                jax.ShapeDtypeStruct(message_shape, bf16),
            ]
            + (
                []
                if final
                else [kept(*state_shape), kept(reach, lane_blocks, LANES), kept(*message_shape)]
            ),
        )
        beyond, added, gathered = (None,) * 3 if final else more
        span *= 2
    head = shifted(head, -1)
    received = swapped(message, 1)
    (grads,) = run(
        final_kernel,
        v(entering, received, table, taps_far, pair_far, rows_far, local_back, finished, last, head),
        [pltpu.HBM((3, rows, channels), bf16)],
        (
            (2, rows, SUB, LANES),
            (SUB * pitch, LANES),
            (lane_blocks * SUB, LANES),
            pltpu.VMEM((2, rows, channels), bf16),
            pltpu.VMEM((2 * SUB, channels), bf16),
            pltpu.SemaphoreType.DMA((2 + lane_blocks // 4,)),
        ),
    )
    return output, grads


def solution(mesh):
    return jax.shard_map(
        on_device,
        mesh=mesh,
        in_specs=(
            P(None, "ctx", "tp"),
            P(None, "tp", None),
            P(None, "tp"),
            P(None, "tp"),
            P("tp"),
            P("ctx", "tp"),
        ),
        out_specs=(P("ctx", "tp"), P(None, "ctx", "tp")),
        check_vma=False,
    )
```

```python
import functools

import jax
import jax.numpy as jnp
from jax import lax
from jax.experimental import pallas as pl
from jax.experimental.pallas import tpu as pltpu
from jax.sharding import PartitionSpec as P

GROUP = 16
LANES = 128
SUB = 8
EPSILON = 1e-05
VMEM_LIMIT = 16 * 1024 * 1024


def halves(lane_blocks):
    return [pl.ds(SUB * h, SUB) for h in range(lane_blocks // SUB)]


def total(terms):
    terms = list(terms)
    while len(terms) > 1:
        paired = [terms[i] + terms[i + 1] for i in range(0, len(terms) - 1, 2)]
        terms = paired + ([terms[-1]] if len(terms) % 2 else [])
    return terms[0]


def spread_rows(source, target, first, pitch, lane_blocks):
    rows = source.shape[0]
    for lb in range(lane_blocks):
        tile = source[:, lb * LANES : (lb + 1) * LANES]
        target[pl.ds(first + lb * pitch, rows), :] = tile.astype(jnp.float32)


def to_send(table, half, states, lag, dtype):
    modes = table.shape[1]
    if dtype != jnp.bfloat16:
        return states
    down, off_down, up, off_up, chosen, off = [], [], [], [], [], []
    for m in range(modes):
        x = states[m]
        near = x.astype(jnp.bfloat16).astype(jnp.float32)
        other = (x + jnp.where(near < x, 0.00390625, -0.00390625) * jnp.abs(x)).astype(jnp.bfloat16).astype(jnp.float32)
        weight = table[1, m, half, :] * jnp.exp(table[2, m, half, :] * -float(lag))
        down.append(near)
        up.append(other)
        off_down.append(weight * (near - x))
        off_up.append(weight * (other - x))
    sum_off = jnp.zeros((SUB, LANES), jnp.float32)
    for turn in range(2):
        for m in range(modes):
            base = sum_off if turn == 0 else sum_off - off[m]
            first, second = base + off_down[m], base + off_up[m]
            take = jnp.abs(second) < jnp.abs(first)
            sum_off = jnp.where(take, second, first)
            if turn == 0:
                off.append(jnp.where(take, off_up[m], off_down[m]))
            else:
                chosen.append(jnp.where(take, up[m], down[m]).astype(jnp.bfloat16))
    return chosen


def row_at(ref, first, pitch, half, place):
    return ref[pl.ds(first + half * SUB * pitch + place, SUB, stride=pitch), :]


def tail_kernel(x, tail, edge, sem):
    rows = x.shape[1]
    move = pltpu.make_async_copy(x.at[:, pl.ds(rows - 2 * SUB, 2 * SUB), :], edge, sem)
    move.start()
    move.wait()
    tail[...] = edge[:, SUB:, :]


def prepare_kernel(
    x_far, filt_far, rate_far, res_far, pair_far, taps_far, first_rows, table, taps, ends,
    x, filt, rate, res, pair, xs, ps, sems,
):
    rows, channels = x.shape[1:]
    modes = rate.shape[0]
    lane_blocks = channels // LANES
    tap_count = taps.shape[1]
    pitch = rows + SUB
    fetches = [
        pltpu.make_async_copy(source, target, sems.at[i])
        for i, (source, target) in enumerate(
            [(filt_far, filt), (rate_far, rate), (res_far, res)]
            + [(x_far.at[1 + s], x.at[s]) for s in range(2)]
        )
    ]
    for fetch in fetches:
        fetch.start()
    spread = (
        lax.broadcasted_iota(jnp.int32, (channels // GROUP, channels), 1) // GROUP
        == lax.broadcasted_iota(jnp.int32, (channels // GROUP, channels), 0)
    ).astype(jnp.bfloat16)
    fetches[0].wait()
    for s in range(3):
        weights = jnp.dot(filt[s], spread, preferred_element_type=jnp.float32)
        for lb in range(lane_blocks):
            ps[pl.ds(lb * SUB, tap_count), :] = weights[:, lb * LANES : (lb + 1) * LANES]
        for h, half in enumerate(halves(lane_blocks)):
            for i in range(tap_count):
                taps[s, i, half, :] = row_at(ps, 0, SUB, h, i)
    stores = [pltpu.make_async_copy(taps, taps_far, sems.at[5])]
    stores[0].start()
    fetches[1].wait()
    fetches[2].wait()
    spread_rows(rate, ps, 0, modes, lane_blocks)
    spread_rows(res, ps, lane_blocks * modes, modes, lane_blocks)
    for h, half in enumerate(halves(lane_blocks)):
        for m in range(modes):
            r = row_at(ps, 0, modes, h, m)
            c = row_at(ps, lane_blocks * modes, modes, h, m)
            table[0, m, half, :] = jnp.exp(-r)
            table[1, m, half, :] = c * jnp.sqrt(2.0 * r)
            table[2, m, half, :] = r
    zero = jnp.zeros((SUB, LANES), jnp.float32)
    for s in range(2):
        fetches[3 + s].wait()
        spread_rows(x.at[s], xs, s * lane_blocks * pitch, pitch, lane_blocks)
    for h, half in enumerate(halves(lane_blocks)):
        for s in range(2):
            w = [taps[1 + s, i, half, :] for i in range(tap_count)]

            def body(block, window):
                window = list(window)
                for k in range(SUB):
                    t = block * SUB + k
                    window.append(row_at(xs, s * lane_blocks * pitch, pitch, h, t))
                    pair[s, t, half, :] = total(w[i] * window[-1 - i] for i in range(tap_count))
                return tuple(window[-(tap_count - 1) :])

            lax.fori_loop(0, rows // SUB, body, (zero,) * (tap_count - 1))
            stores.append(
                pltpu.make_async_copy(
                    pair.at[s, :, half, :], pair_far.at[s, :, half, :], sems.at[6 + 2 * h + s]
                )
            )
            stores[-1].start()
            first_rows[s, :, half, :] = pair[s, :SUB, half, :]
        decay = [table[0, m, half, :] for m in range(modes)]

        def step(t, state):
            u = pair[0, t, half, :] * pair[1, t, half, :]
            return tuple(decay[m] * state[m] + u for m in range(modes))

        state = (zero,) * modes
        for t in range(tap_count - 1, SUB):
            state = step(t, state)

        def block_step(block, state):
            for k in range(SUB):
                state = step(block * SUB + k, state)
            return state

        state = lax.fori_loop(1, rows // SUB, block_step, state)
        for m in range(modes):
            ends[m, half, :] = state[m]
    for store in stores:
        store.wait()


def head_kernel(rows, first_in, halo, table, taps, ends, first_rows, state_out, message, hs):
    modes, lane_blocks = ends.shape[:2]
    reach = taps.shape[1] - 1
    for s in range(2):
        spread_rows(halo.at[1 + s], hs, s * lane_blocks * SUB, SUB, lane_blocks)
    for h, half in enumerate(halves(lane_blocks)):
        heads = []
        for s in range(2):
            w = [taps[1 + s, i, half, :] for i in range(reach + 1)]
            before = [row_at(hs, s * lane_blocks * SUB, SUB, h, j) for j in range(SUB)]
            head = []
            for t in range(SUB):
                row = first_in[s, t, half, :]
                if t < reach:
                    row = row + total(w[i] * before[SUB + t - i] for i in range(t + 1, reach + 1))
                    head.append(row)
                first_rows[s, t, half, :] = row
            heads.append(head)
        product = [heads[0][t] * heads[1][t] for t in range(reach)]
        states = []
        for m in range(modes):
            decay = table[0, m, half, :]
            state = product[0]
            for t in range(1, reach):
                state = decay * state + product[t]
            fade = jnp.exp(table[2, m, half, :] * -float(rows - reach))
            states.append(ends[m, half, :] + fade * state)
            state_out[m, half, :] = states[m]
        for m, value in enumerate(to_send(table, half, states, rows // 2, message.dtype)):
            message[m, half, :] = value


def query_kernel(x_far, halo, taps, gain, grad_far, query, scaled, x, grad, xs, gs, sems):
    rows, channels = x.shape
    lane_blocks = channels // LANES
    tap_count = taps.shape[1]
    pitch = rows + SUB
    fetches = [
        pltpu.make_async_copy(x_far.at[0], x, sems.at[0]),
        pltpu.make_async_copy(grad_far, grad, sems.at[1]),
    ]
    for fetch in fetches:
        fetch.start()
    spread_rows(halo.at[0], xs, 0, pitch, lane_blocks)
    fetches[0].wait()
    spread_rows(x, xs, SUB, pitch, lane_blocks)
    fetches[1].wait()
    spread_rows(grad, gs, 0, pitch, lane_blocks)
    for h, half in enumerate(halves(lane_blocks)):
        w = [taps[0, i, half, :] for i in range(tap_count)]
        g = gain[half, :]

        def body(block, window):
            window = list(window)
            for k in range(SUB):
                t = block * SUB + k
                window.append(row_at(xs, SUB, pitch, h, t))
                query[t, half, :] = total(w[i] * window[-1 - i] for i in range(tap_count))
                scaled[t, half, :] = g * row_at(gs, 0, pitch, h, t)
            return tuple(window[-(tap_count - 1) :])

        lax.fori_loop(
            0, rows // SUB, body, tuple(row_at(xs, 0, pitch, h, SUB + 1 - tap_count + j) for j in range(tap_count - 1))
        )


def local_kernel(pair, first_rows, table, local, rows_far, sem):
    rows = local.shape[0]
    modes, lane_blocks = table.shape[1:3]
    zero = jnp.zeros((SUB, LANES), jnp.float32)
    store = pltpu.make_async_copy(first_rows, rows_far, sem)
    store.start()
    for half in halves(lane_blocks):
        decay = [table[0, m, half, :] for m in range(modes)]
        scale = [table[1, m, half, :] for m in range(modes)]

        def block_step(source, block, state):
            for k in range(SUB):
                t = block * SUB + k
                u = source[0, t, half, :] * source[1, t, half, :]
                state = tuple(decay[m] * state[m] + u for m in range(modes))
                local[t, half, :] = total(scale[m] * state[m] for m in range(modes))
            return state

        state = block_step(first_rows, 0, (zero,) * modes)
        lax.fori_loop(1, rows // SUB, functools.partial(block_step, pair), state)
    store.wait()


def carry_kernel(span, place, entering, got, table, query, local, scaled, long_conv, sums, sq, cr):
    rows = local.shape[0]
    modes, lane_blocks = table.shape[1:3]
    for h, half in enumerate(halves(lane_blocks)):
        decay = [table[0, m, half, :] for m in range(modes)]
        start = []
        for m in range(modes):
            other = got[m, half, :].astype(jnp.float32)
            incoming = entering[m, half, :] + joined_term(rows, span, place, table[2, m, half, :], other)
            start.append(table[1, m, half, :] * decay[m] * incoming)

        def block_step(block, state):
            for k in range(SUB):
                t = block * SUB + k
                row = local[t, half, :] + total(state)
                state = tuple(decay[m] * state[m] for m in range(modes))
                long_conv[t, half, :] = row
                modulated = query[t, half, :] * row
                place = pl.ds(pl.multiple_of(t * SUB, SUB), SUB)
                square = modulated * modulated
                cross = scaled[t, half, :] * modulated
                sq[place, :] = square if h == 0 else sq[place, :] + square
                cr[place, :] = cross if h == 0 else cr[place, :] + cross
            return state

        lax.fori_loop(0, rows // SUB, block_step, tuple(start))
    for which, ref in enumerate((sq, cr)):
        blocks = []
        for b in range(rows // SUB):
            blocks.append(
                total(
                    ref[pl.ds(b * SUB * SUB + s, SUB, stride=SUB), :] for s in range(SUB)
                )
            )
        by_row = jnp.concatenate(blocks, axis=0)
        sums[which : which + 1, :] = jnp.sum(jnp.transpose(by_row), axis=0, keepdims=True)


def mixed_kernel(
    width, sums, table, query, long_conv, scaled, rows_far, mixed, long_grad, state_out, message, inv, head, inv_s, off_s,
    first_rows, sem,
):
    fetch = pltpu.make_async_copy(rows_far, first_rows, sem)
    fetch.start()
    rows = long_conv.shape[0]
    modes, lane_blocks = table.shape[1:3]
    zero = jnp.zeros((SUB, LANES), jnp.float32)
    inverse = lax.rsqrt(sums[0:1, :] / width + EPSILON)
    offset = inverse * inverse * inverse * sums[1:2, :] / width
    inv_s[...] = jnp.transpose(jnp.broadcast_to(inverse, (LANES, rows)))
    off_s[...] = jnp.transpose(jnp.broadcast_to(offset, (LANES, rows)))
    inv[...] = inv_s[...]
    blocks = rows // SUB
    for half in halves(lane_blocks):
        decay = [table[0, m, half, :] for m in range(modes)]

        def row(t, state):
            q = query[t, half, :]
            modulated = q * long_conv[t, half, :]
            mix = inv_s[pl.ds(t, 1), :] * scaled[t, half, :] - off_s[pl.ds(t, 1), :] * modulated
            mixed[t, half, :] = mix
            lg = mix * q
            long_grad[t, half, :] = lg
            return tuple(decay[m] * state[m] + lg for m in range(modes))

        def block_step(block, state):
            for k in range(SUB):
                state = row((blocks - 1 - block) * SUB + SUB - 1 - k, state)
            return state

        state = lax.fori_loop(0, blocks - 1, block_step, (zero,) * modes)
        if half.start == 0:
            fetch.wait()
        for t in reversed(range(SUB)):
            state = row(t, state)
            if t < head.shape[1]:
                gated = total(table[1, m, half, :] * state[m] for m in range(modes))
                found = (
                    mixed[t, half, :] * long_conv[t, half, :],
                    gated,
                    first_rows[1, t, half, :],
                    first_rows[0, t, half, :],
                )
                for i, value in enumerate(found):
                    head[i, t, half, :] = value
        for m, value in enumerate(to_send(table, half, state, rows // 2, message.dtype)):
            state_out[m, half, :] = state[m]
            message[m, half, :] = value


def back_kernel(table, long_grad, head_in, local, head):
    head[...] = head_in[...].astype(head.dtype)
    rows = long_grad.shape[0]
    modes, lane_blocks = table.shape[1:3]
    blocks = rows // SUB
    zero = jnp.zeros((SUB, LANES), jnp.float32)
    for half in halves(lane_blocks):
        decay = [table[0, m, half, :] for m in range(modes)]
        scale = [table[1, m, half, :] for m in range(modes)]

        def block_step(block, state):
            for k in range(SUB):
                t = (blocks - 1 - block) * SUB + SUB - 1 - k
                lg = long_grad[t, half, :]
                state = tuple(decay[m] * state[m] + lg for m in range(modes))
                local[t, half, :] = total(scale[m] * state[m] for m in range(modes))
            return state

        lax.fori_loop(0, blocks, block_step, (zero,) * modes)

def output_kernel(inv, taps, gain, query, long_conv, mixed, output, finished, last, os, qs):
    rows = long_conv.shape[0]
    lane_blocks = taps.shape[2]
    tap_count = taps.shape[1]
    pitch = rows + SUB
    blocks = rows // SUB
    zero = jnp.zeros((SUB, LANES), jnp.float32)
    for h, half in enumerate(halves(lane_blocks)):
        g = gain[half, :]
        w = [taps[0, i, half, :] for i in range(tap_count)]

        def out_step(block, window):
            window = list(window)
            for k in range(SUB):
                t = (blocks - 1 - block) * SUB + SUB - 1 - k
                long_row = long_conv[t, half, :]
                window.insert(0, mixed[t, half, :] * long_row)
                row = g * (query[t, half, :] * long_row) * inv[pl.ds(t, 1), :]
                os[pl.ds(h * SUB * pitch + t, SUB, stride=pitch), :] = row
                qs[pl.ds(h * SUB * pitch + t, SUB, stride=pitch), :] = total(
                    w[i] * window[i] for i in range(tap_count)
                )
            return tuple(window[: tap_count - 1])

        lax.fori_loop(0, blocks, out_step, (zero,) * (tap_count - 1))
    for lb in range(lane_blocks):
        columns = slice(lb * LANES, (lb + 1) * LANES)
        output[:, columns] = os[pl.ds(lb * pitch, rows), :].astype(output.dtype)
        finished[:, columns] = qs[pl.ds(lb * pitch, rows), :].astype(finished.dtype)
        last[pl.ds(lb * SUB, SUB), :] = qs[pl.ds(lb * pitch + rows - SUB, SUB), :]


def far_rows(table, half, state, rows, reach):
    modes = table.shape[1]
    at = [
        table[1, m, half, :]
        * state[m]
        * jnp.exp(table[2, m, half, :] * -float(rows - reach + 1))
        for m in range(modes)
    ]
    found = [None] * reach
    for i in reversed(range(reach)):
        found[i] = total(at)
        if i:
            at = [at[m] * table[0, m, half, :] for m in range(modes)]
    return found


def gather_kernel(rows, place, table, state, first, second, third, entering, message, *whole):
    modes, lane_blocks = state.shape[:2]
    inside = lax.rem(place[0], 4)
    for half in halves(lane_blocks):
        sent = []
        for m in range(modes):
            rate = table[2, m, half, :]
            found = None
            at_end = jnp.exp(rate * -steps(3 - inside, rows)) * state[m, half, :]
            for k, got in enumerate((first, second, third)):
                other = got[m, half, :].astype(jnp.float32)
                other_inside = inside ^ (k + 1)
                at_end = at_end + jnp.exp(rate * -steps(3 - other_inside, rows)) * other
                ahead = inside - other_inside
                term = jnp.where(above(ahead, 0), jnp.exp(rate * -steps(ahead - 1, rows)) * other, 0.0)
                found = term if found is None else found + term
            entering[m, half, :] = found
            sent.append(at_end)
            if whole:
                whole[0][m, half, :] = at_end
        for m, value in enumerate(to_send(table, half, sent, rows // 2, message.dtype)):
            message[m, half, :] = value


def join_kernel(rows, span, place, table, entering, whole, got, entering_out, message, whole_out):
    modes, lane_blocks = entering.shape[:2]
    upper = above(lax.rem(lax.div(place[0], span), 2), 0)
    for half in halves(lane_blocks):
        sent = []
        for m in range(modes):
            rate = table[2, m, half, :]
            other, mine = got[m, half, :].astype(jnp.float32), whole[m, half, :]
            entering_out[m, half, :] = entering[m, half, :] + joined_term(rows, span, place, rate, other)
            fade = jnp.exp(rate * -float(rows * span))
            sent.append(jnp.where(upper, mine, other) + fade * jnp.where(upper, other, mine))
            whole_out[m, half, :] = sent[m]
        for m, value in enumerate(to_send(table, half, sent, rows // 2, message.dtype)):
            message[m, half, :] = value


def steps(shards, rows):
    return jnp.maximum(shards, 0).astype(jnp.float32) * float(rows)


def above(value, bound):
    return jnp.full((SUB, LANES), value) > bound


def joined_term(rows, span, place, rate, other):
    upper = above(lax.rem(lax.div(place[0], span), 2), 0)
    return jnp.where(upper, jnp.exp(rate * -steps(lax.rem(place[0], span), rows)) * other, 0.0)


def joined_back_terms(rows, span, place, rate, other):
    lower = ~above(lax.rem(lax.div(place[0], span), 2), 0)
    to_end = span - 1 - lax.rem(place[0], span)
    here = jnp.where(lower, jnp.exp(rate * -steps(to_end, rows)) * other, 0.0)
    onward = jnp.where(lower & above(to_end, 0), jnp.exp(rate * -steps(to_end - 1, rows)) * other, 0.0)
    return here, onward


def joined_rows(span, place, other):
    lower = ~above(lax.rem(lax.div(place[0], span), 2), 0)
    at_end = ~above(span - 1 - lax.rem(place[0], span), 0)
    return jnp.where(lower & at_end, other, 0.0)


def gather_back_kernel(rows, reach, place, table, state, first, second, third, entering, beyond, added, message, *whole):
    modes, lane_blocks = state.shape[:2]
    inside = lax.rem(place[0], 4)
    for half in halves(lane_blocks):
        sent, rest = [], []
        for m in range(modes):
            rate = table[2, m, half, :]
            mine = state[m, half, :]
            at_start = jnp.exp(rate * -steps(inside, rows)) * mine
            after_first = jnp.where(above(inside, 0), jnp.exp(rate * -steps(inside - 1, rows)) * mine, 0.0)
            here = onward = jnp.zeros((SUB, LANES), jnp.float32)
            for k, got in enumerate((first, second, third)):
                other = got[m, half, :].astype(jnp.float32)
                other_inside = inside ^ (k + 1)
                at_start = at_start + jnp.exp(rate * -steps(other_inside, rows)) * other
                after_first = after_first + jnp.where(
                    above(other_inside, 0), jnp.exp(rate * -steps(other_inside - 1, rows)) * other, 0.0
                )
                ahead = other_inside - inside
                here = here + jnp.where(above(ahead, 0), jnp.exp(rate * -steps(ahead - 1, rows)) * other, 0.0)
                onward = onward + jnp.where(above(ahead, 1), jnp.exp(rate * -steps(ahead - 2, rows)) * other, 0.0)
            entering[m, half, :] = here
            beyond[m, half, :] = onward
            sent.append(at_start)
            rest.append(after_first)
            if whole:
                whole[0][m, half, :] = at_start
        for m, value in enumerate(to_send(table, half, sent, rows // 2, message.dtype)):
            message[m, half, :] = value
        found = far_rows(table, half, rest, rows, reach)
        for i in range(reach):
            added[i, half, :] = jnp.zeros((SUB, LANES), jnp.float32)
            message[modes + i, half, :] = found[i].astype(message.dtype)
            if whole:
                whole[0][modes + i, half, :] = found[i]


def join_back_kernel(
    rows, reach, span, place, table, entering, beyond, added, whole, got,
    entering_out, beyond_out, added_out, message, whole_out,
):
    modes, lane_blocks = entering.shape[:2]
    upper = above(lax.rem(lax.div(place[0], span), 2), 0)
    for half in halves(lane_blocks):
        sent, rest = [], []
        for m in range(modes):
            rate = table[2, m, half, :]
            other, mine = got[m, half, :].astype(jnp.float32), whole[m, half, :]
            here, onward = joined_back_terms(rows, span, place, rate, other)
            entering_out[m, half, :] = entering[m, half, :] + here
            beyond_out[m, half, :] = beyond[m, half, :] + onward
            low, high = jnp.where(upper, other, mine), jnp.where(upper, mine, other)
            sent.append(low + jnp.exp(rate * -float(rows * span)) * high)
            rest.append(jnp.exp(rate * -float(rows * (span - 1))) * high)
            whole_out[m, half, :] = sent[m]
        for m, value in enumerate(to_send(table, half, sent, rows // 2, message.dtype)):
            message[m, half, :] = value
        found = far_rows(table, half, rest, rows, reach)
        for i in range(reach):
            other, mine = got[modes + i, half, :].astype(jnp.float32), whole[modes + i, half, :]
            added_out[i, half, :] = added[i, half, :] + joined_rows(span, place, other)
            value = jnp.where(upper, other, mine) + found[i]
            message[modes + i, half, :] = value.astype(message.dtype)
            whole_out[modes + i, half, :] = value


def final_kernel(
    span, place, entering, beyond_in, added, got, table, taps, pair, first_rows, local, query, last, head, grads, cg, os, ls, made, edge, sems
):
    rows = local.shape[0]
    modes, lane_blocks = table.shape[1:3]
    tap_count = taps.shape[1]
    reach = tap_count - 1
    pitch = rows + SUB
    blocks = rows // SUB
    kept = rows - 2 * SUB
    moves = [
        pltpu.make_async_copy(
            query.at[pl.ds(0, kept), :], grads.at[0, pl.ds(0, kept), :], sems.at[0]
        )
    ]
    moves[0].start()
    ls[...] = last[...]
    for h, half in enumerate(halves(lane_blocks)):
        decay = [table[0, m, half, :] for m in range(modes)]
        start, onward = [], []
        for m in range(modes):
            other = got[m, half, :].astype(jnp.float32)
            here, later = joined_back_terms(rows, span, place, table[2, m, half, :], other)
            start.append(table[1, m, half, :] * decay[m] * (entering[m, half, :] + here))
            onward.append(beyond_in[m, half, :] + later)

        def block_step(source, block, state):
            for k in range(SUB):
                t = (blocks - 1 - block) * SUB + SUB - 1 - k
                gated = local[t, half, :] + total(state)
                state = tuple(decay[m] * state[m] for m in range(modes))
                cg[0, t, :, :] = gated * source[1, t, half, :]
                cg[1, t, :, :] = gated * source[0, t, half, :]
            return state

        state = lax.fori_loop(0, blocks - 1, functools.partial(block_step, pair), tuple(start))
        block_step(first_rows, blocks - 1, state)
        own = far_rows(table, half, onward, rows, reach)
        beyond = [[], [], []]
        for i in range(reach):
            rows_there = joined_rows(span, place, got[modes + i, half, :].astype(jnp.float32))
            gated = head[1, i, half, :].astype(jnp.float32) + own[i] + added[i, half, :] + rows_there
            beyond[0].append(head[0, i, half, :].astype(jnp.float32))
            beyond[1].append(gated * head[2, i, half, :].astype(jnp.float32))
            beyond[2].append(gated * head[3, i, half, :].astype(jnp.float32))
        for t in range(SUB - reach, SUB):
            edge_rows = pl.ds(h * SUB * SUB + t, SUB, stride=SUB)
            ls[edge_rows, :] += total(
                taps[0, i, half, :] * beyond[0][t + i - SUB] for i in range(SUB - t, tap_count)
            )
        for s in range(1, 3):
            w = [taps[s, i, half, :] for i in range(tap_count)]

            def conv_step(block, window):
                window = list(window)
                for k in range(SUB):
                    t = (blocks - 1 - block) * SUB + SUB - 1 - k
                    window.insert(0, cg[s - 1, t, :, :])
                    os[pl.ds(t, SUB, stride=pitch), :] = total(
                        w[i] * window[i] for i in range(tap_count)
                    )
                return tuple(window[:reach])

            lax.fori_loop(0, blocks, conv_step, tuple(beyond[s]))
            for lb in range(SUB):
                first = (h * SUB + lb) * LANES
                made[s - 1, :, first : first + LANES] = os[pl.ds(lb * pitch, rows), :].astype(made.dtype)
            columns = pl.ds(h * SUB * LANES, SUB * LANES)
            moves.append(
                pltpu.make_async_copy(
                    made.at[s - 1, :, columns], grads.at[s, :, columns], sems.at[len(moves)]
                )
            )
            moves[-1].start()
    for lb in range(lane_blocks):
        columns = slice(lb * LANES, (lb + 1) * LANES)
        ending = jnp.concatenate(
            [query[kept : kept + SUB, columns].astype(jnp.float32), ls[pl.ds(lb * SUB, SUB), :]], axis=0
        )
        edge[:, columns] = ending.astype(edge.dtype)
    moves.append(
        pltpu.make_async_copy(edge, grads.at[0, pl.ds(kept, 2 * SUB), :], sems.at[len(moves)])
    )
    moves[-1].start()
    for move in moves:
        move.wait()


def kept(*shape, dtype=jnp.float32):
    return pltpu.VMEM(shape, dtype)


def run(kernel, ins, outs, scratch=(), work=0, aliases=None):
    ins = [pltpu.with_memory_space_constraint(a, space) for a, space in ins]
    spaces = [getattr(o, "memory_space", pltpu.VMEM) for o in outs]
    return pl.pallas_call(
        kernel,
        out_shape=outs,
        in_specs=[pl.BlockSpec(memory_space=jax.typeof(a).memory_space) for a in ins],
        out_specs=[pl.BlockSpec(memory_space=space) for space in spaces],
        scratch_shapes=[pltpu.VMEM(s, jnp.float32) if isinstance(s, tuple) else s for s in scratch],
        input_output_aliases=aliases or {},
        compiler_params=pltpu.CompilerParams(vmem_limit_bytes=VMEM_LIMIT),
        cost_estimate=pl.CostEstimate(flops=work, bytes_accessed=4 * 1024 * 1024, transcendentals=0),
    )(*ins)


def shifted(block, distance):
    devices = range(lax.axis_size("ctx"))
    route = [(i, i + distance) for i in devices if i + distance in devices]
    return lax.ppermute(block, "ctx", route)


def swapped(block, distance):
    return lax.ppermute(block, "ctx", [(i, i ^ distance) for i in range(lax.axis_size("ctx"))])


def on_device(streams, short_filter, decay_rate, residue, norm_gain, out_grad):
    rows, channels = streams.shape[1:]
    modes = decay_rate.shape[0]
    lane_blocks = channels // LANES
    tap_count = short_filter.shape[2]
    reach = tap_count - 1
    pitch = rows + SUB
    count = lax.axis_size("ctx")
    row_shape = (rows, lane_blocks, LANES)
    state_shape = (modes, lane_blocks, LANES)
    bf16 = jnp.bfloat16
    single = count <= 8
    wire = bf16 if single else jnp.float32

    def v(*arrays):
        return [(a, pltpu.VMEM) for a in arrays]

    def far(*arrays):
        return [(a, pltpu.HBM) for a in arrays]

    (tail,) = run(
        tail_kernel,
        far(streams),
        [jax.ShapeDtypeStruct((3, SUB, channels), bf16)],
        (pltpu.VMEM((3, 2 * SUB, channels), bf16), pltpu.SemaphoreType.DMA(())),
    )
    halo = shifted(tail, 1)
    gain = norm_gain.reshape(lane_blocks, LANES)
    pair_far, taps_far, first_rows, table, taps, ends = run(
        prepare_kernel,
        far(streams, jnp.swapaxes(short_filter, 1, 2), decay_rate, residue),
        [
            pltpu.HBM((2, *row_shape), jnp.float32),
            pltpu.HBM((3, tap_count, lane_blocks, LANES), jnp.float32),
            kept(2, SUB, lane_blocks, LANES),
            kept(3, *state_shape),
            kept(3, tap_count, lane_blocks, LANES),
            kept(*state_shape),
        ],
        (
            pltpu.VMEM((2, rows, channels), bf16),
            pltpu.VMEM((3, tap_count, channels // GROUP), bf16),
            (modes, channels),
            (modes, channels),
            (2, *row_shape),
            (2 * lane_blocks * pitch, LANES),
            (2 * lane_blocks * modes, LANES),
            pltpu.SemaphoreType.DMA((6 + lane_blocks // 4,)),
        ),
        work=10**9,
    )
    first_rows, state, message = run(
        functools.partial(head_kernel, rows),
        v(first_rows, halo, table, taps, ends),
        [kept(2, SUB, lane_blocks, LANES), kept(*state_shape), jax.ShapeDtypeStruct(state_shape, wire)],
        ((2 * lane_blocks * SUB, LANES),),
    )
    place = lax.axis_index("ctx").astype(jnp.int32)[None]

    query, scaled = run(
        query_kernel,
        far(streams) + v(halo, taps, gain) + far(out_grad),
        [kept(*row_shape), kept(*row_shape)],
        (
            pltpu.VMEM((rows, channels), bf16),
            pltpu.VMEM((rows, channels), bf16),
            (lane_blocks * pitch, LANES),
            (lane_blocks * pitch, LANES),
            pltpu.SemaphoreType.DMA((2,)),
        ),
        work=2 * 10**9,
    )
    local, rows_far = run(
        local_kernel,
        v(pair_far, first_rows, table),
        [kept(*row_shape), pltpu.HBM((2, SUB, lane_blocks, LANES), jnp.float32)],
        (pltpu.SemaphoreType.DMA(()),),
        work=2 * 10**9,
    )
    got = [swapped(message, k) for k in (1, 2, 3)]
    *got, query, scaled = lax.optimization_barrier((*got, query, scaled))
    entering, message, *whole = run(
        functools.partial(gather_kernel, rows),
        [(place, pltpu.SMEM)] + v(table, state, *got),
        [kept(*state_shape), jax.ShapeDtypeStruct(state_shape, wire)]
        + ([] if single else [kept(*state_shape)]),
    )
    span = 4
    got = swapped(message, span)
    while 2 * span < count:
        entering, message, *whole = run(
            functools.partial(join_kernel, rows, span),
            [(place, pltpu.SMEM)] + v(table, entering, *whole, got),
            [kept(*state_shape), jax.ShapeDtypeStruct(state_shape, wire), kept(*state_shape)],
        )
        span *= 2
        got = swapped(message, span)
    got, local = lax.optimization_barrier((got, local))
    long_conv, sums = run(
        functools.partial(carry_kernel, span),
        [(place, pltpu.SMEM)] + v(entering, got, table, query, local, scaled),
        [kept(*row_shape), kept(2, rows)],
        ((rows * SUB, LANES), (rows * SUB, LANES)),
        aliases={5: 0},
    )
    sums = lax.psum(sums, "tp")
    mixed, long_grad, back, message, inv, head = run(
        functools.partial(mixed_kernel, float(channels * lax.axis_size("tp"))),
        v(sums, table, query, long_conv, scaled) + far(rows_far),
        [
            kept(*row_shape),
            kept(*row_shape),
            kept(*state_shape),
            jax.ShapeDtypeStruct(state_shape, wire),
            kept(rows, LANES),
            kept(4, reach, lane_blocks, LANES),
        ],
        (
            (rows, LANES),
            (rows, LANES),
            (2, SUB, lane_blocks, LANES),
            pltpu.SemaphoreType.DMA(()),
        ),
        aliases={4: 0},
    )

    local_back, head = run(
        back_kernel,
        v(table, long_grad, head),
        [kept(*row_shape), jax.ShapeDtypeStruct(head.shape, bf16)],
        work=2 * 10**9,
    )
    message_shape = (modes + reach, lane_blocks, LANES)
    adjoint = [kept(*state_shape), kept(*state_shape), kept(reach, lane_blocks, LANES)]
    adjoint.append(jax.ShapeDtypeStruct(message_shape, wire))
    got = [swapped(message, k) for k in (1, 2, 3)]
    *got, local_back, mixed = lax.optimization_barrier((*got, local_back, mixed))
    output, finished, last = run(
        output_kernel,
        v(inv, taps_far, gain, query, long_conv, mixed),
        [
            jax.ShapeDtypeStruct((rows, channels), bf16),
            kept(rows, channels, dtype=bf16),
            kept(lane_blocks * SUB, LANES),
        ],
        ((lane_blocks * pitch, LANES), (lane_blocks * pitch, LANES)),
        work=2 * 10**9,
    )
    entering, beyond, added, message, *whole = run(
        functools.partial(gather_back_kernel, rows, reach),
        [(place, pltpu.SMEM)] + v(table, back, *got),
        adjoint + ([] if single else [kept(*message_shape)]),
    )
    span = 4
    got = swapped(message, span)
    while 2 * span < count:
        entering, beyond, added, message, *whole = run(
            functools.partial(join_back_kernel, rows, reach, span),
            [(place, pltpu.SMEM)] + v(table, entering, beyond, added, *whole, got),
            adjoint + [kept(*message_shape)],
        )
        span *= 2
        got = swapped(message, span)
    head = shifted(head, -1)
    got, finished = lax.optimization_barrier((got, finished))
    (grads,) = run(
        functools.partial(final_kernel, span),
        [(place, pltpu.SMEM)] + v(entering, beyond, added, got, table, taps_far, pair_far, rows_far, local_back, finished, last, head),
        [pltpu.HBM((3, rows, channels), bf16)],
        (
            (2, rows, SUB, LANES),
            (SUB * pitch, LANES),
            (lane_blocks * SUB, LANES),
            pltpu.VMEM((2, rows, channels), bf16),
            pltpu.VMEM((2 * SUB, channels), bf16),
            pltpu.SemaphoreType.DMA((2 + lane_blocks // 4,)),
        ),
    )
    return output, grads


def solution(mesh):
    return jax.shard_map(
        on_device,
        mesh=mesh,
        in_specs=(
            P(None, "ctx", "tp"),
            P(None, "tp", None),
            P(None, "tp"),
            P(None, "tp"),
            P("tp"),
            P("ctx", "tp"),
        ),
        out_specs=(P("ctx", "tp"), P(None, "ctx", "tp")),
        check_vma=False,
    )
```

```python
import functools

import jax
import jax.numpy as jnp
from jax import lax
from jax.experimental import pallas as pl
from jax.experimental.pallas import tpu as pltpu
from jax.sharding import PartitionSpec as P

GROUP = 16
LANES = 128
SUB = 8
EPSILON = 1e-05
VMEM_LIMIT = 16 * 1024 * 1024


def halves(lane_blocks):
    return [pl.ds(SUB * h, SUB) for h in range(lane_blocks // SUB)]


def total(terms):
    terms = list(terms)
    while len(terms) > 1:
        paired = [terms[i] + terms[i + 1] for i in range(0, len(terms) - 1, 2)]
        terms = paired + ([terms[-1]] if len(terms) % 2 else [])
    return terms[0]


def spread_rows(source, target, first, pitch, lane_blocks):
    rows = source.shape[0]
    for lb in range(lane_blocks):
        tile = source[:, lb * LANES : (lb + 1) * LANES]
        target[pl.ds(first + lb * pitch, rows), :] = tile.astype(jnp.float32)


def to_send(table, half, states, lag, dtype):
    modes = table.shape[1]
    if dtype != jnp.bfloat16:
        return states
    down, off_down, up, off_up, chosen, off = [], [], [], [], [], []
    for m in range(modes):
        x = states[m]
        near = x.astype(jnp.bfloat16).astype(jnp.float32)
        other = (x + jnp.where(near < x, 0.00390625, -0.00390625) * jnp.abs(x)).astype(jnp.bfloat16).astype(jnp.float32)
        weight = table[1, m, half, :] * jnp.exp(table[2, m, half, :] * -float(lag))
        down.append(near)
        up.append(other)
        off_down.append(weight * (near - x))
        off_up.append(weight * (other - x))
    sum_off = jnp.zeros((SUB, LANES), jnp.float32)
    for turn in range(2):
        for m in range(modes):
            base = sum_off if turn == 0 else sum_off - off[m]
            first, second = base + off_down[m], base + off_up[m]
            take = jnp.abs(second) < jnp.abs(first)
            sum_off = jnp.where(take, second, first)
            if turn == 0:
                off.append(jnp.where(take, off_up[m], off_down[m]))
            else:
                chosen.append(jnp.where(take, up[m], down[m]).astype(jnp.bfloat16))
    return chosen


def row_at(ref, first, pitch, half, place):
    return ref[pl.ds(first + half * SUB * pitch + place, SUB, stride=pitch), :]


def tail_kernel(x, tail, edge, sem):
    rows = x.shape[1]
    move = pltpu.make_async_copy(x.at[:, pl.ds(rows - 2 * SUB, 2 * SUB), :], edge, sem)
    move.start()
    move.wait()
    tail[...] = edge[:, SUB:, :]


def prepare_kernel(
    x_far, filt_far, rate_far, res_far, pair_far, taps_far, first_rows, table, taps, ends,
    x, filt, rate, res, pair, xs, ps, sems,
):
    rows, channels = x.shape[1:]
    modes = rate.shape[0]
    lane_blocks = channels // LANES
    tap_count = taps.shape[1]
    pitch = rows + SUB
    count = lane_blocks // SUB
    width = SUB * LANES
    fetches = [
        pltpu.make_async_copy(source, target, sems.at[i])
        for i, (source, target) in enumerate(
            [(filt_far, filt), (rate_far, rate), (res_far, res)]
            + [
                (x_far.at[1 + s, :, pl.ds(h * width, width)], x.at[s, :, pl.ds(h * width, width)])
                for h in range(count)
                for s in range(2)
            ]
        )
    ]
    for fetch in fetches:
        fetch.start()
    spread = (
        lax.broadcasted_iota(jnp.int32, (channels // GROUP, channels), 1) // GROUP
        == lax.broadcasted_iota(jnp.int32, (channels // GROUP, channels), 0)
    ).astype(jnp.bfloat16)
    fetches[0].wait()
    for s in range(3):
        weights = jnp.dot(filt[s], spread, preferred_element_type=jnp.float32)
        for lb in range(lane_blocks):
            ps[pl.ds(lb * SUB, tap_count), :] = weights[:, lb * LANES : (lb + 1) * LANES]
        for h, half in enumerate(halves(lane_blocks)):
            for i in range(tap_count):
                taps[s, i, half, :] = row_at(ps, 0, SUB, h, i)
    stores = [pltpu.make_async_copy(taps, taps_far, sems.at[3 + 2 * count])]
    stores[0].start()
    fetches[1].wait()
    fetches[2].wait()
    spread_rows(rate, ps, 0, modes, lane_blocks)
    spread_rows(res, ps, lane_blocks * modes, modes, lane_blocks)
    for h, half in enumerate(halves(lane_blocks)):
        for m in range(modes):
            r = row_at(ps, 0, modes, h, m)
            c = row_at(ps, lane_blocks * modes, modes, h, m)
            table[0, m, half, :] = jnp.exp(-r)
            table[1, m, half, :] = c * jnp.sqrt(2.0 * r)
            table[2, m, half, :] = r
    zero = jnp.zeros((SUB, LANES), jnp.float32)
    for h, half in enumerate(halves(lane_blocks)):
        for s in range(2):
            fetches[3 + 2 * h + s].wait()
            part = x.at[s, :, pl.ds(h * width, width)]
            spread_rows(part, xs, (s * lane_blocks + h * SUB) * pitch, pitch, SUB)
            w = [taps[1 + s, i, half, :] for i in range(tap_count)]

            def body(block, window):
                window = list(window)
                for k in range(SUB):
                    t = block * SUB + k
                    window.append(row_at(xs, s * lane_blocks * pitch, pitch, h, t))
                    pair[s, t, half, :] = total(w[i] * window[-1 - i] for i in range(tap_count))
                return tuple(window[-(tap_count - 1) :])

            lax.fori_loop(0, rows // SUB, body, (zero,) * (tap_count - 1))
            stores.append(
                pltpu.make_async_copy(
                    pair.at[s, :, half, :], pair_far.at[s, :, half, :], sems.at[4 + 2 * count + 2 * h + s]
                )
            )
            stores[-1].start()
            first_rows[s, :, half, :] = pair[s, :SUB, half, :]
    for half in halves(lane_blocks):
        decay = [table[0, m, half, :] for m in range(modes)]

        def step(t, state):
            u = pair[0, t, half, :] * pair[1, t, half, :]
            return tuple(decay[m] * state[m] + u for m in range(modes))

        state = (zero,) * modes
        for t in range(tap_count - 1, SUB):
            state = step(t, state)

        def block_step(block, state):
            for k in range(SUB):
                state = step(block * SUB + k, state)
            return state

        state = lax.fori_loop(1, rows // SUB, block_step, state)
        for m in range(modes):
            ends[m, half, :] = state[m]
    for store in stores:
        store.wait()


def head_kernel(rows, first_in, halo, table, taps, ends, first_rows, state_out, message, hs):
    modes, lane_blocks = ends.shape[:2]
    reach = taps.shape[1] - 1
    for s in range(2):
        spread_rows(halo.at[1 + s], hs, s * lane_blocks * SUB, SUB, lane_blocks)
    for h, half in enumerate(halves(lane_blocks)):
        heads = []
        for s in range(2):
            w = [taps[1 + s, i, half, :] for i in range(reach + 1)]
            before = [row_at(hs, s * lane_blocks * SUB, SUB, h, j) for j in range(SUB)]
            head = []
            for t in range(SUB):
                row = first_in[s, t, half, :]
                if t < reach:
                    row = row + total(w[i] * before[SUB + t - i] for i in range(t + 1, reach + 1))
                    head.append(row)
                first_rows[s, t, half, :] = row
            heads.append(head)
        product = [heads[0][t] * heads[1][t] for t in range(reach)]
        states = []
        for m in range(modes):
            decay = table[0, m, half, :]
            state = product[0]
            for t in range(1, reach):
                state = decay * state + product[t]
            fade = jnp.exp(table[2, m, half, :] * -float(rows - reach))
            states.append(ends[m, half, :] + fade * state)
            state_out[m, half, :] = states[m]
        for m, value in enumerate(to_send(table, half, states, rows // 2, message.dtype)):
            message[m, half, :] = value


def query_kernel(x_far, halo, taps, gain, grad_far, query, scaled, x, grad, xs, gs, sems):
    rows, channels = x.shape
    lane_blocks = channels // LANES
    tap_count = taps.shape[1]
    pitch = rows + SUB
    fetches = [
        pltpu.make_async_copy(x_far.at[0], x, sems.at[0]),
        pltpu.make_async_copy(grad_far, grad, sems.at[1]),
    ]
    for fetch in fetches:
        fetch.start()
    spread_rows(halo.at[0], xs, 0, pitch, lane_blocks)
    fetches[0].wait()
    spread_rows(x, xs, SUB, pitch, lane_blocks)
    fetches[1].wait()
    spread_rows(grad, gs, 0, pitch, lane_blocks)
    for h, half in enumerate(halves(lane_blocks)):
        w = [taps[0, i, half, :] for i in range(tap_count)]
        g = gain[half, :]

        def body(block, window):
            window = list(window)
            for k in range(SUB):
                t = block * SUB + k
                window.append(row_at(xs, SUB, pitch, h, t))
                query[t, half, :] = total(w[i] * window[-1 - i] for i in range(tap_count))
                scaled[t, half, :] = g * row_at(gs, 0, pitch, h, t)
            return tuple(window[-(tap_count - 1) :])

        lax.fori_loop(
            0, rows // SUB, body, tuple(row_at(xs, 0, pitch, h, SUB + 1 - tap_count + j) for j in range(tap_count - 1))
        )


def local_kernel(pair, first_rows, table, local, rows_far, sem):
    rows = local.shape[0]
    modes, lane_blocks = table.shape[1:3]
    zero = jnp.zeros((SUB, LANES), jnp.float32)
    store = pltpu.make_async_copy(first_rows, rows_far, sem)
    store.start()
    for half in halves(lane_blocks):
        decay = [table[0, m, half, :] for m in range(modes)]
        scale = [table[1, m, half, :] for m in range(modes)]

        def block_step(source, block, state):
            for k in range(SUB):
                t = block * SUB + k
                u = source[0, t, half, :] * source[1, t, half, :]
                state = tuple(decay[m] * state[m] + u for m in range(modes))
                local[t, half, :] = total(scale[m] * state[m] for m in range(modes))
            return state

        state = block_step(first_rows, 0, (zero,) * modes)
        lax.fori_loop(1, rows // SUB, functools.partial(block_step, pair), state)
    store.wait()


def carry_kernel(span, place, entering, got, table, query, local, scaled, long_conv, sums, sq, cr):
    rows = local.shape[0]
    modes, lane_blocks = table.shape[1:3]
    for h, half in enumerate(halves(lane_blocks)):
        decay = [table[0, m, half, :] for m in range(modes)]
        start = []
        for m in range(modes):
            other = got[m, half, :].astype(jnp.float32)
            incoming = entering[m, half, :] + joined_term(rows, span, place, table[2, m, half, :], other)
            start.append(table[1, m, half, :] * decay[m] * incoming)

        def block_step(block, state):
            for k in range(SUB):
                t = block * SUB + k
                row = local[t, half, :] + total(state)
                state = tuple(decay[m] * state[m] for m in range(modes))
                long_conv[t, half, :] = row
                modulated = query[t, half, :] * row
                place = pl.ds(pl.multiple_of(t * SUB, SUB), SUB)
                square = modulated * modulated
                cross = scaled[t, half, :] * modulated
                sq[place, :] = square if h == 0 else sq[place, :] + square
                cr[place, :] = cross if h == 0 else cr[place, :] + cross
            return state

        lax.fori_loop(0, rows // SUB, block_step, tuple(start))
    for which, ref in enumerate((sq, cr)):
        blocks = []
        for b in range(rows // SUB):
            blocks.append(
                total(
                    ref[pl.ds(b * SUB * SUB + s, SUB, stride=SUB), :] for s in range(SUB)
                )
            )
        by_row = jnp.concatenate(blocks, axis=0)
        sums[which : which + 1, :] = jnp.sum(jnp.transpose(by_row), axis=0, keepdims=True)


def mixed_kernel(
    width, sums, table, query, long_conv, scaled, rows_far, mixed, long_grad, state_out, message, inv, head, inv_s, off_s,
    first_rows, sem,
):
    fetch = pltpu.make_async_copy(rows_far, first_rows, sem)
    fetch.start()
    rows = long_conv.shape[0]
    modes, lane_blocks = table.shape[1:3]
    zero = jnp.zeros((SUB, LANES), jnp.float32)
    inverse = lax.rsqrt(sums[0:1, :] / width + EPSILON)
    offset = inverse * inverse * inverse * sums[1:2, :] / width
    inv_s[...] = jnp.transpose(jnp.broadcast_to(inverse, (LANES, rows)))
    off_s[...] = jnp.transpose(jnp.broadcast_to(offset, (LANES, rows)))
    inv[...] = inv_s[...]
    blocks = rows // SUB
    for half in halves(lane_blocks):
        decay = [table[0, m, half, :] for m in range(modes)]

        def row(t, state):
            q = query[t, half, :]
            modulated = q * long_conv[t, half, :]
            mix = inv_s[pl.ds(t, 1), :] * scaled[t, half, :] - off_s[pl.ds(t, 1), :] * modulated
            mixed[t, half, :] = mix
            lg = mix * q
            long_grad[t, half, :] = lg
            return tuple(decay[m] * state[m] + lg for m in range(modes))

        def block_step(block, state):
            for k in range(SUB):
                state = row((blocks - 1 - block) * SUB + SUB - 1 - k, state)
            return state

        state = lax.fori_loop(0, blocks - 1, block_step, (zero,) * modes)
        if half.start == 0:
            fetch.wait()
        for t in reversed(range(SUB)):
            state = row(t, state)
            if t < head.shape[1]:
                gated = total(table[1, m, half, :] * state[m] for m in range(modes))
                found = (
                    mixed[t, half, :] * long_conv[t, half, :],
                    gated,
                    first_rows[1, t, half, :],
                    first_rows[0, t, half, :],
                )
                for i, value in enumerate(found):
                    head[i, t, half, :] = value
        for m, value in enumerate(to_send(table, half, state, rows // 2, message.dtype)):
            state_out[m, half, :] = state[m]
            message[m, half, :] = value


def back_kernel(table, long_grad, head_in, local, head):
    head[...] = head_in[...].astype(head.dtype)
    rows = long_grad.shape[0]
    modes, lane_blocks = table.shape[1:3]
    blocks = rows // SUB
    zero = jnp.zeros((SUB, LANES), jnp.float32)
    for half in halves(lane_blocks):
        decay = [table[0, m, half, :] for m in range(modes)]
        scale = [table[1, m, half, :] for m in range(modes)]

        def block_step(block, state):
            for k in range(SUB):
                t = (blocks - 1 - block) * SUB + SUB - 1 - k
                lg = long_grad[t, half, :]
                state = tuple(decay[m] * state[m] + lg for m in range(modes))
                local[t, half, :] = total(scale[m] * state[m] for m in range(modes))
            return state

        lax.fori_loop(0, blocks, block_step, (zero,) * modes)

def output_kernel(inv, taps, gain, query, long_conv, mixed, output, finished, last, os, qs):
    rows = long_conv.shape[0]
    lane_blocks = taps.shape[2]
    tap_count = taps.shape[1]
    pitch = rows + SUB
    blocks = rows // SUB
    zero = jnp.zeros((SUB, LANES), jnp.float32)
    for h, half in enumerate(halves(lane_blocks)):
        g = gain[half, :]
        w = [taps[0, i, half, :] for i in range(tap_count)]

        def out_step(block, window):
            window = list(window)
            for k in range(SUB):
                t = (blocks - 1 - block) * SUB + SUB - 1 - k
                long_row = long_conv[t, half, :]
                window.insert(0, mixed[t, half, :] * long_row)
                row = g * (query[t, half, :] * long_row) * inv[pl.ds(t, 1), :]
                os[pl.ds(h * SUB * pitch + t, SUB, stride=pitch), :] = row
                qs[pl.ds(h * SUB * pitch + t, SUB, stride=pitch), :] = total(
                    w[i] * window[i] for i in range(tap_count)
                )
            return tuple(window[: tap_count - 1])

        lax.fori_loop(0, blocks, out_step, (zero,) * (tap_count - 1))
    for lb in range(lane_blocks):
        columns = slice(lb * LANES, (lb + 1) * LANES)
        output[:, columns] = os[pl.ds(lb * pitch, rows), :].astype(output.dtype)
        finished[:, columns] = qs[pl.ds(lb * pitch, rows), :].astype(finished.dtype)
        last[pl.ds(lb * SUB, SUB), :] = qs[pl.ds(lb * pitch + rows - SUB, SUB), :]


def far_rows(table, half, state, rows, reach):
    modes = table.shape[1]
    at = [
        table[1, m, half, :]
        * state[m]
        * jnp.exp(table[2, m, half, :] * -float(rows - reach + 1))
        for m in range(modes)
    ]
    found = [None] * reach
    for i in reversed(range(reach)):
        found[i] = total(at)
        if i:
            at = [at[m] * table[0, m, half, :] for m in range(modes)]
    return found


def gather_kernel(rows, place, table, state, first, second, third, entering, message, *whole):
    modes, lane_blocks = state.shape[:2]
    inside = lax.rem(place[0], 4)
    for half in halves(lane_blocks):
        sent = []
        for m in range(modes):
            rate = table[2, m, half, :]
            found = None
            at_end = jnp.exp(rate * -steps(3 - inside, rows)) * state[m, half, :]
            for k, got in enumerate((first, second, third)):
                other = got[m, half, :].astype(jnp.float32)
                other_inside = inside ^ (k + 1)
                at_end = at_end + jnp.exp(rate * -steps(3 - other_inside, rows)) * other
                ahead = inside - other_inside
                term = jnp.where(above(ahead, 0), jnp.exp(rate * -steps(ahead - 1, rows)) * other, 0.0)
                found = term if found is None else found + term
            entering[m, half, :] = found
            sent.append(at_end)
            if whole:
                whole[0][m, half, :] = at_end
        for m, value in enumerate(to_send(table, half, sent, rows // 2, message.dtype)):
            message[m, half, :] = value


def join_kernel(rows, span, place, table, entering, whole, got, entering_out, message, whole_out):
    modes, lane_blocks = entering.shape[:2]
    upper = above(lax.rem(lax.div(place[0], span), 2), 0)
    for half in halves(lane_blocks):
        sent = []
        for m in range(modes):
            rate = table[2, m, half, :]
            other, mine = got[m, half, :].astype(jnp.float32), whole[m, half, :]
            entering_out[m, half, :] = entering[m, half, :] + joined_term(rows, span, place, rate, other)
            fade = jnp.exp(rate * -float(rows * span))
            sent.append(jnp.where(upper, mine, other) + fade * jnp.where(upper, other, mine))
            whole_out[m, half, :] = sent[m]
        for m, value in enumerate(to_send(table, half, sent, rows // 2, message.dtype)):
            message[m, half, :] = value


def steps(shards, rows):
    return jnp.maximum(shards, 0).astype(jnp.float32) * float(rows)


def above(value, bound):
    return jnp.full((SUB, LANES), value) > bound


def joined_term(rows, span, place, rate, other):
    upper = above(lax.rem(lax.div(place[0], span), 2), 0)
    return jnp.where(upper, jnp.exp(rate * -steps(lax.rem(place[0], span), rows)) * other, 0.0)


def joined_back_terms(rows, span, place, rate, other):
    lower = ~above(lax.rem(lax.div(place[0], span), 2), 0)
    to_end = span - 1 - lax.rem(place[0], span)
    here = jnp.where(lower, jnp.exp(rate * -steps(to_end, rows)) * other, 0.0)
    onward = jnp.where(lower & above(to_end, 0), jnp.exp(rate * -steps(to_end - 1, rows)) * other, 0.0)
    return here, onward


def joined_rows(span, place, other):
    lower = ~above(lax.rem(lax.div(place[0], span), 2), 0)
    at_end = ~above(span - 1 - lax.rem(place[0], span), 0)
    return jnp.where(lower & at_end, other, 0.0)


def gather_back_kernel(rows, reach, place, table, state, first, second, third, entering, beyond, added, message, *whole):
    modes, lane_blocks = state.shape[:2]
    inside = lax.rem(place[0], 4)
    for half in halves(lane_blocks):
        sent, rest = [], []
        for m in range(modes):
            rate = table[2, m, half, :]
            mine = state[m, half, :]
            at_start = jnp.exp(rate * -steps(inside, rows)) * mine
            after_first = jnp.where(above(inside, 0), jnp.exp(rate * -steps(inside - 1, rows)) * mine, 0.0)
            here = onward = jnp.zeros((SUB, LANES), jnp.float32)
            for k, got in enumerate((first, second, third)):
                other = got[m, half, :].astype(jnp.float32)
                other_inside = inside ^ (k + 1)
                at_start = at_start + jnp.exp(rate * -steps(other_inside, rows)) * other
                after_first = after_first + jnp.where(
                    above(other_inside, 0), jnp.exp(rate * -steps(other_inside - 1, rows)) * other, 0.0
                )
                ahead = other_inside - inside
                here = here + jnp.where(above(ahead, 0), jnp.exp(rate * -steps(ahead - 1, rows)) * other, 0.0)
                onward = onward + jnp.where(above(ahead, 1), jnp.exp(rate * -steps(ahead - 2, rows)) * other, 0.0)
            entering[m, half, :] = here
            beyond[m, half, :] = onward
            sent.append(at_start)
            rest.append(after_first)
            if whole:
                whole[0][m, half, :] = at_start
        for m, value in enumerate(to_send(table, half, sent, rows // 2, message.dtype)):
            message[m, half, :] = value
        found = far_rows(table, half, rest, rows, reach)
        for i in range(reach):
            added[i, half, :] = jnp.zeros((SUB, LANES), jnp.float32)
            message[modes + i, half, :] = found[i].astype(message.dtype)
            if whole:
                whole[0][modes + i, half, :] = found[i]


def join_back_kernel(
    rows, reach, span, place, table, entering, beyond, added, whole, got,
    entering_out, beyond_out, added_out, message, whole_out,
):
    modes, lane_blocks = entering.shape[:2]
    upper = above(lax.rem(lax.div(place[0], span), 2), 0)
    for half in halves(lane_blocks):
        sent, rest = [], []
        for m in range(modes):
            rate = table[2, m, half, :]
            other, mine = got[m, half, :].astype(jnp.float32), whole[m, half, :]
            here, onward = joined_back_terms(rows, span, place, rate, other)
            entering_out[m, half, :] = entering[m, half, :] + here
            beyond_out[m, half, :] = beyond[m, half, :] + onward
            low, high = jnp.where(upper, other, mine), jnp.where(upper, mine, other)
            sent.append(low + jnp.exp(rate * -float(rows * span)) * high)
            rest.append(jnp.exp(rate * -float(rows * (span - 1))) * high)
            whole_out[m, half, :] = sent[m]
        for m, value in enumerate(to_send(table, half, sent, rows // 2, message.dtype)):
            message[m, half, :] = value
        found = far_rows(table, half, rest, rows, reach)
        for i in range(reach):
            other, mine = got[modes + i, half, :].astype(jnp.float32), whole[modes + i, half, :]
            added_out[i, half, :] = added[i, half, :] + joined_rows(span, place, other)
            value = jnp.where(upper, other, mine) + found[i]
            message[modes + i, half, :] = value.astype(message.dtype)
            whole_out[modes + i, half, :] = value


def final_kernel(
    span, place, entering, beyond_in, added, got, table, taps, pair, first_rows, local, query, last, head, grads, cg, os, ls, made, edge, sems
):
    rows = local.shape[0]
    modes, lane_blocks = table.shape[1:3]
    tap_count = taps.shape[1]
    reach = tap_count - 1
    pitch = rows + SUB
    blocks = rows // SUB
    kept = rows - 2 * SUB
    moves = [
        pltpu.make_async_copy(
            query.at[pl.ds(0, kept), :], grads.at[0, pl.ds(0, kept), :], sems.at[0]
        )
    ]
    moves[0].start()
    ls[...] = last[...]
    for h, half in enumerate(halves(lane_blocks)):
        later = [head[0, i, half, :].astype(jnp.float32) for i in range(reach)]
        for t in range(SUB - reach, SUB):
            edge_rows = pl.ds(h * SUB * SUB + t, SUB, stride=SUB)
            ls[edge_rows, :] += total(
                taps[0, i, half, :] * later[t + i - SUB] for i in range(SUB - t, tap_count)
            )
    for lb in range(lane_blocks):
        columns = slice(lb * LANES, (lb + 1) * LANES)
        ending = jnp.concatenate(
            [query[kept : kept + SUB, columns].astype(jnp.float32), ls[pl.ds(lb * SUB, SUB), :]], axis=0
        )
        edge[:, columns] = ending.astype(edge.dtype)
    moves.append(
        pltpu.make_async_copy(edge, grads.at[0, pl.ds(kept, 2 * SUB), :], sems.at[len(moves)])
    )
    moves[-1].start()
    for h, half in enumerate(halves(lane_blocks)):
        decay = [table[0, m, half, :] for m in range(modes)]
        start, onward = [], []
        for m in range(modes):
            other = got[m, half, :].astype(jnp.float32)
            here, later = joined_back_terms(rows, span, place, table[2, m, half, :], other)
            start.append(table[1, m, half, :] * decay[m] * (entering[m, half, :] + here))
            onward.append(beyond_in[m, half, :] + later)

        def block_step(source, block, state):
            for k in range(SUB):
                t = (blocks - 1 - block) * SUB + SUB - 1 - k
                gated = local[t, half, :] + total(state)
                state = tuple(decay[m] * state[m] for m in range(modes))
                cg[0, t, :, :] = gated * source[1, t, half, :]
                cg[1, t, :, :] = gated * source[0, t, half, :]
            return state

        state = lax.fori_loop(0, blocks - 1, functools.partial(block_step, pair), tuple(start))
        block_step(first_rows, blocks - 1, state)
        own = far_rows(table, half, onward, rows, reach)
        beyond = [None, [], []]
        for i in range(reach):
            rows_there = joined_rows(span, place, got[modes + i, half, :].astype(jnp.float32))
            gated = head[1, i, half, :].astype(jnp.float32) + own[i] + added[i, half, :] + rows_there
            beyond[1].append(gated * head[2, i, half, :].astype(jnp.float32))
            beyond[2].append(gated * head[3, i, half, :].astype(jnp.float32))
        for s in range(1, 3):
            w = [taps[s, i, half, :] for i in range(tap_count)]

            def conv_step(block, window):
                window = list(window)
                for k in range(SUB):
                    t = (blocks - 1 - block) * SUB + SUB - 1 - k
                    window.insert(0, cg[s - 1, t, :, :])
                    os[pl.ds(t, SUB, stride=pitch), :] = total(
                        w[i] * window[i] for i in range(tap_count)
                    )
                return tuple(window[:reach])

            lax.fori_loop(0, blocks, conv_step, tuple(beyond[s]))
            for lb in range(SUB):
                first = (h * SUB + lb) * LANES
                made[s - 1, :, first : first + LANES] = os[pl.ds(lb * pitch, rows), :].astype(made.dtype)
            columns = pl.ds(h * SUB * LANES, SUB * LANES)
            moves.append(
                pltpu.make_async_copy(
                    made.at[s - 1, :, columns], grads.at[s, :, columns], sems.at[len(moves)]
                )
            )
            moves[-1].start()
    for move in moves:
        move.wait()


def kept(*shape, dtype=jnp.float32):
    return pltpu.VMEM(shape, dtype)


def run(kernel, ins, outs, scratch=(), work=0, aliases=None):
    ins = [pltpu.with_memory_space_constraint(a, space) for a, space in ins]
    spaces = [getattr(o, "memory_space", pltpu.VMEM) for o in outs]
    return pl.pallas_call(
        kernel,
        out_shape=outs,
        in_specs=[pl.BlockSpec(memory_space=jax.typeof(a).memory_space) for a in ins],
        out_specs=[pl.BlockSpec(memory_space=space) for space in spaces],
        scratch_shapes=[pltpu.VMEM(s, jnp.float32) if isinstance(s, tuple) else s for s in scratch],
        input_output_aliases=aliases or {},
        compiler_params=pltpu.CompilerParams(vmem_limit_bytes=VMEM_LIMIT),
        cost_estimate=pl.CostEstimate(flops=work, bytes_accessed=4 * 1024 * 1024, transcendentals=0),
    )(*ins)


def shifted(block, distance):
    devices = range(lax.axis_size("ctx"))
    route = [(i, i + distance) for i in devices if i + distance in devices]
    return lax.ppermute(block, "ctx", route)


def swapped(block, distance):
    return lax.ppermute(block, "ctx", [(i, i ^ distance) for i in range(lax.axis_size("ctx"))])


def on_device(streams, short_filter, decay_rate, residue, norm_gain, out_grad):
    rows, channels = streams.shape[1:]
    modes = decay_rate.shape[0]
    lane_blocks = channels // LANES
    tap_count = short_filter.shape[2]
    reach = tap_count - 1
    pitch = rows + SUB
    count = lax.axis_size("ctx")
    row_shape = (rows, lane_blocks, LANES)
    state_shape = (modes, lane_blocks, LANES)
    bf16 = jnp.bfloat16
    single = count <= 8
    wire = bf16 if single else jnp.float32

    def v(*arrays):
        return [(a, pltpu.VMEM) for a in arrays]

    def far(*arrays):
        return [(a, pltpu.HBM) for a in arrays]

    (tail,) = run(
        tail_kernel,
        far(streams),
        [jax.ShapeDtypeStruct((3, SUB, channels), bf16)],
        (pltpu.VMEM((3, 2 * SUB, channels), bf16), pltpu.SemaphoreType.DMA(())),
    )
    halo = shifted(tail, 1)
    gain = norm_gain.reshape(lane_blocks, LANES)
    pair_far, taps_far, first_rows, table, taps, ends = run(
        prepare_kernel,
        far(streams, jnp.swapaxes(short_filter, 1, 2), decay_rate, residue),
        [
            pltpu.HBM((2, *row_shape), jnp.float32),
            pltpu.HBM((3, tap_count, lane_blocks, LANES), jnp.float32),
            kept(2, SUB, lane_blocks, LANES),
            kept(3, *state_shape),
            kept(3, tap_count, lane_blocks, LANES),
            kept(*state_shape),
        ],
        (
            pltpu.VMEM((2, rows, channels), bf16),
            pltpu.VMEM((3, tap_count, channels // GROUP), bf16),
            (modes, channels),
            (modes, channels),
            (2, *row_shape),
            (2 * lane_blocks * pitch, LANES),
            (2 * lane_blocks * modes, LANES),
            pltpu.SemaphoreType.DMA((4 + lane_blocks // 2,)),
        ),
        work=10**9,
    )
    first_rows, state, message = run(
        functools.partial(head_kernel, rows),
        v(first_rows, halo, table, taps, ends),
        [kept(2, SUB, lane_blocks, LANES), kept(*state_shape), jax.ShapeDtypeStruct(state_shape, wire)],
        ((2 * lane_blocks * SUB, LANES),),
    )
    place = lax.axis_index("ctx").astype(jnp.int32)[None]

    query, scaled = run(
        query_kernel,
        far(streams) + v(halo, taps, gain) + far(out_grad),
        [kept(*row_shape), kept(*row_shape)],
        (
            pltpu.VMEM((rows, channels), bf16),
            pltpu.VMEM((rows, channels), bf16),
            (lane_blocks * pitch, LANES),
            (lane_blocks * pitch, LANES),
            pltpu.SemaphoreType.DMA((2,)),
        ),
        work=2 * 10**9,
    )
    local, rows_far = run(
        local_kernel,
        v(pair_far, first_rows, table),
        [kept(*row_shape), pltpu.HBM((2, SUB, lane_blocks, LANES), jnp.float32)],
        (pltpu.SemaphoreType.DMA(()),),
        work=2 * 10**9,
    )
    got = [swapped(message, k) for k in (1, 2, 3)]
    *got, query, scaled = lax.optimization_barrier((*got, query, scaled))
    entering, message, *whole = run(
        functools.partial(gather_kernel, rows),
        [(place, pltpu.SMEM)] + v(table, state, *got),
        [kept(*state_shape), jax.ShapeDtypeStruct(state_shape, wire)]
        + ([] if single else [kept(*state_shape)]),
    )
    span = 4
    got = swapped(message, span)
    while 2 * span < count:
        entering, message, *whole = run(
            functools.partial(join_kernel, rows, span),
            [(place, pltpu.SMEM)] + v(table, entering, *whole, got),
            [kept(*state_shape), jax.ShapeDtypeStruct(state_shape, wire), kept(*state_shape)],
        )
        span *= 2
        got = swapped(message, span)
    got, local = lax.optimization_barrier((got, local))
    long_conv, sums = run(
        functools.partial(carry_kernel, span),
        [(place, pltpu.SMEM)] + v(entering, got, table, query, local, scaled),
        [kept(*row_shape), kept(2, rows)],
        ((rows * SUB, LANES), (rows * SUB, LANES)),
    )
    sums = lax.psum(sums, "tp")
    mixed, long_grad, back, message, inv, head = run(
        functools.partial(mixed_kernel, float(channels * lax.axis_size("tp"))),
        v(sums, table, query, long_conv, scaled) + far(rows_far),
        [
            kept(*row_shape),
            kept(*row_shape),
            kept(*state_shape),
            jax.ShapeDtypeStruct(state_shape, wire),
            kept(rows, LANES),
            kept(4, reach, lane_blocks, LANES),
        ],
        (
            (rows, LANES),
            (rows, LANES),
            (2, SUB, lane_blocks, LANES),
            pltpu.SemaphoreType.DMA(()),
        ),
    )

    local_back, head = run(
        back_kernel,
        v(table, long_grad, head),
        [kept(*row_shape), jax.ShapeDtypeStruct(head.shape, bf16)],
        work=2 * 10**9,
    )
    message_shape = (modes + reach, lane_blocks, LANES)
    adjoint = [kept(*state_shape), kept(*state_shape), kept(reach, lane_blocks, LANES)]
    adjoint.append(jax.ShapeDtypeStruct(message_shape, wire))
    got = [swapped(message, k) for k in (1, 2, 3)]
    *got, local_back, mixed = lax.optimization_barrier((*got, local_back, mixed))
    output, finished, last = run(
        output_kernel,
        v(inv, taps_far, gain, query, long_conv, mixed),
        [
            jax.ShapeDtypeStruct((rows, channels), bf16),
            kept(rows, channels, dtype=bf16),
            kept(lane_blocks * SUB, LANES),
        ],
        ((lane_blocks * pitch, LANES), (lane_blocks * pitch, LANES)),
        work=2 * 10**9,
    )
    entering, beyond, added, message, *whole = run(
        functools.partial(gather_back_kernel, rows, reach),
        [(place, pltpu.SMEM)] + v(table, back, *got),
        adjoint + ([] if single else [kept(*message_shape)]),
    )
    span = 4
    got = swapped(message, span)
    while 2 * span < count:
        entering, beyond, added, message, *whole = run(
            functools.partial(join_back_kernel, rows, reach, span),
            [(place, pltpu.SMEM)] + v(table, entering, beyond, added, *whole, got),
            adjoint + [kept(*message_shape)],
        )
        span *= 2
        got = swapped(message, span)
    head = shifted(head, -1)
    got, finished = lax.optimization_barrier((got, finished))
    (grads,) = run(
        functools.partial(final_kernel, span),
        [(place, pltpu.SMEM)] + v(entering, beyond, added, got, table, taps_far, pair_far, rows_far, local_back, finished, last, head),
        [pltpu.HBM((3, rows, channels), bf16)],
        (
            (2, rows, SUB, LANES),
            (SUB * pitch, LANES),
            (lane_blocks * SUB, LANES),
            pltpu.VMEM((2, rows, channels), bf16),
            pltpu.VMEM((2 * SUB, channels), bf16),
            pltpu.SemaphoreType.DMA((2 + lane_blocks // 4,)),
        ),
    )
    return output, grads


def solution(mesh):
    return jax.shard_map(
        on_device,
        mesh=mesh,
        in_specs=(
            P(None, "ctx", "tp"),
            P(None, "tp", None),
            P(None, "tp"),
            P(None, "tp"),
            P("tp"),
            P("ctx", "tp"),
        ),
        out_specs=(P("ctx", "tp"), P(None, "ctx", "tp")),
        check_vma=False,
    )
```

```python
import functools

import jax
import jax.numpy as jnp
from jax import lax
from jax.experimental import pallas as pl
from jax.experimental.pallas import tpu as pltpu
from jax.sharding import PartitionSpec as P

GROUP = 16
LANES = 128
SUB = 8
EPSILON = 1e-05
VMEM_LIMIT = 16 * 1024 * 1024


def halves(lane_blocks):
    return [pl.ds(SUB * h, SUB) for h in range(lane_blocks // SUB)]


def total(terms):
    terms = list(terms)
    while len(terms) > 1:
        paired = [terms[i] + terms[i + 1] for i in range(0, len(terms) - 1, 2)]
        terms = paired + ([terms[-1]] if len(terms) % 2 else [])
    return terms[0]


def spread_rows(source, target, first, pitch, lane_blocks):
    rows = source.shape[0]
    for lb in range(lane_blocks):
        tile = source[:, lb * LANES : (lb + 1) * LANES]
        target[pl.ds(first + lb * pitch, rows), :] = tile.astype(jnp.float32)


def to_send(table, half, states, lag, dtype):
    modes = table.shape[1]
    if dtype != jnp.bfloat16:
        return states
    down, off_down, up, off_up, chosen, off = [], [], [], [], [], []
    for m in range(modes):
        x = states[m]
        near = x.astype(jnp.bfloat16).astype(jnp.float32)
        other = (x + jnp.where(near < x, 0.00390625, -0.00390625) * jnp.abs(x)).astype(jnp.bfloat16).astype(jnp.float32)
        weight = table[1, m, half, :] * jnp.exp(table[2, m, half, :] * -float(lag))
        down.append(near)
        up.append(other)
        off_down.append(weight * (near - x))
        off_up.append(weight * (other - x))
    sum_off = jnp.zeros((SUB, LANES), jnp.float32)
    for turn in range(2):
        for m in range(modes):
            base = sum_off if turn == 0 else sum_off - off[m]
            first, second = base + off_down[m], base + off_up[m]
            take = jnp.abs(second) < jnp.abs(first)
            sum_off = jnp.where(take, second, first)
            if turn == 0:
                off.append(jnp.where(take, off_up[m], off_down[m]))
            else:
                chosen.append(jnp.where(take, up[m], down[m]).astype(jnp.bfloat16))
    return chosen


def row_at(ref, first, pitch, half, place):
    return ref[pl.ds(first + half * SUB * pitch + place, SUB, stride=pitch), :]


def tail_kernel(x, tail, edge, sem):
    rows = x.shape[1]
    move = pltpu.make_async_copy(x.at[:, pl.ds(rows - 2 * SUB, 2 * SUB), :], edge, sem)
    move.start()
    move.wait()
    tail[...] = edge[:, SUB:, :]


def prepare_kernel(
    x_far, filt_far, rate_far, res_far, pair_far, taps_far, first_rows, table, taps, ends,
    x, filt, rate, res, pair, xs, ps, sems,
):
    rows, channels = x.shape[1:]
    modes = rate.shape[0]
    lane_blocks = channels // LANES
    tap_count = taps.shape[1]
    pitch = rows + SUB
    count = lane_blocks // SUB
    width = SUB * LANES
    fetches = [
        pltpu.make_async_copy(source, target, sems.at[i])
        for i, (source, target) in enumerate(
            [(filt_far, filt), (rate_far, rate), (res_far, res)]
            + [
                (x_far.at[1 + s, :, pl.ds(h * width, width)], x.at[s, :, pl.ds(h * width, width)])
                for h in range(count)
                for s in range(2)
            ]
        )
    ]
    for fetch in fetches:
        fetch.start()
    spread = (
        lax.broadcasted_iota(jnp.int32, (channels // GROUP, channels), 1) // GROUP
        == lax.broadcasted_iota(jnp.int32, (channels // GROUP, channels), 0)
    ).astype(jnp.bfloat16)
    fetches[0].wait()
    for s in range(3):
        weights = jnp.dot(filt[s], spread, preferred_element_type=jnp.float32)
        for lb in range(lane_blocks):
            ps[pl.ds(lb * SUB, tap_count), :] = weights[:, lb * LANES : (lb + 1) * LANES]
        for h, half in enumerate(halves(lane_blocks)):
            for i in range(tap_count):
                taps[s, i, half, :] = row_at(ps, 0, SUB, h, i)
    stores = [pltpu.make_async_copy(taps, taps_far, sems.at[3 + 2 * count])]
    stores[0].start()
    fetches[1].wait()
    fetches[2].wait()
    spread_rows(rate, ps, 0, modes, lane_blocks)
    spread_rows(res, ps, lane_blocks * modes, modes, lane_blocks)
    for h, half in enumerate(halves(lane_blocks)):
        for m in range(modes):
            r = row_at(ps, 0, modes, h, m)
            c = row_at(ps, lane_blocks * modes, modes, h, m)
            table[0, m, half, :] = jnp.exp(-r)
            table[1, m, half, :] = c * jnp.sqrt(2.0 * r)
            table[2, m, half, :] = r
    zero = jnp.zeros((SUB, LANES), jnp.float32)
    for h, half in enumerate(halves(lane_blocks)):
        for s in range(2):
            fetches[3 + 2 * h + s].wait()
            part = x.at[s, :, pl.ds(h * width, width)]
            spread_rows(part, xs, (s * lane_blocks + h * SUB) * pitch, pitch, SUB)
            w = [taps[1 + s, i, half, :] for i in range(tap_count)]

            def body(block, window):
                window = list(window)
                for k in range(SUB):
                    t = block * SUB + k
                    window.append(row_at(xs, s * lane_blocks * pitch, pitch, h, t))
                    pair[s, t, half, :] = total(w[i] * window[-1 - i] for i in range(tap_count))
                return tuple(window[-(tap_count - 1) :])

            lax.fori_loop(0, rows // SUB, body, (zero,) * (tap_count - 1))
            stores.append(
                pltpu.make_async_copy(
                    pair.at[s, :, half, :], pair_far.at[s, :, half, :], sems.at[4 + 2 * count + 2 * h + s]
                )
            )
            stores[-1].start()
            first_rows[s, :, half, :] = pair[s, :SUB, half, :]
    for half in halves(lane_blocks):
        decay = [table[0, m, half, :] for m in range(modes)]

        def step(t, state):
            u = pair[0, t, half, :] * pair[1, t, half, :]
            return tuple(decay[m] * state[m] + u for m in range(modes))

        state = (zero,) * modes
        for t in range(tap_count - 1, SUB):
            state = step(t, state)

        def block_step(block, state):
            for k in range(SUB):
                state = step(block * SUB + k, state)
            return state

        state = lax.fori_loop(1, rows // SUB, block_step, state)
        for m in range(modes):
            ends[m, half, :] = state[m]
    for store in stores:
        store.wait()


def head_kernel(rows, first_in, halo, table, taps, ends, first_rows, state_out, message, hs):
    modes, lane_blocks = ends.shape[:2]
    reach = taps.shape[1] - 1
    for s in range(2):
        spread_rows(halo.at[1 + s], hs, s * lane_blocks * SUB, SUB, lane_blocks)
    for h, half in enumerate(halves(lane_blocks)):
        heads = []
        for s in range(2):
            w = [taps[1 + s, i, half, :] for i in range(reach + 1)]
            before = [row_at(hs, s * lane_blocks * SUB, SUB, h, j) for j in range(SUB)]
            head = []
            for t in range(SUB):
                row = first_in[s, t, half, :]
                if t < reach:
                    row = row + total(w[i] * before[SUB + t - i] for i in range(t + 1, reach + 1))
                    head.append(row)
                first_rows[s, t, half, :] = row
            heads.append(head)
        product = [heads[0][t] * heads[1][t] for t in range(reach)]
        states = []
        for m in range(modes):
            decay = table[0, m, half, :]
            state = product[0]
            for t in range(1, reach):
                state = decay * state + product[t]
            fade = jnp.exp(table[2, m, half, :] * -float(rows - reach))
            states.append(ends[m, half, :] + fade * state)
            state_out[m, half, :] = states[m]
        for m, value in enumerate(to_send(table, half, states, rows // 2, message.dtype)):
            message[m, half, :] = value


def query_kernel(x_far, halo, taps, gain, grad_far, query, scaled, x, grad, xs, gs, sems):
    rows, channels = x.shape
    lane_blocks = channels // LANES
    tap_count = taps.shape[1]
    pitch = rows + SUB
    fetches = [
        pltpu.make_async_copy(x_far.at[0], x, sems.at[0]),
        pltpu.make_async_copy(grad_far, grad, sems.at[1]),
    ]
    for fetch in fetches:
        fetch.start()
    spread_rows(halo.at[0], xs, 0, pitch, lane_blocks)
    fetches[0].wait()
    spread_rows(x, xs, SUB, pitch, lane_blocks)
    fetches[1].wait()
    spread_rows(grad, gs, 0, pitch, lane_blocks)
    for h, half in enumerate(halves(lane_blocks)):
        w = [taps[0, i, half, :] for i in range(tap_count)]
        g = gain[half, :]

        def body(block, window):
            window = list(window)
            for k in range(SUB):
                t = block * SUB + k
                window.append(row_at(xs, SUB, pitch, h, t))
                query[t, half, :] = total(w[i] * window[-1 - i] for i in range(tap_count))
                scaled[t, half, :] = g * row_at(gs, 0, pitch, h, t)
            return tuple(window[-(tap_count - 1) :])

        lax.fori_loop(
            0, rows // SUB, body, tuple(row_at(xs, 0, pitch, h, SUB + 1 - tap_count + j) for j in range(tap_count - 1))
        )


def local_kernel(pair, first_rows, table, local, rows_far, sem):
    rows = local.shape[0]
    modes, lane_blocks = table.shape[1:3]
    zero = jnp.zeros((SUB, LANES), jnp.float32)
    store = pltpu.make_async_copy(first_rows, rows_far, sem)
    store.start()
    for half in halves(lane_blocks):
        decay = [table[0, m, half, :] for m in range(modes)]
        scale = [table[1, m, half, :] for m in range(modes)]

        def block_step(source, block, state):
            for k in range(SUB):
                t = block * SUB + k
                u = source[0, t, half, :] * source[1, t, half, :]
                state = tuple(decay[m] * state[m] + u for m in range(modes))
                local[t, half, :] = total(scale[m] * state[m] for m in range(modes))
            return state

        state = block_step(first_rows, 0, (zero,) * modes)
        lax.fori_loop(1, rows // SUB, functools.partial(block_step, pair), state)
    store.wait()


def carry_kernel(span, place, entering, got, table, query, local, scaled, long_conv, sums, sq, cr):
    rows = local.shape[0]
    modes, lane_blocks = table.shape[1:3]
    for h, half in enumerate(halves(lane_blocks)):
        decay = [table[0, m, half, :] for m in range(modes)]
        start = []
        for m in range(modes):
            other = got[m, half, :].astype(jnp.float32)
            incoming = entering[m, half, :] + joined_term(rows, span, place, table[2, m, half, :], other)
            start.append(table[1, m, half, :] * decay[m] * incoming)

        def block_step(block, state):
            for k in range(SUB):
                t = block * SUB + k
                row = local[t, half, :] + total(state)
                state = tuple(decay[m] * state[m] for m in range(modes))
                long_conv[t, half, :] = row
                modulated = query[t, half, :] * row
                place = pl.ds(pl.multiple_of(t * SUB, SUB), SUB)
                square = modulated * modulated
                cross = scaled[t, half, :] * modulated
                sq[place, :] = square if h == 0 else sq[place, :] + square
                cr[place, :] = cross if h == 0 else cr[place, :] + cross
            return state

        lax.fori_loop(0, rows // SUB, block_step, tuple(start))
    for which, ref in enumerate((sq, cr)):
        blocks = []
        for b in range(rows // SUB):
            blocks.append(
                total(
                    ref[pl.ds(b * SUB * SUB + s, SUB, stride=SUB), :] for s in range(SUB)
                )
            )
        by_row = jnp.concatenate(blocks, axis=0)
        sums[which : which + 1, :] = jnp.sum(jnp.transpose(by_row), axis=0, keepdims=True)


def mixed_kernel(
    width, sums, table, query, long_conv, scaled, rows_far, mixed, long_grad, state_out, message, inv, head, inv_s, off_s,
    first_rows, sem,
):
    fetch = pltpu.make_async_copy(rows_far, first_rows, sem)
    fetch.start()
    rows = long_conv.shape[0]
    modes, lane_blocks = table.shape[1:3]
    zero = jnp.zeros((SUB, LANES), jnp.float32)
    inverse = lax.rsqrt(sums[0:1, :] / width + EPSILON)
    offset = inverse * inverse * inverse * sums[1:2, :] / width
    inv_s[...] = jnp.transpose(jnp.broadcast_to(inverse, (LANES, rows)))
    off_s[...] = jnp.transpose(jnp.broadcast_to(offset, (LANES, rows)))
    inv[...] = inv_s[...]
    blocks = rows // SUB
    for half in halves(lane_blocks):
        decay = [table[0, m, half, :] for m in range(modes)]

        def row(t, state):
            q = query[t, half, :]
            modulated = q * long_conv[t, half, :]
            mix = inv_s[pl.ds(t, 1), :] * scaled[t, half, :] - off_s[pl.ds(t, 1), :] * modulated
            mixed[t, half, :] = mix
            lg = mix * q
            long_grad[t, half, :] = lg
            return tuple(decay[m] * state[m] + lg for m in range(modes))

        def block_step(block, state):
            for k in range(SUB):
                state = row((blocks - 1 - block) * SUB + SUB - 1 - k, state)
            return state

        state = lax.fori_loop(0, blocks - 1, block_step, (zero,) * modes)
        if half.start == 0:
            fetch.wait()
        for t in reversed(range(SUB)):
            state = row(t, state)
            if t < head.shape[1]:
                gated = total(table[1, m, half, :] * state[m] for m in range(modes))
                found = (
                    mixed[t, half, :] * long_conv[t, half, :],
                    gated,
                    first_rows[1, t, half, :],
                    first_rows[0, t, half, :],
                )
                for i, value in enumerate(found):
                    head[i, t, half, :] = value.astype(head.dtype)
        for m, value in enumerate(to_send(table, half, state, rows // 2, message.dtype)):
            state_out[m, half, :] = state[m]
            message[m, half, :] = value


def back_kernel(table, long_grad, local):
    rows = long_grad.shape[0]
    modes, lane_blocks = table.shape[1:3]
    blocks = rows // SUB
    zero = jnp.zeros((SUB, LANES), jnp.float32)
    for half in halves(lane_blocks):
        decay = [table[0, m, half, :] for m in range(modes)]
        scale = [table[1, m, half, :] for m in range(modes)]

        def block_step(block, state):
            for k in range(SUB):
                t = (blocks - 1 - block) * SUB + SUB - 1 - k
                lg = long_grad[t, half, :]
                state = tuple(decay[m] * state[m] + lg for m in range(modes))
                local[t, half, :] = total(scale[m] * state[m] for m in range(modes))
            return state

        lax.fori_loop(0, blocks, block_step, (zero,) * modes)

def output_kernel(inv, taps, gain, query, long_conv, mixed, output, finished, last, os, qs):
    rows = long_conv.shape[0]
    lane_blocks = taps.shape[2]
    tap_count = taps.shape[1]
    pitch = rows + SUB
    blocks = rows // SUB
    zero = jnp.zeros((SUB, LANES), jnp.float32)
    for h, half in enumerate(halves(lane_blocks)):
        g = gain[half, :]
        w = [taps[0, i, half, :] for i in range(tap_count)]

        def out_step(block, window):
            window = list(window)
            for k in range(SUB):
                t = (blocks - 1 - block) * SUB + SUB - 1 - k
                long_row = long_conv[t, half, :]
                window.insert(0, mixed[t, half, :] * long_row)
                row = g * (query[t, half, :] * long_row) * inv[pl.ds(t, 1), :]
                os[pl.ds(h * SUB * pitch + t, SUB, stride=pitch), :] = row
                qs[pl.ds(h * SUB * pitch + t, SUB, stride=pitch), :] = total(
                    w[i] * window[i] for i in range(tap_count)
                )
            return tuple(window[: tap_count - 1])

        lax.fori_loop(0, blocks, out_step, (zero,) * (tap_count - 1))
    for lb in range(lane_blocks):
        columns = slice(lb * LANES, (lb + 1) * LANES)
        output[:, columns] = os[pl.ds(lb * pitch, rows), :].astype(output.dtype)
        finished[:, columns] = qs[pl.ds(lb * pitch, rows), :].astype(finished.dtype)
        last[pl.ds(lb * SUB, SUB), :] = qs[pl.ds(lb * pitch + rows - SUB, SUB), :]


def far_rows(table, half, state, rows, reach):
    modes = table.shape[1]
    at = [
        table[1, m, half, :]
        * state[m]
        * jnp.exp(table[2, m, half, :] * -float(rows - reach + 1))
        for m in range(modes)
    ]
    found = [None] * reach
    for i in reversed(range(reach)):
        found[i] = total(at)
        if i:
            at = [at[m] * table[0, m, half, :] for m in range(modes)]
    return found


def gather_kernel(rows, place, table, state, first, second, third, entering, message, *whole):
    modes, lane_blocks = state.shape[:2]
    inside = lax.rem(place[0], 4)
    for half in halves(lane_blocks):
        sent = []
        for m in range(modes):
            rate = table[2, m, half, :]
            found = None
            at_end = jnp.exp(rate * -steps(3 - inside, rows)) * state[m, half, :]
            for k, got in enumerate((first, second, third)):
                other = got[m, half, :].astype(jnp.float32)
                other_inside = inside ^ (k + 1)
                at_end = at_end + jnp.exp(rate * -steps(3 - other_inside, rows)) * other
                ahead = inside - other_inside
                term = jnp.where(above(ahead, 0), jnp.exp(rate * -steps(ahead - 1, rows)) * other, 0.0)
                found = term if found is None else found + term
            entering[m, half, :] = found
            sent.append(at_end)
            if whole:
                whole[0][m, half, :] = at_end
        for m, value in enumerate(to_send(table, half, sent, rows // 2, message.dtype)):
            message[m, half, :] = value


def join_kernel(rows, span, place, table, entering, whole, got, entering_out, message, whole_out):
    modes, lane_blocks = entering.shape[:2]
    upper = above(lax.rem(lax.div(place[0], span), 2), 0)
    for half in halves(lane_blocks):
        sent = []
        for m in range(modes):
            rate = table[2, m, half, :]
            other, mine = got[m, half, :].astype(jnp.float32), whole[m, half, :]
            entering_out[m, half, :] = entering[m, half, :] + joined_term(rows, span, place, rate, other)
            fade = jnp.exp(rate * -float(rows * span))
            sent.append(jnp.where(upper, mine, other) + fade * jnp.where(upper, other, mine))
            whole_out[m, half, :] = sent[m]
        for m, value in enumerate(to_send(table, half, sent, rows // 2, message.dtype)):
            message[m, half, :] = value


def steps(shards, rows):
    return jnp.maximum(shards, 0).astype(jnp.float32) * float(rows)


def above(value, bound):
    return jnp.full((SUB, LANES), value) > bound


def joined_term(rows, span, place, rate, other):
    upper = above(lax.rem(lax.div(place[0], span), 2), 0)
    return jnp.where(upper, jnp.exp(rate * -steps(lax.rem(place[0], span), rows)) * other, 0.0)


def joined_back_terms(rows, span, place, rate, other):
    lower = ~above(lax.rem(lax.div(place[0], span), 2), 0)
    to_end = span - 1 - lax.rem(place[0], span)
    here = jnp.where(lower, jnp.exp(rate * -steps(to_end, rows)) * other, 0.0)
    onward = jnp.where(lower & above(to_end, 0), jnp.exp(rate * -steps(to_end - 1, rows)) * other, 0.0)
    return here, onward


def joined_rows(span, place, other):
    lower = ~above(lax.rem(lax.div(place[0], span), 2), 0)
    at_end = ~above(span - 1 - lax.rem(place[0], span), 0)
    return jnp.where(lower & at_end, other, 0.0)


def gather_back_kernel(rows, reach, place, table, state, first, second, third, entering, beyond, added, message, *whole):
    modes, lane_blocks = state.shape[:2]
    inside = lax.rem(place[0], 4)
    for half in halves(lane_blocks):
        sent, rest = [], []
        for m in range(modes):
            rate = table[2, m, half, :]
            mine = state[m, half, :]
            at_start = jnp.exp(rate * -steps(inside, rows)) * mine
            after_first = jnp.where(above(inside, 0), jnp.exp(rate * -steps(inside - 1, rows)) * mine, 0.0)
            here = onward = jnp.zeros((SUB, LANES), jnp.float32)
            for k, got in enumerate((first, second, third)):
                other = got[m, half, :].astype(jnp.float32)
                other_inside = inside ^ (k + 1)
                at_start = at_start + jnp.exp(rate * -steps(other_inside, rows)) * other
                after_first = after_first + jnp.where(
                    above(other_inside, 0), jnp.exp(rate * -steps(other_inside - 1, rows)) * other, 0.0
                )
                ahead = other_inside - inside
                here = here + jnp.where(above(ahead, 0), jnp.exp(rate * -steps(ahead - 1, rows)) * other, 0.0)
                onward = onward + jnp.where(above(ahead, 1), jnp.exp(rate * -steps(ahead - 2, rows)) * other, 0.0)
            entering[m, half, :] = here
            beyond[m, half, :] = onward
            sent.append(at_start)
            rest.append(after_first)
            if whole:
                whole[0][m, half, :] = at_start
        for m, value in enumerate(to_send(table, half, sent, rows // 2, message.dtype)):
            message[m, half, :] = value
        found = far_rows(table, half, rest, rows, reach)
        for i in range(reach):
            added[i, half, :] = jnp.zeros((SUB, LANES), jnp.float32)
            message[modes + i, half, :] = found[i].astype(message.dtype)
            if whole:
                whole[0][modes + i, half, :] = found[i]


def join_back_kernel(
    rows, reach, span, place, table, entering, beyond, added, whole, got,
    entering_out, beyond_out, added_out, message, whole_out,
):
    modes, lane_blocks = entering.shape[:2]
    upper = above(lax.rem(lax.div(place[0], span), 2), 0)
    for half in halves(lane_blocks):
        sent, rest = [], []
        for m in range(modes):
            rate = table[2, m, half, :]
            other, mine = got[m, half, :].astype(jnp.float32), whole[m, half, :]
            here, onward = joined_back_terms(rows, span, place, rate, other)
            entering_out[m, half, :] = entering[m, half, :] + here
            beyond_out[m, half, :] = beyond[m, half, :] + onward
            low, high = jnp.where(upper, other, mine), jnp.where(upper, mine, other)
            sent.append(low + jnp.exp(rate * -float(rows * span)) * high)
            rest.append(jnp.exp(rate * -float(rows * (span - 1))) * high)
            whole_out[m, half, :] = sent[m]
        for m, value in enumerate(to_send(table, half, sent, rows // 2, message.dtype)):
            message[m, half, :] = value
        found = far_rows(table, half, rest, rows, reach)
        for i in range(reach):
            other, mine = got[modes + i, half, :].astype(jnp.float32), whole[modes + i, half, :]
            added_out[i, half, :] = added[i, half, :] + joined_rows(span, place, other)
            value = jnp.where(upper, other, mine) + found[i]
            message[modes + i, half, :] = value.astype(message.dtype)
            whole_out[modes + i, half, :] = value


def final_kernel(
    span, place, entering, beyond_in, added, got, table, taps, pair, first_rows, local, query, last, head, grads, cg, os, ls, made, edge, sems
):
    rows = local.shape[0]
    modes, lane_blocks = table.shape[1:3]
    tap_count = taps.shape[1]
    reach = tap_count - 1
    pitch = rows + SUB
    blocks = rows // SUB
    kept = rows - 2 * SUB
    moves = [
        pltpu.make_async_copy(
            query.at[pl.ds(0, kept), :], grads.at[0, pl.ds(0, kept), :], sems.at[0]
        )
    ]
    moves[0].start()
    ls[...] = last[...]
    for h, half in enumerate(halves(lane_blocks)):
        later = [head[0, i, half, :].astype(jnp.float32) for i in range(reach)]
        for t in range(SUB - reach, SUB):
            edge_rows = pl.ds(h * SUB * SUB + t, SUB, stride=SUB)
            ls[edge_rows, :] += total(
                taps[0, i, half, :] * later[t + i - SUB] for i in range(SUB - t, tap_count)
            )
    for lb in range(lane_blocks):
        columns = slice(lb * LANES, (lb + 1) * LANES)
        ending = jnp.concatenate(
            [query[kept : kept + SUB, columns].astype(jnp.float32), ls[pl.ds(lb * SUB, SUB), :]], axis=0
        )
        edge[:, columns] = ending.astype(edge.dtype)
    moves.append(
        pltpu.make_async_copy(edge, grads.at[0, pl.ds(kept, 2 * SUB), :], sems.at[len(moves)])
    )
    moves[-1].start()
    for h, half in enumerate(halves(lane_blocks)):
        decay = [table[0, m, half, :] for m in range(modes)]
        start, onward = [], []
        for m in range(modes):
            other = got[m, half, :].astype(jnp.float32)
            here, later = joined_back_terms(rows, span, place, table[2, m, half, :], other)
            start.append(table[1, m, half, :] * decay[m] * (entering[m, half, :] + here))
            onward.append(beyond_in[m, half, :] + later)

        def block_step(source, block, state):
            for k in range(SUB):
                t = (blocks - 1 - block) * SUB + SUB - 1 - k
                gated = local[t, half, :] + total(state)
                state = tuple(decay[m] * state[m] for m in range(modes))
                cg[0, t, :, :] = gated * source[1, t, half, :]
                cg[1, t, :, :] = gated * source[0, t, half, :]
            return state

        state = lax.fori_loop(0, blocks - 1, functools.partial(block_step, pair), tuple(start))
        block_step(first_rows, blocks - 1, state)
        own = far_rows(table, half, onward, rows, reach)
        beyond = [None, [], []]
        for i in range(reach):
            rows_there = joined_rows(span, place, got[modes + i, half, :].astype(jnp.float32))
            gated = head[1, i, half, :].astype(jnp.float32) + own[i] + added[i, half, :] + rows_there
            beyond[1].append(gated * head[2, i, half, :].astype(jnp.float32))
            beyond[2].append(gated * head[3, i, half, :].astype(jnp.float32))
        for s in range(1, 3):
            w = [taps[s, i, half, :] for i in range(tap_count)]

            def conv_step(block, window):
                window = list(window)
                for k in range(SUB):
                    t = (blocks - 1 - block) * SUB + SUB - 1 - k
                    window.insert(0, cg[s - 1, t, :, :])
                    os[pl.ds(t, SUB, stride=pitch), :] = total(
                        w[i] * window[i] for i in range(tap_count)
                    )
                return tuple(window[:reach])

            lax.fori_loop(0, blocks, conv_step, tuple(beyond[s]))
            for lb in range(SUB):
                first = (h * SUB + lb) * LANES
                made[s - 1, :, first : first + LANES] = os[pl.ds(lb * pitch, rows), :].astype(made.dtype)
            columns = pl.ds(h * SUB * LANES, SUB * LANES)
            moves.append(
                pltpu.make_async_copy(
                    made.at[s - 1, :, columns], grads.at[s, :, columns], sems.at[len(moves)]
                )
            )
            moves[-1].start()
    for move in moves:
        move.wait()


def kept(*shape, dtype=jnp.float32):
    return pltpu.VMEM(shape, dtype)


def run(kernel, ins, outs, scratch=(), work=0, aliases=None):
    ins = [pltpu.with_memory_space_constraint(a, space) for a, space in ins]
    spaces = [getattr(o, "memory_space", pltpu.VMEM) for o in outs]
    return pl.pallas_call(
        kernel,
        out_shape=outs,
        in_specs=[pl.BlockSpec(memory_space=jax.typeof(a).memory_space) for a in ins],
        out_specs=[pl.BlockSpec(memory_space=space) for space in spaces],
        scratch_shapes=[pltpu.VMEM(s, jnp.float32) if isinstance(s, tuple) else s for s in scratch],
        input_output_aliases=aliases or {},
        compiler_params=pltpu.CompilerParams(vmem_limit_bytes=VMEM_LIMIT),
        cost_estimate=pl.CostEstimate(flops=work, bytes_accessed=4 * 1024 * 1024, transcendentals=0),
    )(*ins)


def shifted(block, distance):
    devices = range(lax.axis_size("ctx"))
    route = [(i, i + distance) for i in devices if i + distance in devices]
    return lax.ppermute(block, "ctx", route)


def swapped(block, distance):
    return lax.ppermute(block, "ctx", [(i, i ^ distance) for i in range(lax.axis_size("ctx"))])


def on_device(streams, short_filter, decay_rate, residue, norm_gain, out_grad):
    rows, channels = streams.shape[1:]
    modes = decay_rate.shape[0]
    lane_blocks = channels // LANES
    tap_count = short_filter.shape[2]
    reach = tap_count - 1
    pitch = rows + SUB
    count = lax.axis_size("ctx")
    row_shape = (rows, lane_blocks, LANES)
    state_shape = (modes, lane_blocks, LANES)
    bf16 = jnp.bfloat16
    single = count <= 8
    wire = bf16 if single else jnp.float32

    def v(*arrays):
        return [(a, pltpu.VMEM) for a in arrays]

    def far(*arrays):
        return [(a, pltpu.HBM) for a in arrays]

    (tail,) = run(
        tail_kernel,
        far(streams),
        [jax.ShapeDtypeStruct((3, SUB, channels), bf16)],
        (pltpu.VMEM((3, 2 * SUB, channels), bf16), pltpu.SemaphoreType.DMA(())),
    )
    halo = shifted(tail, 1)
    gain = norm_gain.reshape(lane_blocks, LANES)
    pair_far, taps_far, first_rows, table, taps, ends = run(
        prepare_kernel,
        far(streams, jnp.swapaxes(short_filter, 1, 2), decay_rate, residue),
        [
            pltpu.HBM((2, *row_shape), jnp.float32),
            pltpu.HBM((3, tap_count, lane_blocks, LANES), jnp.float32),
            kept(2, SUB, lane_blocks, LANES),
            kept(3, *state_shape),
            kept(3, tap_count, lane_blocks, LANES),
            kept(*state_shape),
        ],
        (
            pltpu.VMEM((2, rows, channels), bf16),
            pltpu.VMEM((3, tap_count, channels // GROUP), bf16),
            (modes, channels),
            (modes, channels),
            (2, *row_shape),
            (2 * lane_blocks * pitch, LANES),
            (2 * lane_blocks * modes, LANES),
            pltpu.SemaphoreType.DMA((4 + lane_blocks // 2,)),
        ),
        work=10**9,
    )
    first_rows, state, message = run(
        functools.partial(head_kernel, rows),
        v(first_rows, halo, table, taps, ends),
        [kept(2, SUB, lane_blocks, LANES), kept(*state_shape), jax.ShapeDtypeStruct(state_shape, wire)],
        ((2 * lane_blocks * SUB, LANES),),
    )
    place = lax.axis_index("ctx").astype(jnp.int32)[None]

    query, scaled = run(
        query_kernel,
        far(streams) + v(halo, taps, gain) + far(out_grad),
        [kept(*row_shape), kept(*row_shape)],
        (
            pltpu.VMEM((rows, channels), bf16),
            pltpu.VMEM((rows, channels), bf16),
            (lane_blocks * pitch, LANES),
            (lane_blocks * pitch, LANES),
            pltpu.SemaphoreType.DMA((2,)),
        ),
        work=2 * 10**9,
    )
    local, rows_far = run(
        local_kernel,
        v(pair_far, first_rows, table),
        [kept(*row_shape), pltpu.HBM((2, SUB, lane_blocks, LANES), jnp.float32)],
        (pltpu.SemaphoreType.DMA(()),),
        work=2 * 10**9,
    )
    got = [swapped(message, k) for k in (1, 2, 3)]
    *got, query, scaled = lax.optimization_barrier((*got, query, scaled))
    entering, message, *whole = run(
        functools.partial(gather_kernel, rows),
        [(place, pltpu.SMEM)] + v(table, state, *got),
        [kept(*state_shape), jax.ShapeDtypeStruct(state_shape, wire)]
        + ([] if single else [kept(*state_shape)]),
    )
    span = 4
    got = swapped(message, span)
    while 2 * span < count:
        entering, message, *whole = run(
            functools.partial(join_kernel, rows, span),
            [(place, pltpu.SMEM)] + v(table, entering, *whole, got),
            [kept(*state_shape), jax.ShapeDtypeStruct(state_shape, wire), kept(*state_shape)],
        )
        span *= 2
        got = swapped(message, span)
    got, local = lax.optimization_barrier((got, local))
    long_conv, sums = run(
        functools.partial(carry_kernel, span),
        [(place, pltpu.SMEM)] + v(entering, got, table, query, local, scaled),
        [kept(*row_shape), kept(2, rows)],
        ((rows * SUB, LANES), (rows * SUB, LANES)),
    )
    sums = lax.psum(sums, "tp")
    mixed, long_grad, back, message, inv, head = run(
        functools.partial(mixed_kernel, float(channels * lax.axis_size("tp"))),
        v(sums, table, query, long_conv, scaled) + far(rows_far),
        [
            kept(*row_shape),
            kept(*row_shape),
            kept(*state_shape),
            jax.ShapeDtypeStruct(state_shape, wire),
            kept(rows, LANES),
            jax.ShapeDtypeStruct((4, reach, lane_blocks, LANES), bf16),
        ],
        (
            (rows, LANES),
            (rows, LANES),
            (2, SUB, lane_blocks, LANES),
            pltpu.SemaphoreType.DMA(()),
        ),
    )

    (local_back,) = run(
        back_kernel, v(table, long_grad), [kept(*row_shape)], work=2 * 10**9
    )
    message_shape = (modes + reach, lane_blocks, LANES)
    adjoint = [kept(*state_shape), kept(*state_shape), kept(reach, lane_blocks, LANES)]
    adjoint.append(jax.ShapeDtypeStruct(message_shape, wire))
    got = [swapped(message, k) for k in (1, 2, 3)]
    *got, local_back, mixed = lax.optimization_barrier((*got, local_back, mixed))
    output, finished, last = run(
        output_kernel,
        v(inv, taps_far, gain, query, long_conv, mixed),
        [
            jax.ShapeDtypeStruct((rows, channels), bf16),
            kept(rows, channels, dtype=bf16),
            kept(lane_blocks * SUB, LANES),
        ],
        ((lane_blocks * pitch, LANES), (lane_blocks * pitch, LANES)),
        work=2 * 10**9,
    )
    entering, beyond, added, message, *whole = run(
        functools.partial(gather_back_kernel, rows, reach),
        [(place, pltpu.SMEM)] + v(table, back, *got),
        adjoint + ([] if single else [kept(*message_shape)]),
    )
    span = 4
    got = swapped(message, span)
    while 2 * span < count:
        entering, beyond, added, message, *whole = run(
            functools.partial(join_back_kernel, rows, reach, span),
            [(place, pltpu.SMEM)] + v(table, entering, beyond, added, *whole, got),
            adjoint + [kept(*message_shape)],
        )
        span *= 2
        got = swapped(message, span)
    head = shifted(head, -1)
    got, finished = lax.optimization_barrier((got, finished))
    (grads,) = run(
        functools.partial(final_kernel, span),
        [(place, pltpu.SMEM)] + v(entering, beyond, added, got, table, taps_far, pair_far, rows_far, local_back, finished, last, head),
        [pltpu.HBM((3, rows, channels), bf16)],
        (
            (2, rows, SUB, LANES),
            (SUB * pitch, LANES),
            (lane_blocks * SUB, LANES),
            pltpu.VMEM((2, rows, channels), bf16),
            pltpu.VMEM((2 * SUB, channels), bf16),
            pltpu.SemaphoreType.DMA((2 + lane_blocks // 4,)),
        ),
    )
    return output, grads


def solution(mesh):
    return jax.shard_map(
        on_device,
        mesh=mesh,
        in_specs=(
            P(None, "ctx", "tp"),
            P(None, "tp", None),
            P(None, "tp"),
            P(None, "tp"),
            P("tp"),
            P("ctx", "tp"),
        ),
        out_specs=(P("ctx", "tp"), P(None, "ctx", "tp")),
        check_vma=False,
    )
```

```python
import functools

import jax
import jax.numpy as jnp
from jax import lax
from jax.experimental import pallas as pl
from jax.experimental.pallas import tpu as pltpu
from jax.sharding import PartitionSpec as P

GROUP = 16
LANES = 128
SUB = 8
EPSILON = 1e-05
VMEM_LIMIT = 16 * 1024 * 1024


def halves(lane_blocks):
    return [pl.ds(SUB * h, SUB) for h in range(lane_blocks // SUB)]


def total(terms):
    terms = list(terms)
    while len(terms) > 1:
        paired = [terms[i] + terms[i + 1] for i in range(0, len(terms) - 1, 2)]
        terms = paired + ([terms[-1]] if len(terms) % 2 else [])
    return terms[0]


def spread_rows(source, target, first, pitch, lane_blocks):
    rows = source.shape[0]
    for lb in range(lane_blocks):
        tile = source[:, lb * LANES : (lb + 1) * LANES]
        target[pl.ds(first + lb * pitch, rows), :] = tile.astype(jnp.float32)


def to_send(table, half, states, lag, dtype):
    modes = table.shape[1]
    if dtype != jnp.bfloat16:
        return states
    down, off_down, up, off_up, chosen, off = [], [], [], [], [], []
    for m in range(modes):
        x = states[m]
        near = x.astype(jnp.bfloat16).astype(jnp.float32)
        other = (x + jnp.where(near < x, 0.00390625, -0.00390625) * jnp.abs(x)).astype(jnp.bfloat16).astype(jnp.float32)
        weight = table[1, m, half, :] * jnp.exp(table[2, m, half, :] * -float(lag))
        down.append(near)
        up.append(other)
        off_down.append(weight * (near - x))
        off_up.append(weight * (other - x))
    sum_off = jnp.zeros((SUB, LANES), jnp.float32)
    for turn in range(2):
        for m in range(modes):
            base = sum_off if turn == 0 else sum_off - off[m]
            first, second = base + off_down[m], base + off_up[m]
            take = jnp.abs(second) < jnp.abs(first)
            sum_off = jnp.where(take, second, first)
            if turn == 0:
                off.append(jnp.where(take, off_up[m], off_down[m]))
            else:
                chosen.append(jnp.where(take, up[m], down[m]).astype(jnp.bfloat16))
    return chosen


def row_at(ref, first, pitch, half, place):
    return ref[pl.ds(first + half * SUB * pitch + place, SUB, stride=pitch), :]


def tail_kernel(x, tail, edge, sem):
    rows = x.shape[1]
    move = pltpu.make_async_copy(x.at[:, pl.ds(rows - 2 * SUB, 2 * SUB), :], edge, sem)
    move.start()
    move.wait()
    tail[...] = edge[:, SUB:, :]


def prepare_kernel(
    x_far, filt_far, rate_far, res_far, pair_far, taps_far, first_rows, table, taps, ends,
    x, filt, rate, res, pair, xs, ps, sems,
):
    rows, channels = x.shape[1:]
    modes = rate.shape[0]
    lane_blocks = channels // LANES
    tap_count = taps.shape[1]
    pitch = rows + SUB
    count = lane_blocks // SUB
    width = SUB * LANES
    fetches = [
        pltpu.make_async_copy(source, target, sems.at[i])
        for i, (source, target) in enumerate(
            [(filt_far, filt), (rate_far, rate), (res_far, res)]
            + [
                (x_far.at[1 + s, :, pl.ds(h * width, width)], x.at[s, :, pl.ds(h * width, width)])
                for h in range(count)
                for s in range(2)
            ]
        )
    ]
    for fetch in fetches:
        fetch.start()
    spread = (
        lax.broadcasted_iota(jnp.int32, (channels // GROUP, channels), 1) // GROUP
        == lax.broadcasted_iota(jnp.int32, (channels // GROUP, channels), 0)
    ).astype(jnp.bfloat16)
    fetches[0].wait()
    for s in range(3):
        weights = jnp.dot(filt[s], spread, preferred_element_type=jnp.float32)
        for lb in range(lane_blocks):
            ps[pl.ds(lb * SUB, tap_count), :] = weights[:, lb * LANES : (lb + 1) * LANES]
        for h, half in enumerate(halves(lane_blocks)):
            for i in range(tap_count):
                taps[s, i, half, :] = row_at(ps, 0, SUB, h, i)
    stores = [pltpu.make_async_copy(taps, taps_far, sems.at[3 + 2 * count])]
    stores[0].start()
    fetches[1].wait()
    fetches[2].wait()
    spread_rows(rate, ps, 0, modes, lane_blocks)
    spread_rows(res, ps, lane_blocks * modes, modes, lane_blocks)
    for h, half in enumerate(halves(lane_blocks)):
        for m in range(modes):
            r = row_at(ps, 0, modes, h, m)
            c = row_at(ps, lane_blocks * modes, modes, h, m)
            table[0, m, half, :] = jnp.exp(-r)
            table[1, m, half, :] = c * jnp.sqrt(2.0 * r)
            table[2, m, half, :] = r
    zero = jnp.zeros((SUB, LANES), jnp.float32)
    for h, half in enumerate(halves(lane_blocks)):
        for s in range(2):
            fetches[3 + 2 * h + s].wait()
            part = x.at[s, :, pl.ds(h * width, width)]
            spread_rows(part, xs, (s * lane_blocks + h * SUB) * pitch, pitch, SUB)
            w = [taps[1 + s, i, half, :] for i in range(tap_count)]

            def body(block, window):
                window = list(window)
                for k in range(SUB):
                    t = block * SUB + k
                    window.append(row_at(xs, s * lane_blocks * pitch, pitch, h, t))
                    pair[s, t, half, :] = total(w[i] * window[-1 - i] for i in range(tap_count))
                return tuple(window[-(tap_count - 1) :])

            lax.fori_loop(0, rows // SUB, body, (zero,) * (tap_count - 1))
            stores.append(
                pltpu.make_async_copy(
                    pair.at[s, :, half, :], pair_far.at[s, :, half, :], sems.at[4 + 2 * count + 2 * h + s]
                )
            )
            stores[-1].start()
            first_rows[s, :, half, :] = pair[s, :SUB, half, :]
    for half in halves(lane_blocks):
        decay = [table[0, m, half, :] for m in range(modes)]

        def step(t, state):
            u = pair[0, t, half, :] * pair[1, t, half, :]
            return tuple(decay[m] * state[m] + u for m in range(modes))

        state = (zero,) * modes
        for t in range(tap_count - 1, SUB):
            state = step(t, state)

        def block_step(block, state):
            for k in range(SUB):
                state = step(block * SUB + k, state)
            return state

        state = lax.fori_loop(1, rows // SUB, block_step, state)
        for m in range(modes):
            ends[m, half, :] = state[m]
    for store in stores:
        store.wait()


def head_kernel(rows, first_in, halo, table, taps, ends, first_rows, state_out, message, hs):
    modes, lane_blocks = ends.shape[:2]
    reach = taps.shape[1] - 1
    for s in range(2):
        spread_rows(halo.at[1 + s], hs, s * lane_blocks * SUB, SUB, lane_blocks)
    for h, half in enumerate(halves(lane_blocks)):
        heads = []
        for s in range(2):
            w = [taps[1 + s, i, half, :] for i in range(reach + 1)]
            before = [row_at(hs, s * lane_blocks * SUB, SUB, h, j) for j in range(SUB)]
            head = []
            for t in range(SUB):
                row = first_in[s, t, half, :]
                if t < reach:
                    row = row + total(w[i] * before[SUB + t - i] for i in range(t + 1, reach + 1))
                    head.append(row)
                first_rows[s, t, half, :] = row
            heads.append(head)
        product = [heads[0][t] * heads[1][t] for t in range(reach)]
        states = []
        for m in range(modes):
            decay = table[0, m, half, :]
            state = product[0]
            for t in range(1, reach):
                state = decay * state + product[t]
            fade = jnp.exp(table[2, m, half, :] * -float(rows - reach))
            states.append(ends[m, half, :] + fade * state)
            state_out[m, half, :] = states[m]
        for m, value in enumerate(to_send(table, half, states, rows // 2, message.dtype)):
            message[m, half, :] = value


def query_kernel(x_far, halo, taps, gain, grad_far, query, scaled, x, grad, xs, gs, sems):
    rows, channels = x.shape
    lane_blocks = channels // LANES
    tap_count = taps.shape[1]
    pitch = rows + SUB
    fetches = [
        pltpu.make_async_copy(x_far.at[0], x, sems.at[0]),
        pltpu.make_async_copy(grad_far, grad, sems.at[1]),
    ]
    for fetch in fetches:
        fetch.start()
    spread_rows(halo.at[0], xs, 0, pitch, lane_blocks)
    fetches[0].wait()
    spread_rows(x, xs, SUB, pitch, lane_blocks)
    fetches[1].wait()
    spread_rows(grad, gs, 0, pitch, lane_blocks)
    for h, half in enumerate(halves(lane_blocks)):
        w = [taps[0, i, half, :] for i in range(tap_count)]
        g = gain[half, :]

        def body(block, window):
            window = list(window)
            for k in range(SUB):
                t = block * SUB + k
                window.append(row_at(xs, SUB, pitch, h, t))
                query[t, half, :] = total(w[i] * window[-1 - i] for i in range(tap_count))
                scaled[t, half, :] = g * row_at(gs, 0, pitch, h, t)
            return tuple(window[-(tap_count - 1) :])

        lax.fori_loop(
            0, rows // SUB, body, tuple(row_at(xs, 0, pitch, h, SUB + 1 - tap_count + j) for j in range(tap_count - 1))
        )


def local_kernel(pair, first_rows, table, local, rows_far, sem):
    rows = local.shape[0]
    modes, lane_blocks = table.shape[1:3]
    zero = jnp.zeros((SUB, LANES), jnp.float32)
    store = pltpu.make_async_copy(first_rows, rows_far, sem)
    store.start()
    for half in halves(lane_blocks):
        decay = [table[0, m, half, :] for m in range(modes)]
        scale = [table[1, m, half, :] for m in range(modes)]

        def block_step(source, block, state):
            for k in range(SUB):
                t = block * SUB + k
                u = source[0, t, half, :] * source[1, t, half, :]
                state = tuple(decay[m] * state[m] + u for m in range(modes))
                local[t, half, :] = total(scale[m] * state[m] for m in range(modes))
            return state

        state = block_step(first_rows, 0, (zero,) * modes)
        lax.fori_loop(1, rows // SUB, functools.partial(block_step, pair), state)
    store.wait()


def carry_kernel(span, place, entering, got, table, query, local, scaled, long_conv, sums, sq, cr):
    rows = local.shape[0]
    modes, lane_blocks = table.shape[1:3]
    for h, half in enumerate(halves(lane_blocks)):
        decay = [table[0, m, half, :] for m in range(modes)]
        start = []
        for m in range(modes):
            other = got[m, half, :].astype(jnp.float32)
            incoming = entering[m, half, :] + joined_term(rows, span, place, table[2, m, half, :], other)
            start.append(table[1, m, half, :] * decay[m] * incoming)

        def block_step(block, state):
            for k in range(SUB):
                t = block * SUB + k
                row = local[t, half, :] + total(state)
                state = tuple(decay[m] * state[m] for m in range(modes))
                long_conv[t, half, :] = row
                modulated = query[t, half, :] * row
                place = pl.ds(pl.multiple_of(t * SUB, SUB), SUB)
                square = modulated * modulated
                cross = scaled[t, half, :] * modulated
                sq[place, :] = square if h == 0 else sq[place, :] + square
                cr[place, :] = cross if h == 0 else cr[place, :] + cross
            return state

        lax.fori_loop(0, rows // SUB, block_step, tuple(start))
    for which, ref in enumerate((sq, cr)):
        blocks = []
        for b in range(rows // SUB):
            blocks.append(
                total(
                    ref[pl.ds(b * SUB * SUB + s, SUB, stride=SUB), :] for s in range(SUB)
                )
            )
        by_row = jnp.concatenate(blocks, axis=0)
        sums[which : which + 1, :] = jnp.sum(jnp.transpose(by_row), axis=0, keepdims=True)


def mixed_kernel(
    width, sums, table, query, long_conv, scaled, rows_far, mixed, long_grad, state_out, message, inv, head, inv_s, off_s,
    first_rows, sem,
):
    fetch = pltpu.make_async_copy(rows_far, first_rows, sem)
    fetch.start()
    rows = long_conv.shape[0]
    modes, lane_blocks = table.shape[1:3]
    zero = jnp.zeros((SUB, LANES), jnp.float32)
    inverse = lax.rsqrt(sums[0:1, :] / width + EPSILON)
    offset = inverse * inverse * inverse * sums[1:2, :] / width
    inv_s[...] = jnp.transpose(jnp.broadcast_to(inverse, (LANES, rows)))
    off_s[...] = jnp.transpose(jnp.broadcast_to(offset, (LANES, rows)))
    inv[...] = inv_s[...]
    blocks = rows // SUB
    for half in halves(lane_blocks):
        decay = [table[0, m, half, :] for m in range(modes)]

        def row(t, state):
            q = query[t, half, :]
            modulated = q * long_conv[t, half, :]
            mix = inv_s[pl.ds(t, 1), :] * scaled[t, half, :] - off_s[pl.ds(t, 1), :] * modulated
            mixed[t, half, :] = mix
            lg = mix * q
            long_grad[t, half, :] = lg
            return tuple(decay[m] * state[m] + lg for m in range(modes))

        def block_step(block, state):
            for k in range(SUB):
                state = row((blocks - 1 - block) * SUB + SUB - 1 - k, state)
            return state

        state = lax.fori_loop(0, blocks - 1, block_step, (zero,) * modes)
        if half.start == 0:
            fetch.wait()
        for t in reversed(range(SUB)):
            state = row(t, state)
            if t < head.shape[1]:
                gated = total(table[1, m, half, :] * state[m] for m in range(modes))
                found = (
                    mixed[t, half, :] * long_conv[t, half, :],
                    gated,
                    first_rows[1, t, half, :],
                    first_rows[0, t, half, :],
                )
                for i, value in enumerate(found):
                    head[i, t, half, :] = value.astype(head.dtype)
        for m, value in enumerate(to_send(table, half, state, rows // 2, message.dtype)):
            state_out[m, half, :] = state[m]
            message[m, half, :] = value


def back_kernel(table, long_grad, local):
    rows = long_grad.shape[0]
    modes, lane_blocks = table.shape[1:3]
    blocks = rows // SUB
    zero = jnp.zeros((SUB, LANES), jnp.float32)
    for half in halves(lane_blocks):
        decay = [table[0, m, half, :] for m in range(modes)]
        scale = [table[1, m, half, :] for m in range(modes)]

        def block_step(block, state):
            for k in range(SUB):
                t = (blocks - 1 - block) * SUB + SUB - 1 - k
                lg = long_grad[t, half, :]
                state = tuple(decay[m] * state[m] + lg for m in range(modes))
                local[t, half, :] = total(scale[m] * state[m] for m in range(modes))
            return state

        lax.fori_loop(0, blocks, block_step, (zero,) * modes)

def output_kernel(inv, taps, gain, query, long_conv, mixed, output, finished, last, os, qs):
    rows = long_conv.shape[0]
    lane_blocks = taps.shape[2]
    tap_count = taps.shape[1]
    pitch = rows + SUB
    blocks = rows // SUB
    zero = jnp.zeros((SUB, LANES), jnp.float32)
    for h, half in enumerate(halves(lane_blocks)):
        g = gain[half, :]
        w = [taps[0, i, half, :] for i in range(tap_count)]

        def out_step(block, window):
            window = list(window)
            for k in range(SUB):
                t = (blocks - 1 - block) * SUB + SUB - 1 - k
                long_row = long_conv[t, half, :]
                window.insert(0, mixed[t, half, :] * long_row)
                row = g * (query[t, half, :] * long_row) * inv[pl.ds(t, 1), :]
                os[pl.ds(h * SUB * pitch + t, SUB, stride=pitch), :] = row
                qs[pl.ds(h * SUB * pitch + t, SUB, stride=pitch), :] = total(
                    w[i] * window[i] for i in range(tap_count)
                )
            return tuple(window[: tap_count - 1])

        lax.fori_loop(0, blocks, out_step, (zero,) * (tap_count - 1))
    for lb in range(lane_blocks):
        columns = slice(lb * LANES, (lb + 1) * LANES)
        output[:, columns] = os[pl.ds(lb * pitch, rows), :].astype(output.dtype)
        finished[:, columns] = qs[pl.ds(lb * pitch, rows), :].astype(finished.dtype)
        last[pl.ds(lb * SUB, SUB), :] = qs[pl.ds(lb * pitch + rows - SUB, SUB), :]


def far_rows(table, half, state, rows, reach):
    modes = table.shape[1]
    at = [
        table[1, m, half, :]
        * state[m]
        * jnp.exp(table[2, m, half, :] * -float(rows - reach + 1))
        for m in range(modes)
    ]
    found = [None] * reach
    for i in reversed(range(reach)):
        found[i] = total(at)
        if i:
            at = [at[m] * table[0, m, half, :] for m in range(modes)]
    return found


def gather_kernel(rows, place, table, state, first, second, third, entering, message, *whole):
    modes, lane_blocks = state.shape[:2]
    inside = lax.rem(place[0], 4)
    for half in halves(lane_blocks):
        sent = []
        for m in range(modes):
            rate = table[2, m, half, :]
            found = None
            at_end = jnp.exp(rate * -steps(3 - inside, rows)) * state[m, half, :]
            for k, got in enumerate((first, second, third)):
                other = got[m, half, :].astype(jnp.float32)
                other_inside = inside ^ (k + 1)
                at_end = at_end + jnp.exp(rate * -steps(3 - other_inside, rows)) * other
                ahead = inside - other_inside
                term = jnp.where(above(ahead, 0), jnp.exp(rate * -steps(ahead - 1, rows)) * other, 0.0)
                found = term if found is None else found + term
            entering[m, half, :] = found
            sent.append(at_end)
            if whole:
                whole[0][m, half, :] = at_end
        for m, value in enumerate(to_send(table, half, sent, rows // 2, message.dtype)):
            message[m, half, :] = value


def join_kernel(rows, span, place, table, entering, whole, got, entering_out, message, whole_out):
    modes, lane_blocks = entering.shape[:2]
    upper = above(lax.rem(lax.div(place[0], span), 2), 0)
    for half in halves(lane_blocks):
        sent = []
        for m in range(modes):
            rate = table[2, m, half, :]
            other, mine = got[m, half, :].astype(jnp.float32), whole[m, half, :]
            entering_out[m, half, :] = entering[m, half, :] + joined_term(rows, span, place, rate, other)
            fade = jnp.exp(rate * -float(rows * span))
            sent.append(jnp.where(upper, mine, other) + fade * jnp.where(upper, other, mine))
            whole_out[m, half, :] = sent[m]
        for m, value in enumerate(to_send(table, half, sent, rows // 2, message.dtype)):
            message[m, half, :] = value


def steps(shards, rows):
    return jnp.maximum(shards, 0).astype(jnp.float32) * float(rows)


def above(value, bound):
    return jnp.full((SUB, LANES), value) > bound


def joined_term(rows, span, place, rate, other):
    upper = above(lax.rem(lax.div(place[0], span), 2), 0)
    return jnp.where(upper, jnp.exp(rate * -steps(lax.rem(place[0], span), rows)) * other, 0.0)


def joined_back_terms(rows, span, place, rate, other):
    lower = ~above(lax.rem(lax.div(place[0], span), 2), 0)
    to_end = span - 1 - lax.rem(place[0], span)
    here = jnp.where(lower, jnp.exp(rate * -steps(to_end, rows)) * other, 0.0)
    onward = jnp.where(lower & above(to_end, 0), jnp.exp(rate * -steps(to_end - 1, rows)) * other, 0.0)
    return here, onward


def joined_rows(span, place, other):
    lower = ~above(lax.rem(lax.div(place[0], span), 2), 0)
    at_end = ~above(span - 1 - lax.rem(place[0], span), 0)
    return jnp.where(lower & at_end, other, 0.0)


def gather_back_kernel(rows, reach, place, table, state, first, second, third, entering, beyond, added, message, *whole):
    modes, lane_blocks = state.shape[:2]
    inside = lax.rem(place[0], 4)
    for half in halves(lane_blocks):
        sent, rest = [], []
        for m in range(modes):
            rate = table[2, m, half, :]
            mine = state[m, half, :]
            at_start = jnp.exp(rate * -steps(inside, rows)) * mine
            after_first = jnp.where(above(inside, 0), jnp.exp(rate * -steps(inside - 1, rows)) * mine, 0.0)
            here = onward = jnp.zeros((SUB, LANES), jnp.float32)
            for k, got in enumerate((first, second, third)):
                other = got[m, half, :].astype(jnp.float32)
                other_inside = inside ^ (k + 1)
                at_start = at_start + jnp.exp(rate * -steps(other_inside, rows)) * other
                after_first = after_first + jnp.where(
                    above(other_inside, 0), jnp.exp(rate * -steps(other_inside - 1, rows)) * other, 0.0
                )
                ahead = other_inside - inside
                here = here + jnp.where(above(ahead, 0), jnp.exp(rate * -steps(ahead - 1, rows)) * other, 0.0)
                onward = onward + jnp.where(above(ahead, 1), jnp.exp(rate * -steps(ahead - 2, rows)) * other, 0.0)
            entering[m, half, :] = here
            beyond[m, half, :] = onward
            sent.append(at_start)
            rest.append(after_first)
            if whole:
                whole[0][m, half, :] = at_start
        for m, value in enumerate(to_send(table, half, sent, rows // 2, message.dtype)):
            message[m, half, :] = value
        found = far_rows(table, half, rest, rows, reach)
        for i in range(reach):
            added[i, half, :] = jnp.zeros((SUB, LANES), jnp.float32)
            message[modes + i, half, :] = found[i].astype(message.dtype)
            if whole:
                whole[0][modes + i, half, :] = found[i]


def join_back_kernel(
    rows, reach, span, place, table, entering, beyond, added, whole, got,
    entering_out, beyond_out, added_out, message, whole_out,
):
    modes, lane_blocks = entering.shape[:2]
    upper = above(lax.rem(lax.div(place[0], span), 2), 0)
    for half in halves(lane_blocks):
        sent, rest = [], []
        for m in range(modes):
            rate = table[2, m, half, :]
            other, mine = got[m, half, :].astype(jnp.float32), whole[m, half, :]
            here, onward = joined_back_terms(rows, span, place, rate, other)
            entering_out[m, half, :] = entering[m, half, :] + here
            beyond_out[m, half, :] = beyond[m, half, :] + onward
            low, high = jnp.where(upper, other, mine), jnp.where(upper, mine, other)
            sent.append(low + jnp.exp(rate * -float(rows * span)) * high)
            rest.append(jnp.exp(rate * -float(rows * (span - 1))) * high)
            whole_out[m, half, :] = sent[m]
        for m, value in enumerate(to_send(table, half, sent, rows // 2, message.dtype)):
            message[m, half, :] = value
        found = far_rows(table, half, rest, rows, reach)
        for i in range(reach):
            other, mine = got[modes + i, half, :].astype(jnp.float32), whole[modes + i, half, :]
            added_out[i, half, :] = added[i, half, :] + joined_rows(span, place, other)
            value = jnp.where(upper, other, mine) + found[i]
            message[modes + i, half, :] = value.astype(message.dtype)
            whole_out[modes + i, half, :] = value


def final_kernel(
    span, place, entering, beyond_in, added, got, table, taps, pair, first_rows, local, query, last, head, grads, cg, os, ls, made, edge, sems
):
    rows = local.shape[0]
    modes, lane_blocks = table.shape[1:3]
    tap_count = taps.shape[1]
    reach = tap_count - 1
    pitch = rows + SUB
    blocks = rows // SUB
    kept = rows - 2 * SUB
    moves = [
        pltpu.make_async_copy(
            query.at[pl.ds(0, kept), :], grads.at[0, pl.ds(0, kept), :], sems.at[0]
        )
    ]
    moves[0].start()
    ls[...] = last[...]
    for h, half in enumerate(halves(lane_blocks)):
        later = [head[0, i, half, :].astype(jnp.float32) for i in range(reach)]
        for t in range(SUB - reach, SUB):
            edge_rows = pl.ds(h * SUB * SUB + t, SUB, stride=SUB)
            ls[edge_rows, :] += total(
                taps[0, i, half, :] * later[t + i - SUB] for i in range(SUB - t, tap_count)
            )
    for lb in range(lane_blocks):
        columns = slice(lb * LANES, (lb + 1) * LANES)
        ending = jnp.concatenate(
            [query[kept : kept + SUB, columns].astype(jnp.float32), ls[pl.ds(lb * SUB, SUB), :]], axis=0
        )
        edge[:, columns] = ending.astype(edge.dtype)
    moves.append(
        pltpu.make_async_copy(edge, grads.at[0, pl.ds(kept, 2 * SUB), :], sems.at[len(moves)])
    )
    moves[-1].start()
    for h, half in enumerate(halves(lane_blocks)):
        decay = [table[0, m, half, :] for m in range(modes)]
        start, onward = [], []
        for m in range(modes):
            other = got[m, half, :].astype(jnp.float32)
            here, later = joined_back_terms(rows, span, place, table[2, m, half, :], other)
            start.append(table[1, m, half, :] * decay[m] * (entering[m, half, :] + here))
            onward.append(beyond_in[m, half, :] + later)

        def block_step(source, block, state):
            for k in range(SUB):
                t = (blocks - 1 - block) * SUB + SUB - 1 - k
                gated = local[t, half, :] + total(state)
                state = tuple(decay[m] * state[m] for m in range(modes))
                cg[0, t, :, :] = gated * source[1, t, half, :]
                cg[1, t, :, :] = gated * source[0, t, half, :]
            return state

        state = lax.fori_loop(0, blocks - 1, functools.partial(block_step, pair), tuple(start))
        block_step(first_rows, blocks - 1, state)
        own = far_rows(table, half, onward, rows, reach)
        beyond = [None, [], []]
        for i in range(reach):
            rows_there = joined_rows(span, place, got[modes + i, half, :].astype(jnp.float32))
            gated = head[1, i, half, :].astype(jnp.float32) + own[i] + added[i, half, :] + rows_there
            beyond[1].append(gated * head[2, i, half, :].astype(jnp.float32))
            beyond[2].append(gated * head[3, i, half, :].astype(jnp.float32))
        for s in range(1, 3):
            w = [taps[s, i, half, :] for i in range(tap_count)]

            def conv_step(block, window):
                window = list(window)
                for k in range(SUB):
                    t = (blocks - 1 - block) * SUB + SUB - 1 - k
                    window.insert(0, cg[s - 1, t, :, :])
                    os[pl.ds(t, SUB, stride=pitch), :] = total(
                        w[i] * window[i] for i in range(tap_count)
                    )
                return tuple(window[:reach])

            lax.fori_loop(0, blocks, conv_step, tuple(beyond[s]))
            for lb in range(SUB):
                first = (h * SUB + lb) * LANES
                made[s - 1, :, first : first + LANES] = os[pl.ds(lb * pitch, rows), :].astype(made.dtype)
            columns = pl.ds(h * SUB * LANES, SUB * LANES)
            moves.append(
                pltpu.make_async_copy(
                    made.at[s - 1, :, columns], grads.at[s, :, columns], sems.at[len(moves)]
                )
            )
            moves[-1].start()
    for move in moves:
        move.wait()


def kept(*shape, dtype=jnp.float32):
    return pltpu.VMEM(shape, dtype)


def run(kernel, ins, outs, scratch=(), work=0, aliases=None):
    ins = [pltpu.with_memory_space_constraint(a, space) for a, space in ins]
    spaces = [getattr(o, "memory_space", pltpu.VMEM) for o in outs]
    return pl.pallas_call(
        kernel,
        out_shape=outs,
        in_specs=[pl.BlockSpec(memory_space=jax.typeof(a).memory_space) for a in ins],
        out_specs=[pl.BlockSpec(memory_space=space) for space in spaces],
        scratch_shapes=[pltpu.VMEM(s, jnp.float32) if isinstance(s, tuple) else s for s in scratch],
        input_output_aliases=aliases or {},
        compiler_params=pltpu.CompilerParams(vmem_limit_bytes=VMEM_LIMIT),
        cost_estimate=pl.CostEstimate(flops=work, bytes_accessed=4 * 1024 * 1024, transcendentals=0),
    )(*ins)


def shifted(block, distance):
    devices = range(lax.axis_size("ctx"))
    route = [(i, i + distance) for i in devices if i + distance in devices]
    return lax.ppermute(block, "ctx", route)


def swapped(block, distance):
    return lax.ppermute(block, "ctx", [(i, i ^ distance) for i in range(lax.axis_size("ctx"))])


def on_device(streams, short_filter, decay_rate, residue, norm_gain, out_grad):
    rows, channels = streams.shape[1:]
    modes = decay_rate.shape[0]
    lane_blocks = channels // LANES
    tap_count = short_filter.shape[2]
    reach = tap_count - 1
    pitch = rows + SUB
    count = lax.axis_size("ctx")
    row_shape = (rows, lane_blocks, LANES)
    state_shape = (modes, lane_blocks, LANES)
    bf16 = jnp.bfloat16
    single = count <= 8
    wire = bf16 if single else jnp.float32

    def v(*arrays):
        return [(a, pltpu.VMEM) for a in arrays]

    def far(*arrays):
        return [(a, pltpu.HBM) for a in arrays]

    (tail,) = run(
        tail_kernel,
        far(streams),
        [jax.ShapeDtypeStruct((3, SUB, channels), bf16)],
        (pltpu.VMEM((3, 2 * SUB, channels), bf16), pltpu.SemaphoreType.DMA(())),
    )
    halo = shifted(tail, 1)
    gain = norm_gain.reshape(lane_blocks, LANES)
    pair_far, taps_far, first_rows, table, taps, ends = run(
        prepare_kernel,
        far(streams, jnp.swapaxes(short_filter, 1, 2), decay_rate, residue),
        [
            pltpu.HBM((2, *row_shape), jnp.float32),
            pltpu.HBM((3, tap_count, lane_blocks, LANES), jnp.float32),
            kept(2, SUB, lane_blocks, LANES),
            kept(3, *state_shape),
            kept(3, tap_count, lane_blocks, LANES),
            kept(*state_shape),
        ],
        (
            pltpu.VMEM((2, rows, channels), bf16),
            pltpu.VMEM((3, tap_count, channels // GROUP), bf16),
            (modes, channels),
            (modes, channels),
            (2, *row_shape),
            (2 * lane_blocks * pitch, LANES),
            (2 * lane_blocks * modes, LANES),
            pltpu.SemaphoreType.DMA((4 + lane_blocks // 2,)),
        ),
        work=10**9,
    )
    first_rows, state, message = run(
        functools.partial(head_kernel, rows),
        v(first_rows, halo, table, taps, ends),
        [kept(2, SUB, lane_blocks, LANES), kept(*state_shape), jax.ShapeDtypeStruct(state_shape, wire)],
        ((2 * lane_blocks * SUB, LANES),),
    )
    place = lax.axis_index("ctx").astype(jnp.int32)[None]

    query, scaled = run(
        query_kernel,
        far(streams) + v(halo, taps, gain) + far(out_grad),
        [kept(*row_shape), kept(*row_shape)],
        (
            pltpu.VMEM((rows, channels), bf16),
            pltpu.VMEM((rows, channels), bf16),
            (lane_blocks * pitch, LANES),
            (lane_blocks * pitch, LANES),
            pltpu.SemaphoreType.DMA((2,)),
        ),
        work=2 * 10**9,
    )
    local, rows_far = run(
        local_kernel,
        v(pair_far, first_rows, table),
        [kept(*row_shape), pltpu.HBM((2, SUB, lane_blocks, LANES), jnp.float32)],
        (pltpu.SemaphoreType.DMA(()),),
        work=2 * 10**9,
    )
    got = [swapped(message, k) for k in (1, 2, 3)]
    *got, query, scaled = lax.optimization_barrier((*got, query, scaled))
    entering, message, *whole = run(
        functools.partial(gather_kernel, rows),
        [(place, pltpu.SMEM)] + v(table, state, *got),
        [kept(*state_shape), jax.ShapeDtypeStruct(state_shape, wire)]
        + ([] if single else [kept(*state_shape)]),
    )
    span = 4
    got = swapped(message, span)
    while 2 * span < count:
        entering, message, *whole = run(
            functools.partial(join_kernel, rows, span),
            [(place, pltpu.SMEM)] + v(table, entering, *whole, got),
            [kept(*state_shape), jax.ShapeDtypeStruct(state_shape, wire), kept(*state_shape)],
        )
        span *= 2
        got = swapped(message, span)
    got, local = lax.optimization_barrier((got, local))
    long_conv, sums = run(
        functools.partial(carry_kernel, span),
        [(place, pltpu.SMEM)] + v(entering, got, table, query, local, scaled),
        [kept(*row_shape), kept(2, rows)],
        ((rows * SUB, LANES), (rows * SUB, LANES)),
    )
    parts = lax.axis_size("tp")
    if parts & (parts - 1):
        sums = lax.psum(sums, "tp")
    else:
        for k in range(parts.bit_length() - 1):
            sums = sums + lax.ppermute(sums, "tp", [(i, i ^ (1 << k)) for i in range(parts)])
    mixed, long_grad, back, message, inv, head = run(
        functools.partial(mixed_kernel, float(channels * lax.axis_size("tp"))),
        v(sums, table, query, long_conv, scaled) + far(rows_far),
        [
            kept(*row_shape),
            kept(*row_shape),
            kept(*state_shape),
            jax.ShapeDtypeStruct(state_shape, wire),
            kept(rows, LANES),
            jax.ShapeDtypeStruct((4, reach, lane_blocks, LANES), bf16),
        ],
        (
            (rows, LANES),
            (rows, LANES),
            (2, SUB, lane_blocks, LANES),
            pltpu.SemaphoreType.DMA(()),
        ),
    )

    (local_back,) = run(
        back_kernel, v(table, long_grad), [kept(*row_shape)], work=2 * 10**9
    )
    message_shape = (modes + reach, lane_blocks, LANES)
    adjoint = [kept(*state_shape), kept(*state_shape), kept(reach, lane_blocks, LANES)]
    adjoint.append(jax.ShapeDtypeStruct(message_shape, wire))
    got = [swapped(message, k) for k in (1, 2, 3)]
    *got, local_back, mixed = lax.optimization_barrier((*got, local_back, mixed))
    output, finished, last = run(
        output_kernel,
        v(inv, taps_far, gain, query, long_conv, mixed),
        [
            jax.ShapeDtypeStruct((rows, channels), bf16),
            kept(rows, channels, dtype=bf16),
            kept(lane_blocks * SUB, LANES),
        ],
        ((lane_blocks * pitch, LANES), (lane_blocks * pitch, LANES)),
        work=2 * 10**9,
    )
    entering, beyond, added, message, *whole = run(
        functools.partial(gather_back_kernel, rows, reach),
        [(place, pltpu.SMEM)] + v(table, back, *got),
        adjoint + ([] if single else [kept(*message_shape)]),
    )
    span = 4
    got = swapped(message, span)
    while 2 * span < count:
        entering, beyond, added, message, *whole = run(
            functools.partial(join_back_kernel, rows, reach, span),
            [(place, pltpu.SMEM)] + v(table, entering, beyond, added, *whole, got),
            adjoint + [kept(*message_shape)],
        )
        span *= 2
        got = swapped(message, span)
    head = shifted(head, -1)
    got, finished = lax.optimization_barrier((got, finished))
    (grads,) = run(
        functools.partial(final_kernel, span),
        [(place, pltpu.SMEM)] + v(entering, beyond, added, got, table, taps_far, pair_far, rows_far, local_back, finished, last, head),
        [pltpu.HBM((3, rows, channels), bf16)],
        (
            (2, rows, SUB, LANES),
            (SUB * pitch, LANES),
            (lane_blocks * SUB, LANES),
            pltpu.VMEM((2, rows, channels), bf16),
            pltpu.VMEM((2 * SUB, channels), bf16),
            pltpu.SemaphoreType.DMA((2 + lane_blocks // 4,)),
        ),
    )
    return output, grads


def solution(mesh):
    return jax.shard_map(
        on_device,
        mesh=mesh,
        in_specs=(
            P(None, "ctx", "tp"),
            P(None, "tp", None),
            P(None, "tp"),
            P(None, "tp"),
            P("tp"),
            P("ctx", "tp"),
        ),
        out_specs=(P("ctx", "tp"), P(None, "ctx", "tp")),
        check_vma=False,
    )
```
